32 devices in a mesh: dp: 16 (over z, y, x), mp: 2 (over core).
Axes of the slice: x: 2, y: 2, z: 4, core: 2. Of those that a mesh axis runs over, the one named last changes fastest.
Arguments:
- tokens: bfloat16 [32768, 768], P('dp'), may hold values from -6 to 6
- out_grad: bfloat16 [32768, 768], P('dp'), may hold values from -6 to 6
- lengths: int32 [16, 4], P('dp'), may hold values from 1 to 1024, 2048 in all within a row
- counts: int32 [16, 4], P('dp'), may hold values from 1 to 1024
- dest_slot: int32 [4096], replicated, may hold values from 0 to 4095, as said below
- qkv_weight: bfloat16 [3, 768, 768], P(None, None, 'mp'), may hold values from -0.3125 to 0.3125
- out_weight: bfloat16 [768, 768], P('mp'), may hold values from -0.875 to 0.875
- up_weight: bfloat16 [768, 3072], P(None, 'mp'), may hold values from -0.21875 to 0.21875
- down_weight: bfloat16 [3072, 768], P('mp'), may hold values from -0.109375 to 0.109375
- norm1_gain: float32 [768], replicated, may hold values from 0.5 to 1.5
- norm1_shift: float32 [768], replicated, may hold values from -3 to 3
- norm2_gain: float32 [768], replicated, may hold values from 0.5 to 1.5
- norm2_shift: float32 [768], replicated, may hold values from -3 to 3
Outputs:
- mixed_out: bfloat16 [32768, 768], P('dp')
- input_grad: bfloat16 [32768, 768], P('dp')
- qkv_grad: float32 [3, 768, 768], P(None, None, 'mp')
- out_weight_grad: float32 [768, 768], P('mp')
- up_grad: float32 [768, 3072], P(None, 'mp')
- down_grad: float32 [3072, 768], P('mp')
- norm1_gain_grad: float32 [768], replicated
- norm1_shift_grad: float32 [768], replicated
- norm2_gain_grad: float32 [768], replicated
- norm2_shift_grad: float32 [768], replicated
The draws below stay inside these ranges and needn't reach their ends.
Inputs may be any that keep to these rules, and one draw needn't show every extreme that they name: `dest_slot`: a permutation; every group receives 256 pieces, the pieces of one group go to 16 groups, exactly 16 to each. `lengths`: each row sums to 2048.
All inputs are finite; a program needn't handle non-finite values.
Results may differ from the reference program's by a relative error of at most 0.015.
Values may be sent and summed in bfloat16 or wider, within the bound.
A program may use at most 256 MiB of HBM per device.

```python
import math
import jax
import jax.numpy as jnp
import numpy as np
from jax import lax

D = 768
HEADS = 12
HEAD_DIM = 64
FF = 3072
TOK_DEV = 2048
CELLS_DEV = 4
PIECE = 8
PIECES_DEV = 256
CAP = 16
PIECES = 4096
TOKENS = 32768
N_DP = 16


def draw_dest_slot(key, part):
    key = jax.random.fold_in(key, 11)
    key_tau, key_sigma, key_pieces, key_slots = jax.random.split(key, 4)
    offsets = jax.random.permutation(key_tau, N_DP)
    targets = jax.random.permutation(key_sigma, N_DP)
    piece_keys = jax.random.split(key_pieces, N_DP)
    shuffled = jax.vmap(lambda one_key: jax.random.permutation(one_key, PIECES_DEV))(piece_keys)
    picked = targets[shuffled // CAP]
    dest_group = (offsets[:, None] + picked) % N_DP
    tie_break = jax.random.permutation(key_slots, PIECES)
    ordering = jnp.argsort(dest_group.reshape(-1).astype(jnp.int32) * PIECES + tie_break)
    return jnp.zeros((PIECES,), jnp.int32).at[ordering].set(jnp.arange(PIECES, dtype=jnp.int32))


def with_ends(values, rng, low, high):
    longest = values.shape.index(max(values.shape))
    spots = []
    for shift in (0, 1):
        where = [jax.random.randint(jax.random.fold_in(rng, axis), (), 0, length) for axis, length in enumerate(values.shape)]
        where[longest] = (where[longest] + shift) % values.shape[longest]
        spots.append(tuple(where))
    return values.at[spots[0]].set(low).at[spots[1]].set(high)


def block_levels(stream_key, shape, shards, low, top_value):
    loudness, own = 1.0, jax.random.fold_in(stream_key, 6)
    for axis_at, shards_of in shards:
        draws = jnp.exp(jax.random.uniform(jax.random.fold_in(own, axis_at), (shards_of,), jnp.float32, low / len(shards), top_value / len(shards)))
        loudness = loudness * jnp.repeat(draws, shape[axis_at] // shards_of).reshape([-1 if axis == axis_at else 1 for axis in range(len(shape))])
    return loudness


def split_up(amount, total, limit, lean):
    portions = [(1 << 20) // math.isqrt(rank ** lean) + 1 for rank in range(2, amount + 1)]
    spare, given = total - limit - (amount - 1), [1] * (amount - 1)
    while spare > 0:
        candidates = [i for i in range(amount - 1) if given[i] < limit]
        pool, budget = sum([portions[i] for i in candidates]), spare
        for i in candidates:
            extra = min(limit - given[i], max(1, budget * portions[i] // pool), spare)
            given[i] = given[i] + extra
            spare = spare - extra
    return np.array([limit] + given)


def ragged(rng, number_of, total, limit, slope):
    if number_of == 2:
        one = jax.random.randint(rng, (), max(1, total - limit), min(limit, total - 1) + 1)
        return jnp.stack([one, total - one])
    tallies = jnp.asarray(split_up(number_of, total, limit, slope), jnp.int32)
    twos = (number_of - 1) // 2
    giver, sink = tallies[1:1 + 2 * twos:2], tallies[2:2 + 2 * twos:2]
    margin = jnp.minimum(giver - 1, limit - sink)
    moved = jax.random.randint(jax.random.fold_in(rng, 1), (twos,), 0, 1 << 20) % (margin + 1)
    tallies = tallies.at[1:1 + 2 * twos:2].set(giver - moved).at[2:2 + 2 * twos:2].set(sink + moved)
    return tallies[jax.random.permutation(jax.random.fold_in(rng, 2), number_of)]


def normal_values(rng, dims, spread, limit, shards=(), kind=jnp.bfloat16):
    drawn = jax.random.normal(rng, dims, jnp.float32) * spread
    if len(shards) > 0:
        drawn = block_levels(rng, dims, shards, -0.22, 0.18) * drawn
    return jnp.clip(drawn, min=-limit, max=limit).astype(kind)


def setup_inputs(seed: int = 0) -> dict:
    keys = jax.random.split(jax.random.key(seed), 14)
    tokens = normal_values(keys[0], (TOKENS, D), 1.0, 6.0, ((0, 16),))
    out_grad = normal_values(keys[1], (TOKENS, D), 1.0, 6.0, ((0, 16),))
    lengths = jax.vmap(lambda own: ragged(own, CELLS_DEV, TOK_DEV, TOK_DEV // 2, 2))(jax.random.split(keys[2], N_DP)).reshape((N_DP, CELLS_DEV)).astype(jnp.int32)
    counts = with_ends(jax.random.randint(keys[3], (N_DP, CELLS_DEV), 1, TOK_DEV // 2 + 1), jax.random.fold_in(keys[3], 1), 1, (TOK_DEV // 2 + 1) - 1).astype(jnp.int32)
    dest_slot = draw_dest_slot(jax.random.fold_in(keys[13], 71), 0)
    qkv_weight = normal_values(keys[5], (3, D, D), (D // 2) ** -0.5, 0.3125, ((2, 2),))
    out_weight = normal_values(keys[6], (D, D), (D // 16) ** -0.5, 0.875, ((0, 2),))
    up_weight = normal_values(keys[7], (D, FF), D ** -0.5, 0.21875, ((1, 2),))
    down_weight = normal_values(keys[8], (FF, D), FF ** -0.5, 0.109375, ((0, 2),))
    norm1_gain = jnp.clip(1.0 + 0.1 * jax.random.normal(keys[9], (D,), jnp.float32), 0.5, 1.5)
    norm1_shift = normal_values(keys[10], (D,), 0.5, 3.0, (), jnp.float32)
    norm2_gain = jnp.clip(1.0 + 0.1 * jax.random.normal(keys[11], (D,), jnp.float32), 0.5, 1.5)
    norm2_shift = normal_values(keys[12], (D,), 0.5, 3.0, (), jnp.float32)
    return {"tokens": tokens, "out_grad": out_grad, "lengths": lengths, "counts": counts, "dest_slot": dest_slot, "qkv_weight": qkv_weight, "out_weight": out_weight, "up_weight": up_weight, "down_weight": down_weight, "norm1_gain": norm1_gain, "norm1_shift": norm1_shift, "norm2_gain": norm2_gain, "norm2_shift": norm2_shift}


@jax.custom_vjp
def low(v):
    return lax.optimization_barrier(v.astype(jnp.bfloat16)).astype(jnp.float32)

@jax.custom_vjp
def low_back(v):
    return v

def low_keep(v):
    return (low(v), None)

def low_pass(kept, grad):
    return (grad,)

def back_keep(v):
    return (v, None)

def back_low(kept, grad):
    return (low(grad),)
low.defvjp(low_keep, low_pass)
low_back.defvjp(back_keep, back_low)
norm_eps = 1e-05
highest = lax.Precision.HIGHEST

def layer_norm(values, gain, shift):
    row_mean = lax.optimization_barrier(jnp.mean(values, axis=-1, keepdims=True))
    centred = values - row_mean
    variance = lax.optimization_barrier(jnp.mean(centred * centred, axis=-1, keepdims=True))
    return centred * lax.rsqrt(variance + norm_eps) * gain + shift

def cell_layout(cell_lengths, cell_counts, tok_rows):
    ends = jnp.cumsum(cell_lengths).astype(jnp.int32)
    starts = ends - cell_lengths
    places = jnp.arange(tok_rows, dtype=jnp.int32)
    segment = lax.optimization_barrier(jnp.sum((places[:, None] >= ends[None, :]).astype(jnp.int32), axis=1))
    member = segment[:, None] == jnp.arange(cell_lengths.shape[0], dtype=jnp.int32)[None, :]
    first = lax.optimization_barrier(jnp.sum(jnp.where(member, starts[None, :], 0), axis=1))
    live = lax.optimization_barrier(jnp.sum(jnp.where(member, jnp.minimum(cell_counts, cell_lengths)[None, :], 0), axis=1))
    return (segment, places - first < live)

def group_forward(inputs, qkv_w, out_w, up_w, down_w, gain1, shift1, gain2, shift2, segment, is_real):
    tok_rows = inputs.shape[0]
    normed = low(layer_norm(inputs, gain1, shift1))
    projected = low(low_back(jnp.einsum('td,cde->cte', normed, qkv_w, precision=highest)))
    queries = projected[0].reshape(tok_rows, HEADS, HEAD_DIM)
    keys_all = projected[1].reshape(tok_rows, HEADS, HEAD_DIM)
    values_all = projected[2].reshape(tok_rows, HEADS, HEAD_DIM)
    query_rows = min(512, tok_rows)
    block_count = tok_rows // query_rows

    def attend(item):
        query_block, segment_block = item
        scores = jnp.einsum('qhd,khd->hqk', query_block, keys_all, precision=highest) * HEAD_DIM ** (-0.5)
        scores = low_back(scores)
        allowed = (segment_block[:, None] == segment[None, :]) & is_real[None, :]
        scores = jnp.where(allowed[None], scores, -1e+30)
        top_score = lax.optimization_barrier(jnp.max(scores, axis=-1, keepdims=True))
        weights = jnp.exp(scores - top_score)
        probs = low(weights / lax.optimization_barrier(jnp.sum(weights, axis=-1, keepdims=True)))
        return jnp.einsum('hqk,khd->qhd', probs, values_all, precision=highest)
    mixed = lax.map(jax.checkpoint(attend), (queries.reshape(block_count, query_rows, HEADS, HEAD_DIM), segment.reshape(block_count, query_rows)))
    mixed = low(low_back(mixed.reshape(tok_rows, D)))
    after_attn = inputs + low_back(jnp.dot(mixed, out_w, precision=highest))
    normed2 = low(layer_norm(after_attn, gain2, shift2))
    hidden = low_back(jnp.dot(normed2, up_w, precision=highest))
    activated = low(jax.nn.gelu(hidden, approximate=False))
    return after_attn + low_back(jnp.dot(activated, down_w, precision=highest))

def reference(tokens, out_grad, lengths, counts, dest_slot, qkv_weight, out_weight, up_weight, down_weight, norm1_gain, norm1_shift, norm2_gain, norm2_shift):

    def to_buckets(values):
        pieces = values.reshape(PIECES, PIECE * D)
        placed = jnp.zeros_like(pieces).at[dest_slot].set(pieces)
        return placed.reshape(N_DP, TOK_DEV, D)

    def from_buckets(values):
        return values.reshape(PIECES, PIECE * D)[dest_slot].reshape(TOKENS, D)
    weights = (qkv_weight.astype(jnp.float32), out_weight.astype(jnp.float32), up_weight.astype(jnp.float32), down_weight.astype(jnp.float32), norm1_gain.astype(jnp.float32), norm1_shift.astype(jnp.float32), norm2_gain.astype(jnp.float32), norm2_shift.astype(jnp.float32))

    def one_group(carry, item):
        group_x, group_dy, group_lengths, group_counts = item
        segment, is_real = cell_layout(group_lengths, group_counts, TOK_DEV)

        def forward(inputs, *params):
            return group_forward(inputs, *params, segment, is_real)
        result, pullback = jax.vjp(forward, group_x.astype(jnp.float32), *weights)
        cotangent = group_dy.astype(jnp.float32) * is_real[:, None].astype(jnp.float32)
        grads = pullback(cotangent)
        carry = tuple((total + piece for total, piece in zip(carry, grads[1:])))
        return (carry, (result.astype(jnp.bfloat16), grads[0].astype(jnp.bfloat16)))
    start = tuple((jnp.zeros_like(w) for w in weights))
    totals, (outputs, input_grads) = lax.scan(one_group, start, (to_buckets(tokens), to_buckets(out_grad), lengths, counts))
    return (from_buckets(outputs), from_buckets(input_grads), totals[0], totals[1], totals[2], totals[3], totals[4], totals[5], totals[6], totals[7])
```

```python
import functools

import jax
import jax.numpy as jnp
from jax import lax
from jax.experimental import pallas as pl
from jax.experimental.pallas import tpu as pltpu
from jax.sharding import PartitionSpec as P

HEAD_DIM = 64
PIECE = 8
NORM_EPS = 1e-05
MASKED = -1e30
MIB = 2**20
VMEM = pl.BlockSpec(memory_space=pltpu.VMEM)
SMEM = pl.BlockSpec(memory_space=pltpu.SMEM)
NT = (((1,), (1,)), ((), ()))
TN = (((0,), (0,)), ((), ()))


def params(mib):
    return pltpu.CompilerParams(vmem_limit_bytes=mib * MIB)


def cost(flops, nbytes, transcendentals=0):
    return pl.CostEstimate(
        flops=int(flops), bytes_accessed=int(nbytes), transcendentals=int(transcendentals)
    )


def struct(shape, dtype):
    return jax.ShapeDtypeStruct(shape, dtype)


def dot(a, b, dims=None):
    if dims is None:
        return jnp.dot(a, b, preferred_element_type=jnp.float32)
    return lax.dot_general(a, b, dims, preferred_element_type=jnp.float32)


def norm_unit(values):
    mean = jnp.mean(values, axis=-1, keepdims=True)
    centred = values - mean
    variance = jnp.mean(centred * centred, axis=-1, keepdims=True)
    inverse = lax.rsqrt(variance + NORM_EPS)
    return centred * inverse, inverse


def norm_back(grad_unit, unit, inverse):
    first = jnp.mean(grad_unit, axis=-1, keepdims=True)
    second = jnp.mean(grad_unit * unit, axis=-1, keepdims=True)
    return inverse * (grad_unit - first - unit * second)


def slot_table(chosen, values, capacity):
    per = chosen.shape[1]
    place = lax.broadcasted_iota(jnp.int32, (per, per), 0)
    earlier = place < lax.broadcasted_iota(jnp.int32, (per, per), 1)
    rank = dot(chosen.astype(jnp.bfloat16), earlier.astype(jnp.bfloat16)).astype(jnp.int32)
    rank = jnp.where(chosen, rank, -1)
    ranks = jnp.arange(capacity, dtype=jnp.int32)
    hit = rank[:, None, :] == ranks[None, :, None]
    return jnp.sum(jnp.where(hit, values[:, None, :], 0), axis=2)


def gather_kernel(index_ref, source_ref, out_ref):
    def step(j, carry):
        out_ref[j] = source_ref[index_ref[j]]
        return carry

    lax.fori_loop(0, out_ref.shape[0], step, 0, unroll=8)


def gather_pieces(index, source):
    rows, width = source.shape
    count = index.shape[0]
    out = pl.pallas_call(
        gather_kernel,
        out_shape=struct((count, PIECE, width), source.dtype),
        in_specs=[SMEM, VMEM],
        out_specs=VMEM,
        compiler_params=params(32),
        cost_estimate=cost(0, 3 * rows * width),
        name="gather_pieces",
    )(index, source.reshape(rows // PIECE, PIECE, width))
    return out.reshape(count * PIECE, width)


def split_kernel(own_ref, other_ref, source_ref, own_out, other_out):
    def step(j, carry):
        own_out[j] = source_ref[own_ref[j]]
        other_out[j] = source_ref[other_ref[j]]
        return carry

    lax.fori_loop(0, own_out.shape[0], step, 0, unroll=8)


def split_pieces(own, other, source):
    rows, width = source.shape
    count = own.shape[0]
    outs = pl.pallas_call(
        split_kernel,
        out_shape=[struct((count, PIECE, width), source.dtype)] * 2,
        in_specs=[SMEM, SMEM, VMEM],
        out_specs=[VMEM, VMEM],
        compiler_params=params(32),
        cost_estimate=cost(0, 4 * rows * width),
        name="split_pieces",
    )(own, other, source.reshape(rows // PIECE, PIECE, width))
    return tuple(o.reshape(count * PIECE, width) for o in outs)


def merge_kernel(own_ref, other_ref, own_in, other_in, out_ref):
    def step(j, carry):
        out_ref[own_ref[j]] = own_in[j]
        out_ref[other_ref[j]] = other_in[j]
        return carry

    lax.fori_loop(0, own_in.shape[0], step, 0, unroll=8)


def merge_pieces(own, other, own_rows, other_rows):
    rows, width = own_rows.shape
    out = pl.pallas_call(
        merge_kernel,
        out_shape=struct((2 * rows // PIECE, PIECE, width), own_rows.dtype),
        in_specs=[SMEM, SMEM, VMEM, VMEM],
        out_specs=VMEM,
        compiler_params=params(32),
        cost_estimate=cost(0, 8 * rows * width),
        name="merge_pieces",
    )(
        own,
        other,
        own_rows.reshape(rows // PIECE, PIECE, width),
        other_rows.reshape(rows // PIECE, PIECE, width),
    )
    return out.reshape(2 * rows, width)


def project_kernel(
    own_ref, other_ref, own_in, other_in, gain_ref, shift_ref, w_ref, wt_ref, h_ref, n_ref, t_ref, x_all
):
    def step(j, carry):
        x_all[own_ref[j]] = own_in[j]
        x_all[other_ref[j]] = other_in[j]
        return carry

    lax.fori_loop(0, own_in.shape[0], step, 0, unroll=8)
    rows = n_ref.shape[0]
    block = min(256, rows)
    pieces = block // PIECE

    def rows_step(i, carry):
        x = x_all[pl.ds(i * pieces, pieces)].astype(jnp.float32).reshape(block, -1)
        unit, _ = norm_unit(x)
        h = (unit * gain_ref[...] + shift_ref[...]).astype(jnp.bfloat16)
        at = pl.ds(pl.multiple_of(i * block, block), block)
        h_ref[at, :] = h
        n_ref[at, :] = dot(h, w_ref[...]).astype(jnp.bfloat16)
        t_ref[:, at] = dot(wt_ref[...], h, NT).astype(jnp.bfloat16)
        return carry

    lax.fori_loop(0, rows // block, rows_step, 0)


def project(own, other, x_own, x_other, gain, shift, w, wt):
    half, width = x_own.shape
    rows, outs = 2 * half, w.shape[1]
    pieces = half // PIECE
    return pl.pallas_call(
        project_kernel,
        out_shape=[
            struct((rows, width), jnp.bfloat16),
            struct((rows, outs), jnp.bfloat16),
            struct((outs, rows), jnp.bfloat16),
        ],
        in_specs=[SMEM, SMEM] + [VMEM] * 6,
        out_specs=[VMEM] * 3,
        scratch_shapes=[pltpu.VMEM((rows // PIECE, PIECE, width), jnp.bfloat16)],
        compiler_params=params(56),
        cost_estimate=cost(4 * rows * width * outs, 20e6),
        name="project",
    )(own, other, x_own.reshape(pieces, PIECE, width), x_other.reshape(pieces, PIECE, width), gain, shift, w, wt)


def cell_bounds(len_ref, cnt_ref):
    cells = len_ref.shape[1]
    starts, lives, start = [], [], jnp.int32(0)
    for c in range(cells):
        length = len_ref[0, c]
        starts.append(start)
        lives.append(start + jnp.minimum(length, cnt_ref[0, c]))
        start = start + length
    return starts, lives


def key_range(pos, starts, lives):
    low = jnp.zeros_like(pos) + starts[0]
    high = jnp.zeros_like(pos) + lives[0]
    for start, live in zip(starts[1:], lives[1:]):
        inside = pos >= start
        low = jnp.where(inside, start, low)
        high = jnp.where(inside, live, high)
    return low, high


def attend_kernel(
    own_ref, other_ref, len_ref, cnt_ref, k_ref, qt_ref, vt_ref,
    ot_ref, own_out, other_out, lse_ref,
    natural, bias, top, total, acc,
):
    rows, width = k_ref.shape
    heads = width // HEAD_DIM
    bk, bq = bias.shape
    starts, lives = cell_bounds(len_ref, cnt_ref)
    zeros = jnp.zeros((HEAD_DIM, bq), jnp.bfloat16)

    def query_step(i, carry):
        q0 = pl.multiple_of(i * bq, bq)
        cols = pl.ds(q0, bq)
        low, high = key_range(q0 + lax.broadcasted_iota(jnp.int32, (1, bq), 1), starts, lives)
        first, _ = key_range(q0, starts, lives)
        _, last = key_range(q0 + bq - 1, starts, lives)
        top[...] = jnp.full_like(top, MASKED)
        total[...] = jnp.zeros_like(total)
        acc[...] = jnp.zeros_like(acc)

        def key_step(j, carry):
            k0 = pl.multiple_of(j * bk, bk)
            keys = pl.ds(k0, bk)
            kpos = k0 + lax.broadcasted_iota(jnp.int32, (bk, bq), 0)
            bias[...] = jnp.where((kpos >= low) & (kpos < high), 0.0, MASKED)
            for h in range(heads):
                lanes = slice(h // 2 * 128, h // 2 * 128 + 128)
                sub = slice(h * HEAD_DIM, (h + 1) * HEAD_DIM)
                q = qt_ref[sub, cols]
                q = jnp.concatenate([q, zeros] if h % 2 == 0 else [zeros, q], axis=0)
                s = dot(k_ref[keys, lanes], q) + bias[...]
                old = top[h : h + 1, :]
                new = jnp.maximum(old, jnp.max(s, axis=0, keepdims=True))
                p = jnp.exp(s - new)
                decay = jnp.exp(old - new)
                top[h : h + 1, :] = new
                total[h : h + 1, :] = total[h : h + 1, :] * decay + jnp.sum(p, axis=0, keepdims=True)
                acc[sub, :] = acc[sub, :] * decay + dot(vt_ref[sub, keys], p.astype(jnp.bfloat16))
            return carry

        lax.fori_loop(first // bk, (last + bk - 1) // bk, key_step, 0)
        for h in range(heads):
            sub = slice(h * HEAD_DIM, (h + 1) * HEAD_DIM)
            acc[sub, :] = acc[sub, :] / total[h : h + 1, :]
            lse_ref[h : h + 1, cols] = top[h : h + 1, :] + jnp.log(total[h : h + 1, :])
        mixed = acc[...]
        ot_ref[:, cols] = mixed.astype(jnp.bfloat16)
        natural[pl.ds(i * (bq // PIECE), bq // PIECE)] = mixed.T.reshape(bq // PIECE, PIECE, width)
        return carry

    lax.fori_loop(0, rows // bq, query_step, 0)

    def step(j, carry):
        own_out[j] = natural[own_ref[j]].astype(jnp.bfloat16)
        other_out[j] = natural[other_ref[j]].astype(jnp.bfloat16)
        return carry

    lax.fori_loop(0, own_out.shape[0], step, 0, unroll=8)


def attend(own, other, lengths, counts, k, qt, vt):
    rows, width = k.shape
    count = own.shape[0]
    bk = bq = min(256, rows)
    heads = width // HEAD_DIM
    ot, o_own, o_other, lse = pl.pallas_call(
        attend_kernel,
        out_shape=[
            struct((width, rows), jnp.bfloat16),
            struct((count, PIECE, width), jnp.bfloat16),
            struct((count, PIECE, width), jnp.bfloat16),
            struct((8, rows), jnp.float32),
        ],
        in_specs=[SMEM] * 4 + [VMEM] * 3,
        out_specs=[VMEM] * 4,
        scratch_shapes=[
            pltpu.VMEM((rows // PIECE, PIECE, width), jnp.float32),
            pltpu.VMEM((bk, bq), jnp.float32),
            pltpu.VMEM((8, bq), jnp.float32),
            pltpu.VMEM((8, bq), jnp.float32),
            pltpu.VMEM((width, bq), jnp.float32),
        ],
        compiler_params=params(56),
        cost_estimate=cost(2e10, 10e6, heads * rows * rows // 2),
        name="attend",
    )(own, other, lengths, counts, k, qt, vt)
    return ot, o_own.reshape(count * PIECE, width), o_other.reshape(count * PIECE, width), lse


def attend_back_kernel(
    own_ref, other_ref, len_ref, cnt_ref, q_ref, k_ref, v_ref, qt_ref, kt_ref, ot_ref, lse_ref,
    own_in, other_in, out_ref,
    natural, do_t, do_m, q_m, delta, dq_t, dk_acc, dv_acc, bias,
):
    rows, width = k_ref.shape
    heads = width // HEAD_DIM
    bk, bq = bias.shape
    pieces = bq // PIECE
    starts, lives = cell_bounds(len_ref, cnt_ref)
    zeros = jnp.zeros((HEAD_DIM, bq), jnp.bfloat16)

    def place(j, carry):
        natural[own_ref[j]] = own_in[j].astype(jnp.float32)
        natural[other_ref[j]] = other_in[j].astype(jnp.float32)
        return carry

    lax.fori_loop(0, own_in.shape[0], place, 0, unroll=8)
    lane = lax.broadcasted_iota(jnp.int32, (bq, 128), 1)

    def prepare(i, carry):
        q0 = pl.multiple_of(i * bq, bq)
        at = pl.ds(q0, bq)
        do = natural[pl.ds(i * pieces, pieces)].reshape(bq, width)
        dot_t = do.T
        do_t[:, at] = dot_t.astype(jnp.bfloat16)
        for h in range(heads):
            sub = slice(h * HEAD_DIM, (h + 1) * HEAD_DIM)
            delta[h : h + 1, at] = jnp.sum(
                dot_t[sub, :] * ot_ref[sub, at].astype(jnp.float32), axis=0, keepdims=True
            )
            lanes = slice(h // 2 * 128, h // 2 * 128 + 128)
            mine = (lane < HEAD_DIM) if h % 2 == 0 else (lane >= HEAD_DIM)
            do_m[h, at, :] = jnp.where(mine, do[:, lanes], 0.0).astype(jnp.bfloat16)
            q_m[h, at, :] = jnp.where(mine, q_ref[at, lanes].astype(jnp.float32), 0.0).astype(jnp.bfloat16)
        dq_t[:, at] = jnp.zeros((width, bq), jnp.float32)
        return carry

    lax.fori_loop(0, rows // bq, prepare, 0)

    def key_step(j, carry):
        k0 = pl.multiple_of(j * bk, bk)
        keys = pl.ds(k0, bk)
        first, _ = key_range(k0, starts, lives)
        _, last = key_range(k0 + bk - 1, starts, lives)
        dk_acc[...] = jnp.zeros_like(dk_acc)
        dv_acc[...] = jnp.zeros_like(dv_acc)

        def query_step(i, carry):
            q0 = pl.multiple_of(i * bq, bq)
            cols = pl.ds(q0, bq)
            low, high = key_range(q0 + lax.broadcasted_iota(jnp.int32, (1, bq), 1), starts, lives)
            kpos = k0 + lax.broadcasted_iota(jnp.int32, (bk, bq), 0)
            bias[...] = jnp.where((kpos >= low) & (kpos < high), 0.0, MASKED)
            for h in range(0, heads, 2):
                lanes = slice(h // 2 * 128, h // 2 * 128 + 128)
                probs, slopes = [], []
                for e in range(2):
                    g = h + e
                    sub = slice(g * HEAD_DIM, (g + 1) * HEAD_DIM)
                    q = qt_ref[sub, cols]
                    q = jnp.concatenate([q, zeros] if e == 0 else [zeros, q], axis=0)
                    d = do_t[sub, cols]
                    d = jnp.concatenate([d, zeros] if e == 0 else [zeros, d], axis=0)
                    s = dot(k_ref[keys, lanes], q) + bias[...]
                    p = jnp.exp(s - lse_ref[g : g + 1, cols])
                    dp = dot(v_ref[keys, lanes], d)
                    ds = (p * (dp - delta[g : g + 1, cols])).astype(jnp.bfloat16)
                    probs.append(p.astype(jnp.bfloat16))
                    slopes.append(ds)
                    dq_t[sub, cols] += dot(kt_ref[sub, keys], ds)
                for e in range(2):
                    dv_acc[:, lanes] += dot(probs[e], do_m[h + e, cols, :])
                    dk_acc[:, lanes] += dot(slopes[e], q_m[h + e, cols, :])
            return carry

        lax.fori_loop(first // bq, (last + bq - 1) // bq, query_step, 0)
        out_ref[1, keys, :] = dk_acc[...].astype(jnp.bfloat16)
        out_ref[2, keys, :] = dv_acc[...].astype(jnp.bfloat16)
        return carry

    lax.fori_loop(0, rows // bk, key_step, 0)

    def finish(i, carry):
        at = pl.ds(pl.multiple_of(i * bq, bq), bq)
        out_ref[0, at, :] = (dq_t[:, at].T * HEAD_DIM**-0.5).astype(jnp.bfloat16)
        return carry

    lax.fori_loop(0, rows // bq, finish, 0)


def attend_back(own, other, lengths, counts, q, k, v, qt, kt, ot, lse, do_own, do_other):
    rows, width = k.shape
    count = own.shape[0]
    bk = bq = min(256, rows)
    heads = width // HEAD_DIM
    return pl.pallas_call(
        attend_back_kernel,
        out_shape=struct((3, rows, width), jnp.bfloat16),
        in_specs=[SMEM] * 4 + [VMEM] * 9,
        out_specs=VMEM,
        scratch_shapes=[
            pltpu.VMEM((rows // PIECE, PIECE, width), jnp.float32),
            pltpu.VMEM((width, rows), jnp.bfloat16),
            pltpu.VMEM((heads, rows, 128), jnp.bfloat16),
            pltpu.VMEM((heads, rows, 128), jnp.bfloat16),
            pltpu.VMEM((8, rows), jnp.float32),
            pltpu.VMEM((width, rows), jnp.float32),
            pltpu.VMEM((bk, width), jnp.float32),
            pltpu.VMEM((bk, width), jnp.float32),
            pltpu.VMEM((bk, bq), jnp.float32),
        ],
        compiler_params=params(58),
        cost_estimate=cost(5e10, 20e6, heads * rows * rows // 2),
        name="attend_back",
    )(
        own, other, lengths, counts, q, k, v, qt, kt, ot, lse,
        do_own.reshape(count, PIECE, width), do_other.reshape(count, PIECE, width),
    )


def feed_kernel(
    x_ref, oa_ref, ob_ref, dy_ref, real_ref, wo_a, wo_b, up_a, up_b, down_a, down_b, gain_ref, shift_ref,
    out_ref, h_ref, act_a, act_b, du_a, du_b, gr_ref, dar_ref, doa_ref, dob_ref, dy1_ref, norm_ref,
):
    x = x_ref[...].astype(jnp.float32)
    y1 = x + dot(oa_ref[...], wo_a[...]) + dot(ob_ref[...], wo_b[...])
    unit, inverse = norm_unit(y1)
    h = (unit * gain_ref[...] + shift_ref[...]).astype(jnp.bfloat16)
    h_ref[...] = h
    g = dy_ref[...].astype(jnp.float32) * real_ref[...]
    gr = g.astype(jnp.bfloat16)
    gr_ref[...] = gr
    mlp = None
    dh = None
    for up, down, act_ref, du_ref in ((up_a, down_a, act_a, du_a), (up_b, down_b, act_b, du_b)):
        hidden = up.shape[1]
        part = min(768, hidden)
        for at in range(0, hidden, part):
            cols = slice(at, at + part)
            u = dot(h, up[:, cols])
            phi = 0.5 * (1.0 + lax.erf(u * 0.7071067811865476))
            act = (u * phi).astype(jnp.bfloat16)
            act_ref[:, cols] = act
            slope = phi + u * 0.3989422804014327 * jnp.exp(-0.5 * u * u)
            du = (dot(gr, down[cols, :], NT) * slope).astype(jnp.bfloat16)
            du_ref[:, cols] = du
            m = dot(act, down[cols, :])
            d = dot(du, up[:, cols], NT)
            mlp = m if mlp is None else mlp + m
            dh = d if dh is None else dh + d
    out_ref[...] = (y1 + mlp).astype(jnp.bfloat16)
    sums = jnp.concatenate(
        [jnp.sum(dh * unit, axis=0, keepdims=True), jnp.sum(dh, axis=0, keepdims=True)], axis=0
    )

    @pl.when(pl.program_id(0) == 0)
    def _():
        norm_ref[...] = sums

    @pl.when(pl.program_id(0) > 0)
    def _():
        norm_ref[...] += sums

    dy1 = g + norm_back(dh * gain_ref[...], unit, inverse)
    dy1_ref[...] = dy1
    dar = dy1.astype(jnp.bfloat16)
    dar_ref[...] = dar
    doa_ref[...] = dot(dar, wo_a[...], NT).astype(jnp.bfloat16)
    dob_ref[...] = dot(dar, wo_b[...], NT).astype(jnp.bfloat16)


def feed(x, o_own, o_other, dy, real, wo, up, down, gain, shift):
    rows, width = x.shape
    local = o_own.shape[1]
    hidden = up[0].shape[1]
    block = min(256, rows)

    def tall(cols):
        return pl.BlockSpec((block, cols), lambda i: (i, 0))

    def whole(shape):
        return pl.BlockSpec(shape, lambda i: (0, 0), pipeline_mode=pl.Buffered(1))

    bf16 = jnp.bfloat16
    return pl.pallas_call(
        feed_kernel,
        grid=(rows // block,),
        out_shape=[
            struct((rows, width), bf16),
            struct((rows, width), bf16),
            struct((rows, hidden), bf16),
            struct((rows, hidden), bf16),
            struct((rows, hidden), bf16),
            struct((rows, hidden), bf16),
            struct((rows, width), bf16),
            struct((rows, width), bf16),
            struct((rows, local), bf16),
            struct((rows, local), bf16),
            struct((rows, width), jnp.float32),
            struct((2, width), jnp.float32),
        ],
        in_specs=[tall(width), tall(local), tall(local), tall(width), tall(1)]
        + [whole((local, width))] * 2
        + [whole((width, hidden))] * 2
        + [whole((hidden, width))] * 2
        + [whole((1, width))] * 2,
        out_specs=[tall(width)] * 2
        + [tall(hidden)] * 4
        + [tall(width)] * 2
        + [tall(local)] * 2
        + [tall(width), pl.BlockSpec((2, width), lambda i: (0, 0))],
        compiler_params=params(58),
        cost_estimate=cost(2 * rows * width * (hidden * 8 + local * 4), 50e6, rows * hidden * 4),
        name="feed",
    )(x, o_own, o_other, dy, real, *wo, *up, *down, gain, shift)


def finish_kernel(x_ref, own_ref, other_ref, dy1_ref, gain_ref, dx_ref, norm_ref):
    unit, inverse = norm_unit(x_ref[...].astype(jnp.float32))
    dh = own_ref[...].astype(jnp.float32) + other_ref[...].astype(jnp.float32)
    sums = jnp.concatenate(
        [jnp.sum(dh * unit, axis=0, keepdims=True), jnp.sum(dh, axis=0, keepdims=True)], axis=0
    )

    @pl.when(pl.program_id(0) == 0)
    def _():
        norm_ref[...] = sums

    @pl.when(pl.program_id(0) > 0)
    def _():
        norm_ref[...] += sums

    dx = dy1_ref[...] + norm_back(dh * gain_ref[...], unit, inverse)
    dx_ref[...] = dx.astype(jnp.bfloat16)


def finish(x, dh_own, dh_other, dy1, gain):
    rows, width = x.shape
    block = min(256, rows)
    tall = pl.BlockSpec((block, width), lambda i: (i, 0))
    return pl.pallas_call(
        finish_kernel,
        grid=(rows // block,),
        out_shape=[struct((rows, width), jnp.bfloat16), struct((2, width), jnp.float32)],
        in_specs=[tall, tall, tall, tall, pl.BlockSpec((1, width), lambda i: (0, 0))],
        out_specs=[tall, pl.BlockSpec((2, width), lambda i: (0, 0))],
        compiler_params=params(32),
        cost_estimate=cost(0, 12 * rows * width),
        name="finish",
    )(x, dh_own, dh_other, dy1, gain)


def bit_pairs(size, bit):
    return [(i, i ^ bit) for i in range(size)]


def reduce_bits(value, bits, size, me):
    for bit in bits:
        half = value.shape[0] // 2
        mine = (me // bit) % 2
        keep = lax.dynamic_slice_in_dim(value, mine * half, half, 0)
        send = lax.dynamic_slice_in_dim(value, (1 - mine) * half, half, 0)
        got = lax.ppermute(send, "dp", bit_pairs(size, bit))
        value = (keep.astype(jnp.float32) + got.astype(jnp.float32)).astype(jnp.bfloat16)
    return value


def gather_bits(value, bits, size, me):
    for bit in reversed(bits):
        mine = (me // bit) % 2
        got = lax.ppermute(value, "dp", bit_pairs(size, bit))
        first = jnp.where(mine == 0, value, got)
        second = jnp.where(mine == 0, got, value)
        value = jnp.concatenate([first, second], axis=0)
    return value


def sum_all(value, size, me, swapped):
    bits = [1 << b for b in range(size.bit_length() - 1)]
    if swapped and len(bits) > 1:
        bits[0], bits[1] = bits[1], bits[0]
    return gather_bits(reduce_bits(value, bits, size, me), bits, size, me)


def sum_small(value, size):
    value = value + lax.ppermute(value, "mp", [(0, 1), (1, 0)])
    bit = 1
    while bit < size:
        value = value + lax.ppermute(value, "dp", bit_pairs(size, bit))
        bit *= 2
    return value


def swap(value):
    return lax.ppermute(value, "mp", [(0, 1), (1, 0)])


def exchange(value):
    return lax.all_to_all(value, "dp", split_axis=0, concat_axis=0, tiled=True)


def body(
    tokens, out_grad, lengths, counts, dest_slot, qkv_weight, out_weight, up_weight, down_weight,
    norm1_gain, norm1_shift, norm2_gain, norm2_shift,
):
    groups = lax.axis_size("dp")
    me = lax.axis_index("dp")
    core = lax.axis_index("mp")
    rows, width = tokens.shape
    per = rows // PIECE
    capacity = per // groups
    half = capacity // 2
    local = qkv_weight.shape[2]
    bf16 = jnp.bfloat16

    slots = dest_slot.reshape(groups, per)
    my_slots = lax.dynamic_index_in_dim(slots, me, 0, keepdims=True)
    group_ids = jnp.arange(groups, dtype=jnp.int32)[:, None]
    piece_ids = jnp.broadcast_to(jnp.arange(per, dtype=jnp.int32)[None, :], (groups, per))
    source = slot_table(my_slots // per == group_ids, piece_ids, capacity)
    target = slot_table(slots // per == me, slots - me * per, capacity)

    def halves(table):
        own = lax.dynamic_slice_in_dim(table, core * half, half, 1)
        other = lax.dynamic_slice_in_dim(table, (1 - core) * half, half, 1)
        return own.reshape(-1), other.reshape(-1)

    src_own, src_other = halves(source)
    own, other = halves(target)

    x_own = exchange(gather_pieces(src_own, tokens))
    dy_send = gather_pieces(src_own, out_grad)
    x_other = swap(x_own)
    wo = (out_weight, swap(out_weight))
    up = (up_weight, swap(up_weight))
    down = (down_weight, swap(down_weight))
    scaled = jnp.concatenate(
        [qkv_weight[0] * jnp.asarray(HEAD_DIM**-0.5, bf16), qkv_weight[1], qkv_weight[2]], axis=1
    )
    gain1, shift1 = norm1_gain[None], norm1_shift[None]
    gain2, shift2 = norm2_gain[None], norm2_shift[None]

    h1, natural, turned = project(own, other, x_own, x_other, gain1, shift1, scaled, scaled.T)
    q, k, v = (natural[:, i * local : (i + 1) * local] for i in range(3))
    qt, kt, vt = (turned[i * local : (i + 1) * local] for i in range(3))

    dy_send, _ = lax.optimization_barrier((dy_send, x_own))
    dy_own = exchange(dy_send)
    ot, o_own, o_send, lse = attend(own, other, lengths, counts, k, qt, vt)
    o_other = swap(o_send)

    place = (own[:, None] * PIECE + jnp.arange(PIECE, dtype=jnp.int32)[None, :]).reshape(-1, 1)
    real, start = jnp.zeros(place.shape, jnp.bool_), jnp.int32(0)
    for c in range(lengths.shape[1]):
        live = start + jnp.minimum(lengths[0, c], counts[0, c])
        real, start = real | ((place >= start) & (place < live)), start + lengths[0, c]
    real = real.astype(jnp.float32)

    (out_rows, h2, act_a, act_b, du_a, du_b, gr, dar, do_own, do_send, dy1, norm2) = feed(
        x_own, o_own, o_other, dy_own, real, wo, up, down, gain2, shift2
    )
    do_other = swap(do_send)
    out_back = exchange(out_rows)

    def outer(a, b):
        return dot(a, b, TN).astype(bf16)

    up_sum = outer(h2, du_a).astype(jnp.float32) + swap(outer(h2, du_b)).astype(jnp.float32)
    down_sum = outer(act_a, gr).astype(jnp.float32) + swap(outer(act_b, gr)).astype(jnp.float32)
    wo_sum = outer(o_own, dar).astype(jnp.float32) + swap(outer(o_other, dar)).astype(jnp.float32)
    up_grad = sum_all(up_sum.astype(bf16), groups, me, False).astype(jnp.float32)
    down_grad = sum_all(down_sum.astype(bf16), groups, me, True).astype(jnp.float32)
    wo_grad = sum_all(wo_sum.astype(bf16), groups, me, False).astype(jnp.float32)

    grads = attend_back(own, other, lengths, counts, q, k, v, qt, kt, ot, lse, do_own, do_other)
    qkv_part = jnp.einsum("td,cte->cde", h1, grads, preferred_element_type=jnp.float32).astype(bf16)
    dh1 = jnp.einsum("cte,cde->td", grads, qkv_weight, preferred_element_type=jnp.float32).astype(bf16)
    dh_own, dh_send = split_pieces(own, other, dh1)
    dx, norm1 = finish(x_own, dh_own, swap(dh_send), dy1, gain1)
    dx_back = exchange(dx)
    flat = qkv_part.reshape(3 * width, local)
    cut = flat.shape[0] // 2
    qkv_grad = jnp.concatenate(
        [sum_all(flat[:cut], groups, me, False), sum_all(flat[cut:], groups, me, True)], axis=0
    ).reshape(3, width, local).astype(jnp.float32)
    norms = sum_small(jnp.concatenate([norm1, norm2], axis=0), groups)

    mixed_out = merge_pieces(src_own, src_other, out_back, swap(out_back))
    input_grad = merge_pieces(src_own, src_other, dx_back, swap(dx_back))
    return (
        mixed_out, input_grad, qkv_grad, wo_grad, up_grad, down_grad,
        norms[0], norms[1], norms[2], norms[3],
    )


def solution(mesh):
    in_specs = (
        P("dp", None), P("dp", None), P("dp", None), P("dp", None), P(),
        P(None, None, "mp"), P("mp", None), P(None, "mp"), P("mp", None), P(), P(), P(), P(),
    )
    out_specs = (
        P("dp", None), P("dp", None), P(None, None, "mp"), P("mp", None), P(None, "mp"), P("mp", None),
        P(), P(), P(), P(),
    )
    return jax.shard_map(body, mesh=mesh, in_specs=in_specs, out_specs=out_specs, check_vma=False)
```

```python
import functools

import jax
import jax.numpy as jnp
from jax import lax
from jax.experimental import pallas as pl
from jax.experimental.pallas import tpu as pltpu
from jax.sharding import PartitionSpec as P

HEAD_DIM = 64
PIECE = 8
NORM_EPS = 1e-05
MASKED = -1e30
MIB = 2**20
VMEM = pl.BlockSpec(memory_space=pltpu.VMEM)
SMEM = pl.BlockSpec(memory_space=pltpu.SMEM)
NT = (((1,), (1,)), ((), ()))
TN = (((0,), (0,)), ((), ()))


def params(mib):
    return pltpu.CompilerParams(vmem_limit_bytes=mib * MIB)


def cost(flops, nbytes, transcendentals=0):
    return pl.CostEstimate(
        flops=int(flops), bytes_accessed=int(nbytes), transcendentals=int(transcendentals)
    )


def struct(shape, dtype):
    return jax.ShapeDtypeStruct(shape, dtype)


def dot(a, b, dims=None):
    if dims is None:
        return jnp.dot(a, b, preferred_element_type=jnp.float32)
    return lax.dot_general(a, b, dims, preferred_element_type=jnp.float32)


def norm_unit(values):
    mean = jnp.mean(values, axis=-1, keepdims=True)
    centred = values - mean
    variance = jnp.mean(centred * centred, axis=-1, keepdims=True)
    inverse = lax.rsqrt(variance + NORM_EPS)
    return centred * inverse, inverse


def norm_back(grad_unit, unit, inverse):
    first = jnp.mean(grad_unit, axis=-1, keepdims=True)
    second = jnp.mean(grad_unit * unit, axis=-1, keepdims=True)
    return inverse * (grad_unit - first - unit * second)


def slot_table(chosen, values, capacity):
    per = chosen.shape[1]
    place = lax.broadcasted_iota(jnp.int32, (per, per), 0)
    earlier = place < lax.broadcasted_iota(jnp.int32, (per, per), 1)
    rank = dot(chosen.astype(jnp.bfloat16), earlier.astype(jnp.bfloat16)).astype(jnp.int32)
    rank = jnp.where(chosen, rank, -1)
    ranks = jnp.arange(capacity, dtype=jnp.int32)
    hit = rank[:, None, :] == ranks[None, :, None]
    return jnp.sum(jnp.where(hit, values[:, None, :], 0), axis=2)


def gather_kernel(index_ref, source_ref, out_ref):
    def step(j, carry):
        out_ref[j] = source_ref[index_ref[j]]
        return carry

    lax.fori_loop(0, out_ref.shape[0], step, 0, unroll=8)


def gather_pieces(index, source):
    rows, width = source.shape
    count = index.shape[0]
    out = pl.pallas_call(
        gather_kernel,
        out_shape=struct((count, PIECE, width), source.dtype),
        in_specs=[SMEM, VMEM],
        out_specs=VMEM,
        compiler_params=params(32),
        cost_estimate=cost(0, 3 * rows * width),
        name="gather_pieces",
    )(index, source.reshape(rows // PIECE, PIECE, width))
    return out.reshape(count * PIECE, width)


def split_kernel(own_ref, other_ref, source_ref, own_out, other_out):
    def step(j, carry):
        own_out[j] = source_ref[own_ref[j]]
        other_out[j] = source_ref[other_ref[j]]
        return carry

    lax.fori_loop(0, own_out.shape[0], step, 0, unroll=8)


def split_pieces(own, other, source):
    rows, width = source.shape
    count = own.shape[0]
    outs = pl.pallas_call(
        split_kernel,
        out_shape=[struct((count, PIECE, width), source.dtype)] * 2,
        in_specs=[SMEM, SMEM, VMEM],
        out_specs=[VMEM, VMEM],
        compiler_params=params(32),
        cost_estimate=cost(0, 4 * rows * width),
        name="split_pieces",
    )(own, other, source.reshape(rows // PIECE, PIECE, width))
    return tuple(o.reshape(count * PIECE, width) for o in outs)


def merge_kernel(own_ref, other_ref, own_in, other_in, out_ref):
    def step(j, carry):
        out_ref[own_ref[j]] = own_in[j]
        out_ref[other_ref[j]] = other_in[j]
        return carry

    lax.fori_loop(0, own_in.shape[0], step, 0, unroll=8)


def merge_pieces(own, other, own_rows, other_rows):
    rows, width = own_rows.shape
    out = pl.pallas_call(
        merge_kernel,
        out_shape=struct((2 * rows // PIECE, PIECE, width), own_rows.dtype),
        in_specs=[SMEM, SMEM, VMEM, VMEM],
        out_specs=VMEM,
        compiler_params=params(32),
        cost_estimate=cost(0, 8 * rows * width),
        name="merge_pieces",
    )(
        own,
        other,
        own_rows.reshape(rows // PIECE, PIECE, width),
        other_rows.reshape(rows // PIECE, PIECE, width),
    )
    return out.reshape(2 * rows, width)


def project_kernel(
    own_ref, other_ref, own_in, other_in, gain_ref, shift_ref, w_ref, wt_ref,
    ht_ref, q_ref, k_ref, v_ref, qt_ref, kt_ref, vt_ref, x_all,
):
    @pl.when(pl.program_id(0) == 0)
    def _():
        def step(j, carry):
            x_all[own_ref[j]] = own_in[j]
            x_all[other_ref[j]] = other_in[j]
            return carry

        lax.fori_loop(0, own_in.shape[0], step, 0, unroll=8)

    block, local = q_ref.shape
    pieces = block // PIECE
    x = x_all[pl.ds(pl.program_id(0) * pieces, pieces)].astype(jnp.float32).reshape(block, -1)
    unit, _ = norm_unit(x)
    h = (unit * gain_ref[...] + shift_ref[...]).astype(jnp.bfloat16)
    ht_ref[...] = h.T
    natural = dot(h, w_ref[...]).astype(jnp.bfloat16)
    turned = dot(wt_ref[...], h, NT).astype(jnp.bfloat16)
    for i, (n_ref, t_ref) in enumerate(((q_ref, qt_ref), (k_ref, kt_ref), (v_ref, vt_ref))):
        n_ref[...] = natural[:, i * local : (i + 1) * local]
        t_ref[...] = turned[i * local : (i + 1) * local]


def project(own, other, x_own, x_other, gain, shift, w, wt):
    half, width = x_own.shape
    rows, outs = 2 * half, w.shape[1]
    local = outs // 3
    pieces = half // PIECE
    block = min(256, rows)
    bf16 = jnp.bfloat16

    def whole(shape):
        return pl.BlockSpec(shape, lambda i: (0,) * len(shape), pipeline_mode=pl.Buffered(1))

    natural = pl.BlockSpec((block, local), lambda i: (i, 0))
    turned = pl.BlockSpec((local, block), lambda i: (0, i))
    return pl.pallas_call(
        project_kernel,
        grid=(rows // block,),
        out_shape=[struct((width, rows), bf16)] + [struct((rows, local), bf16)] * 3 + [struct((local, rows), bf16)] * 3,
        in_specs=[SMEM, SMEM]
        + [whole((pieces, PIECE, width))] * 2
        + [whole((1, width))] * 2
        + [whole((width, outs)), whole((outs, width))],
        out_specs=[pl.BlockSpec((width, block), lambda i: (0, i))] + [natural] * 3 + [turned] * 3,
        scratch_shapes=[pltpu.VMEM((rows // PIECE, PIECE, width), bf16)],
        compiler_params=params(40),
        cost_estimate=cost(4 * rows * width * outs, 20e6),
        name="project",
    )(own, other, x_own.reshape(pieces, PIECE, width), x_other.reshape(pieces, PIECE, width), gain, shift, w, wt)


def cell_bounds(len_ref, cnt_ref):
    cells = len_ref.shape[1]
    starts, lives, start = [], [], jnp.int32(0)
    for c in range(cells):
        length = len_ref[0, c]
        starts.append(start)
        lives.append(start + jnp.minimum(length, cnt_ref[0, c]))
        start = start + length
    return starts, lives


def key_range(pos, starts, lives):
    low = jnp.zeros_like(pos) + starts[0]
    high = jnp.zeros_like(pos) + lives[0]
    for start, live in zip(starts[1:], lives[1:]):
        inside = pos >= start
        low = jnp.where(inside, start, low)
        high = jnp.where(inside, live, high)
    return low, high


def attend_kernel(
    own_ref, other_ref, len_ref, cnt_ref, k_ref, qt_ref, vt_ref,
    ot_ref, own_out, other_out, lse_ref,
    natural, bias, top, total, acc,
):
    rows, width = k_ref.shape
    heads = width // HEAD_DIM
    bk, bq = bias.shape
    starts, lives = cell_bounds(len_ref, cnt_ref)
    zeros = jnp.zeros((HEAD_DIM, bq), jnp.bfloat16)
    ones = jnp.ones((16, bk), jnp.bfloat16)

    def query_step(i, carry):
        q0 = pl.multiple_of(i * bq, bq)
        cols = pl.ds(q0, bq)
        low, high = key_range(q0 + lax.broadcasted_iota(jnp.int32, (1, bq), 1), starts, lives)
        first, _ = key_range(q0, starts, lives)
        _, last = key_range(q0 + bq - 1, starts, lives)
        origin = first // 128 * 128
        top[...] = jnp.full_like(top, MASKED)
        total[...] = jnp.zeros_like(total)
        acc[...] = jnp.zeros_like(acc)

        def key_step(j, carry):
            begin = origin + j * bk
            k0 = pl.multiple_of(jnp.minimum(begin, rows - bk), 128)
            keys = pl.ds(k0, bk)
            kpos = k0 + lax.broadcasted_iota(jnp.int32, (bk, bq), 0)
            bias[...] = jnp.where((kpos >= jnp.maximum(low, begin)) & (kpos < high), 0.0, MASKED)

            def score(h):
                lanes = slice(h // 2 * 128, h // 2 * 128 + 128)
                q = qt_ref[h * HEAD_DIM : (h + 1) * HEAD_DIM, cols]
                q = jnp.concatenate([q, zeros] if h % 2 == 0 else [zeros, q], axis=0)
                return dot(k_ref[keys, lanes], q)

            s = [score(0), score(1)]
            ps = {}

            def mix(h):
                p, decay = ps.pop(h)
                sub = slice(h * HEAD_DIM, (h + 1) * HEAD_DIM)
                v = jnp.concatenate([vt_ref[sub, keys], ones], axis=0)
                r = dot(v, p)
                acc[sub, :] = acc[sub, :] * decay + r[:HEAD_DIM]
                total[h : h + 1, :] = total[h : h + 1, :] * decay + r[HEAD_DIM : HEAD_DIM + 1]

            for h in range(heads):
                if h + 2 < heads:
                    s.append(score(h + 2))
                x = s[h] + bias[...]
                old = top[h : h + 1, :]
                new = jnp.maximum(old, jnp.max(x, axis=0, keepdims=True))
                p = jnp.exp(x - new).astype(jnp.bfloat16)
                ps[h] = (p, jnp.exp(old - new))
                top[h : h + 1, :] = new
                if h >= 1:
                    mix(h - 1)
            mix(heads - 1)
            return carry

        lax.fori_loop(0, (last - origin + bk - 1) // bk, key_step, 0)
        for h in range(heads):
            sub = slice(h * HEAD_DIM, (h + 1) * HEAD_DIM)
            acc[sub, :] = acc[sub, :] / total[h : h + 1, :]
            lse_ref[h : h + 1, cols] = top[h : h + 1, :] + jnp.log(total[h : h + 1, :])
        mixed = acc[...]
        ot_ref[:, cols] = mixed.astype(jnp.bfloat16)
        natural[pl.ds(i * (bq // PIECE), bq // PIECE)] = mixed.T.reshape(bq // PIECE, PIECE, width)
        return carry

    lax.fori_loop(0, rows // bq, query_step, 0)

    def step(j, carry):
        own_out[j] = natural[own_ref[j]].astype(jnp.bfloat16)
        other_out[j] = natural[other_ref[j]].astype(jnp.bfloat16)
        return carry

    lax.fori_loop(0, own_out.shape[0], step, 0, unroll=8)


def attend(own, other, lengths, counts, k, qt, vt):
    rows, width = k.shape
    count = own.shape[0]
    bk, bq = min(640, rows), min(256, rows)
    heads = width // HEAD_DIM
    ot, o_own, o_other, lse = pl.pallas_call(
        attend_kernel,
        out_shape=[
            struct((width, rows), jnp.bfloat16),
            struct((count, PIECE, width), jnp.bfloat16),
            struct((count, PIECE, width), jnp.bfloat16),
            struct((8, rows), jnp.float32),
        ],
        in_specs=[SMEM] * 4 + [VMEM] * 3,
        out_specs=[VMEM] * 4,
        scratch_shapes=[
            pltpu.VMEM((rows // PIECE, PIECE, width), jnp.float32),
            pltpu.VMEM((bk, bq), jnp.float32),
            pltpu.VMEM((8, bq), jnp.float32),
            pltpu.VMEM((8, bq), jnp.float32),
            pltpu.VMEM((width, bq), jnp.float32),
        ],
        compiler_params=params(56),
        cost_estimate=cost(2e10, 10e6, heads * rows * rows // 2),
        name="attend",
    )(own, other, lengths, counts, k, qt, vt)
    return ot, o_own.reshape(count * PIECE, width), o_other.reshape(count * PIECE, width), lse


def attend_back_kernel(
    own_ref, other_ref, len_ref, cnt_ref, q_ref, k_ref, v_ref, qt_ref, kt_ref, ot_ref, lse_ref,
    own_in, other_in, out_ref,
    natural, do_t, do_m, q_m, delta, dq_t, dk_acc, dv_acc, bias,
):
    rows, width = k_ref.shape
    heads = width // HEAD_DIM
    bk, bq = bias.shape
    pieces = bq // PIECE
    starts, lives = cell_bounds(len_ref, cnt_ref)
    zeros = jnp.zeros((HEAD_DIM, bq), jnp.bfloat16)

    def place(j, carry):
        natural[own_ref[j]] = own_in[j].astype(jnp.float32)
        natural[other_ref[j]] = other_in[j].astype(jnp.float32)
        return carry

    lax.fori_loop(0, own_in.shape[0], place, 0, unroll=8)
    lane = lax.broadcasted_iota(jnp.int32, (bq, 128), 1)

    def prepare(i, carry):
        q0 = pl.multiple_of(i * bq, bq)
        at = pl.ds(q0, bq)
        do = natural[pl.ds(i * pieces, pieces)].reshape(bq, width)
        dot_t = do.T
        do_t[:, at] = dot_t.astype(jnp.bfloat16)
        for h in range(heads):
            sub = slice(h * HEAD_DIM, (h + 1) * HEAD_DIM)
            delta[h : h + 1, at] = jnp.sum(
                dot_t[sub, :] * ot_ref[sub, at].astype(jnp.float32), axis=0, keepdims=True
            )
            lanes = slice(h // 2 * 128, h // 2 * 128 + 128)
            mine = (lane < HEAD_DIM) if h % 2 == 0 else (lane >= HEAD_DIM)
            do_m[h, at, :] = jnp.where(mine, do[:, lanes], 0.0).astype(jnp.bfloat16)
            q_m[h, at, :] = jnp.where(mine, q_ref[at, lanes].astype(jnp.float32), 0.0).astype(jnp.bfloat16)
        dq_t[:, at] = jnp.zeros((width, bq), jnp.float32)
        return carry

    lax.fori_loop(0, rows // bq, prepare, 0)

    def key_step(j, carry):
        k0 = pl.multiple_of(j * bk, bk)
        keys = pl.ds(k0, bk)
        first, last = jnp.int32(rows), jnp.int32(0)
        for start, live in zip(starts, lives):
            met = (start < k0 + bk) & (live > k0)
            first = jnp.where(met, jnp.minimum(first, start), first)
            last = jnp.where(met, live, last)
        origin = first // 128 * 128
        dk_acc[...] = jnp.zeros_like(dk_acc)
        dv_acc[...] = jnp.zeros_like(dv_acc)

        def query_step(i, carry):
            begin = origin + i * bq
            q0 = pl.multiple_of(jnp.minimum(begin, rows - bq), 128)
            cols = pl.ds(q0, bq)
            qpos = q0 + lax.broadcasted_iota(jnp.int32, (1, bq), 1)
            low, high = key_range(qpos, starts, lives)
            low = jnp.where(qpos < begin, rows, low)
            kpos = k0 + lax.broadcasted_iota(jnp.int32, (bk, bq), 0)
            bias[...] = jnp.where((kpos >= low) & (kpos < high), 0.0, MASKED)

            def first_half(g):
                lanes = slice(g // 2 * 128, g // 2 * 128 + 128)
                sub = slice(g * HEAD_DIM, (g + 1) * HEAD_DIM)
                q, d = qt_ref[sub, cols], do_t[sub, cols]
                order = (lambda t: [t, zeros]) if g % 2 == 0 else (lambda t: [zeros, t])
                s = dot(k_ref[keys, lanes], jnp.concatenate(order(q), axis=0))
                dp = dot(v_ref[keys, lanes], jnp.concatenate(order(d), axis=0))
                return s, dp

            def second_half(g, p, ds):
                lanes = slice(g // 2 * 128, g // 2 * 128 + 128)
                sub = slice(g * HEAD_DIM, (g + 1) * HEAD_DIM)
                dv_acc[:, lanes] += dot(p, do_m[g, cols, :])
                dk_acc[:, lanes] += dot(ds, q_m[g, cols, :])
                dq_t[sub, cols] += dot(kt_ref[sub, keys], ds)

            ready = [first_half(0)]
            last_pair = None
            for g in range(heads):
                if g + 1 < heads:
                    ready.append(first_half(g + 1))
                s, dp = ready[g]
                p = jnp.exp(s + bias[...] - lse_ref[g : g + 1, cols])
                ds = (p * (dp - delta[g : g + 1, cols])).astype(jnp.bfloat16)
                if last_pair is not None:
                    second_half(*last_pair)
                last_pair = (g, p.astype(jnp.bfloat16), ds)
            second_half(*last_pair)
            return carry

        lax.fori_loop(0, (last - origin + bq - 1) // bq, query_step, 0)
        out_ref[1, keys, :] = dk_acc[...].astype(jnp.bfloat16)
        out_ref[2, keys, :] = dv_acc[...].astype(jnp.bfloat16)
        return carry

    lax.fori_loop(0, rows // bk, key_step, 0)

    def finish(i, carry):
        at = pl.ds(pl.multiple_of(i * bq, bq), bq)
        out_ref[0, at, :] = (dq_t[:, at].T * HEAD_DIM**-0.5).astype(jnp.bfloat16)
        return carry

    lax.fori_loop(0, rows // bq, finish, 0)


def attend_back(own, other, lengths, counts, q, k, v, qt, kt, ot, lse, do_own, do_other):
    rows, width = k.shape
    count = own.shape[0]
    bk = bq = min(256, rows)
    heads = width // HEAD_DIM
    return pl.pallas_call(
        attend_back_kernel,
        out_shape=struct((3, rows, width), jnp.bfloat16),
        in_specs=[SMEM] * 4 + [VMEM] * 9,
        out_specs=VMEM,
        scratch_shapes=[
            pltpu.VMEM((rows // PIECE, PIECE, width), jnp.float32),
            pltpu.VMEM((width, rows), jnp.bfloat16),
            pltpu.VMEM((heads, rows, 128), jnp.bfloat16),
            pltpu.VMEM((heads, rows, 128), jnp.bfloat16),
            pltpu.VMEM((8, rows), jnp.float32),
            pltpu.VMEM((width, rows), jnp.float32),
            pltpu.VMEM((bk, width), jnp.float32),
            pltpu.VMEM((bk, width), jnp.float32),
            pltpu.VMEM((bk, bq), jnp.float32),
        ],
        compiler_params=params(58),
        cost_estimate=cost(5e10, 20e6, heads * rows * rows // 2),
        name="attend_back",
    )(
        own, other, lengths, counts, q, k, v, qt, kt, ot, lse,
        do_own.reshape(count, PIECE, width), do_other.reshape(count, PIECE, width),
    )


def feed_kernel(
    x_ref, oa_ref, ob_ref, dy_ref, real_ref, wo_a, wo_b, up_a, up_b, down_a, down_b, gain_ref, shift_ref,
    out_ref, up_left_a, up_left_b, down_left_a, down_left_b, h_ref, right_ref, doa_ref, dob_ref, dy1_ref, norm_ref,
):
    x = x_ref[...].astype(jnp.float32)
    y1 = x + dot(oa_ref[...], wo_a[...]) + dot(ob_ref[...], wo_b[...])
    unit, inverse = norm_unit(y1)
    h = (unit * gain_ref[...] + shift_ref[...]).astype(jnp.bfloat16)
    h_ref[...] = h
    g = dy_ref[...].astype(jnp.float32) * real_ref[...]
    gr = g.astype(jnp.bfloat16)
    right_ref[0] = gr
    mlp = None
    dh = None
    for up, down, up_left, down_left, o_ref in (
        (up_a, down_a, up_left_a, down_left_a, oa_ref),
        (up_b, down_b, up_left_b, down_left_b, ob_ref),
    ):
        hidden = up.shape[1]
        part = min(768, hidden)
        for at in range(0, hidden, part):
            cols = slice(at, at + part)
            u = dot(h, up[:, cols])
            phi = 0.5 * (1.0 + lax.erf(u * 0.7071067811865476))
            act = (u * phi).astype(jnp.bfloat16)
            down_left[:, cols] = act
            slope = phi + u * 0.3989422804014327 * jnp.exp(-0.5 * u * u)
            du = (dot(gr, down[cols, :], NT) * slope).astype(jnp.bfloat16)
            up_left[:, cols] = du
            m = dot(act, down[cols, :])
            d = dot(du, up[:, cols], NT)
            mlp = m if mlp is None else mlp + m
            dh = d if dh is None else dh + d
        local = o_ref.shape[1]
        down_left[:, hidden : hidden + local] = o_ref[...]
        down_left[:, hidden + local :] = jnp.zeros_like(down_left[:, hidden + local :])
    out_ref[...] = (y1 + mlp).astype(jnp.bfloat16)
    sums = jnp.concatenate(
        [jnp.sum(dh * unit, axis=0, keepdims=True), jnp.sum(dh, axis=0, keepdims=True)], axis=0
    )

    @pl.when(pl.program_id(0) == 0)
    def _():
        norm_ref[...] = sums

    @pl.when(pl.program_id(0) > 0)
    def _():
        norm_ref[...] += sums

    dy1 = g + norm_back(dh * gain_ref[...], unit, inverse)
    dy1_ref[...] = dy1
    dar = dy1.astype(jnp.bfloat16)
    right_ref[1] = dar
    doa_ref[...] = dot(dar, wo_a[...], NT).astype(jnp.bfloat16)
    dob_ref[...] = dot(dar, wo_b[...], NT).astype(jnp.bfloat16)


def feed(x, o_own, o_other, dy, real, wo, up, down, gain, shift):
    rows, width = x.shape
    local = o_own.shape[1]
    hidden = up[0].shape[1]
    block = min(256, rows)

    def tall(cols):
        return pl.BlockSpec((block, cols), lambda i: (i, 0))

    def whole(shape):
        return pl.BlockSpec(shape, lambda i: (0, 0), pipeline_mode=pl.Buffered(1))

    bf16 = jnp.bfloat16
    lefts = hidden // 3 * 4
    return pl.pallas_call(
        feed_kernel,
        grid=(rows // block,),
        out_shape=[
            struct((rows, width), bf16),
            struct((rows, hidden), bf16),
            struct((rows, hidden), bf16),
            struct((rows, lefts), bf16),
            struct((rows, lefts), bf16),
            struct((rows, width), bf16),
            struct((2, rows, width), bf16),
            struct((rows, local), bf16),
            struct((rows, local), bf16),
            struct((rows, width), jnp.float32),
            struct((2, width), jnp.float32),
        ],
        in_specs=[tall(width), tall(local), tall(local), tall(width), tall(1)]
        + [whole((local, width))] * 2
        + [whole((width, hidden))] * 2
        + [whole((hidden, width))] * 2
        + [whole((1, width))] * 2,
        out_specs=[
            tall(width),
            tall(hidden),
            tall(hidden),
            tall(lefts),
            tall(lefts),
            tall(width),
            pl.BlockSpec((2, block, width), lambda i: (0, i, 0)),
            tall(local),
            tall(local),
            tall(width),
            pl.BlockSpec((2, width), lambda i: (0, 0)),
        ],
        compiler_params=params(58),
        cost_estimate=cost(2 * rows * width * (hidden * 8 + local * 4), 50e6, rows * hidden * 4),
        name="feed",
    )(x, o_own, o_other, dy, real, *wo, *up, *down, gain, shift)


def weight_kernel(order_ref, left_ref, right_ref, out_ref):
    out_ref[0] = dot(left_ref[...], right_ref[0], TN).astype(jnp.bfloat16)


def weight_add_kernel(order_ref, left_ref, right_ref, more_ref, out_ref):
    out_ref[0] = (dot(left_ref[...], right_ref[0], TN) + more_ref[0].astype(jnp.float32)).astype(jnp.bfloat16)


def weight_grads(left, right, order, more=None):
    rows, lefts = left.shape
    count, _, width = right.shape
    block = lefts // NEAR

    def pick(i, order):
        return (order[i] // (NEAR - 1) if count == 2 else 0, 0, 0)

    out = pl.BlockSpec((1, block, width), lambda i, order: (i, 0, 0))
    operands = (left, right) if more is None else (left, right, more)
    return pl.pallas_call(
        weight_kernel if more is None else weight_add_kernel,
        grid_spec=pltpu.PrefetchScalarGridSpec(
            num_scalar_prefetch=1,
            grid=(NEAR,),
            in_specs=[
                pl.BlockSpec((rows, block), lambda i, order: (0, order[i])),
                pl.BlockSpec((1, rows, width), pick),
            ]
            + ([] if more is None else [pl.BlockSpec((1, block, width), lambda i, order: (order[i], 0, 0))]),
            out_specs=out,
        ),
        out_shape=struct((NEAR, block, width), jnp.bfloat16),
        compiler_params=params(40),
        cost_estimate=cost(2 * rows * width * lefts, 20e6),
        name="weight_grads",
    )(order, *operands)


NEAR = 4
MESH = pl.DeviceIdType.MESH


def padded(rows, size):
    return -(-rows // (16 * size)) * 16 * size


def near_send(block, d, size):
    return lax.ppermute(block, "dp", [(i, i ^ d) for i in range(size)])


def add_up(blocks):
    total = blocks[0].astype(jnp.float32)
    for block in blocks[1:]:
        total = total + block.astype(jnp.float32)
    return total.astype(jnp.bfloat16)


def close_kernel(
    size, own_ref, other_ref, chunk_ref, grads_ref, ht_ref, w_ref, x_ref, dy1_ref, gain_ref, norm2_ref,
    first_out, second_out, rows_own, rows_other, norms_out,
    part, natural, swap_s, swap_r, dx, acc_a, acc_b, land_a, land_b, near_b, sum_b, norm_s, norm_r, norm_t,
    near_sem_s, near_sem_r, far_sem_s, far_sem_r, part_s, part_r, trade_s, trade_r, pass_s, pass_r,
    small_s, small_r, mp_s, mp_r, local,
):
    far = size // NEAR
    bits = [1 << b for b in range(far.bit_length() - 1)]
    me = lax.axis_index("dp")
    core = lax.axis_index("mp")
    f, e = me // NEAR, me % NEAR
    rows_all, local_width = grads_ref.shape[1:]
    width = w_ref.shape[1]
    block = min(256, rows_all)
    bf16 = jnp.bfloat16

    def flip(value, mask, top):
        out, b = 0, 1
        while b < top:
            out = out + b * ((value // b + mask // b) % 2)
            b *= 2
        return out

    barrier = pltpu.get_barrier_semaphore()

    def greet(d, carry):
        pl.semaphore_signal(barrier, inc=1, device_id={"dp": (me + d) % size}, device_id_type=MESH)
        return carry

    lax.fori_loop(1, size, greet, 0)
    pl.semaphore_signal(barrier, inc=1, device_id={"mp": 1 - core}, device_id_type=MESH)
    pl.semaphore_wait(barrier, size)

    def remote(source, target, send, recv, device):
        return pltpu.make_async_remote_copy(
            source, target, send, recv, device_id={"dp": device}, device_id_type=MESH
        )

    def beside(source, target, send, recv):
        return pltpu.make_async_remote_copy(
            source, target, send, recv, device_id={"mp": 1 - core}, device_id_type=MESH
        )

    cut = chunk_ref.shape[1] // 2
    halves = (slice(0, cut), slice(cut, 2 * cut))

    def views(first, second):
        return lambda s, *at: first.at[(*at, halves[s])] if s < 2 else second.at[at]

    inputs, accs = views(chunk_ref, sum_b), views(acc_a, acc_b)
    lands, outs = views(land_a, land_b), views(first_out, second_out)
    held = {b: [m for m in range(far) if m % (2 * b) == 0] for b in bits}
    slot = {}
    for b in bits:
        for m in held[b]:
            slot[b, m] = len(slot)
    arrivals = [(b, m) for b in reversed(bits) for m in held[b]]

    def reduce_copy(s, b, m):
        source = inputs(s, flip(f, m + b, far)) if b == 1 else accs(s, m + b)
        k = slot[b, m]
        return remote(source, lands(s, k), far_sem_s.at[s, k], far_sem_r.at[s, k], flip(f, b, far) * NEAR + e)

    def reduce_start(s, b):
        for m in held[b]:
            reduce_copy(s, b, m).start()

    def reduce_step(s, b):
        for m in held[b]:
            reduce_copy(s, b, m).wait_recv()
            base = inputs(s, flip(f, m, far)) if b == 1 else accs(s, m)
            total = (base[...].astype(jnp.float32) + lands(s, slot[b, m])[...].astype(jnp.float32)).astype(bf16)
            if 2 * b == far:
                outs(s, e, f)[...] = total
            else:
                accs(s, m)[...] = total
        if 2 * b < far:
            reduce_start(s, 2 * b)
        else:
            available(s, 0)

    def spread_copy(s, b, m):
        piece = outs(s, e, flip(f, m, far))
        k = slot[b, m]
        return remote(piece, piece, far_sem_s.at[3 + s, k], far_sem_r.at[3 + s, k], flip(f, b, far) * NEAR + e)

    def spread_arrival(s, b, m):
        piece = outs(s, e, flip(f, m + b, far))
        k = slot[b, m]
        return remote(piece, piece, far_sem_s.at[3 + s, k], far_sem_r.at[3 + s, k], flip(f, b, far) * NEAR + e)

    def near_copy(s, d, m):
        piece = outs(s, e, flip(f, m, far))
        return remote(piece, piece, near_sem_s.at[s, d, m], near_sem_r.at[s, d, m], f * NEAR + flip(e, d, NEAR))

    def near_arrival(s, d, m):
        piece = outs(s, flip(e, d, NEAR), flip(f, m, far))
        return remote(piece, piece, near_sem_s.at[s, d, m], near_sem_r.at[s, d, m], f * NEAR + flip(e, d, NEAR))

    def near_pass(s, m):
        source, to = (1, 2) if m % 2 == 0 else (2, 1)
        piece = outs(s, flip(e, source, NEAR), flip(f, m, far))
        return remote(piece, piece, near_sem_s.at[s, 3, m], near_sem_r.at[s, 3, m], f * NEAR + flip(e, to, NEAR))

    def near_passed(s, m):
        to = 2 if m % 2 == 0 else 1
        piece = outs(s, flip(e, 3, NEAR), flip(f, m, far))
        return remote(piece, piece, near_sem_s.at[s, 3, m], near_sem_r.at[s, 3, m], f * NEAR + flip(e, to, NEAR))

    def available(s, m):
        for b in reversed(bits):
            if m % (2 * b) == 0:
                spread_copy(s, b, m).start()
        for d in (1, 2):
            near_copy(s, d, m).start()

    def arrive(s, b, m):
        spread_arrival(s, b, m).wait_recv()
        available(s, m + b)

    def pass_on(s, m):
        for d in (1, 2):
            near_arrival(s, d, m).wait_recv()
        near_pass(s, m).start()

    share = land_b.shape[1]

    def near_block(index):
        return pl.ds(pl.multiple_of(index * (far * share), 16), far * share)

    def part_copy(d):
        to = flip(e, d, NEAR)
        return remote(part.at[near_block(to)], near_b.at[d], part_s.at[d], part_r.at[d], f * NEAR + to)

    def trade(d):
        to = (me + d) % size
        return remote(dx.at[to], rows_own.at[me], trade_s.at[d], trade_r.at[d], to)

    def trade_arrival(d):
        source = (me - d + size) % size
        return remote(dx.at[source], rows_own.at[source], trade_s.at[d], trade_r.at[d], source)

    def passing(d):
        source = (me - d + size) % size
        return beside(rows_own.at[source], rows_other.at[source], pass_s.at[d], pass_r.at[d])

    def small(d):
        to = (me + d) % size
        return remote(norm_s, norm_r.at[me], small_s.at[d], small_r.at[d], to)

    def small_arrival(d):
        source = (me - d + size) % size
        return remote(norm_s, norm_r.at[source], small_s.at[d], small_r.at[d], source)

    reduce_start(0, 1)
    reduce_start(1, 1)

    tall = width // 4

    def part_step(i, carry):
        for c in range(4):
            value = dot(ht_ref[c * tall : (c + 1) * tall, :], grads_ref[i])
            at = pl.multiple_of(i * width + c * tall, 16)
            part[pl.ds(at, tall), :] = value.astype(bf16)
        return carry

    lax.fori_loop(0, 3, part_step, 0)
    used = 3 * width
    if part.shape[0] > used:
        part[used:, :] = jnp.zeros((part.shape[0] - used, local_width), bf16)
    for d in range(1, NEAR):
        part_copy(d).start()
    reduce_step(0, 1)

    pieces = block // PIECE

    def grad_step(i, carry):
        at = pl.ds(pl.multiple_of(i * block, block), block)
        value = dot(grads_ref[0, at, :], w_ref[0], NT)
        value += dot(grads_ref[1, at, :], w_ref[1], NT)
        value += dot(grads_ref[2, at, :], w_ref[2], NT)
        natural[pl.ds(i * pieces, pieces)] = value.reshape(pieces, PIECE, width)
        return carry

    lax.fori_loop(0, rows_all // block, grad_step, 0)

    def pack(j, carry):
        swap_s[j] = natural[other_ref[j]].astype(bf16)
        return carry

    lax.fori_loop(0, swap_s.shape[0], pack, 0, unroll=8)
    half = beside(swap_s, swap_r, mp_s.at[0], mp_r.at[0])
    half.start()
    reduce_step(1, 1)
    for b in bits[1:]:
        reduce_step(0, b)

    half.wait_recv()
    group_rows = dx.shape[1]
    norm_s[...] = jnp.zeros_like(norm_s)
    norm_s[2:4, :] = norm2_ref[...]
    mine = x_ref.shape[0]
    step_rows = min(256, mine)
    step_pieces = step_rows // PIECE

    def finish_step(i, carry):
        def take(j, inner):
            k = i * step_pieces + j
            natural_own[j] = natural[own_ref[k]] + swap_r[k].astype(jnp.float32)
            return inner

        lax.fori_loop(0, step_pieces, take, 0, unroll=8)
        at = pl.ds(pl.multiple_of(i * step_rows, step_rows), step_rows)
        dh = natural_own[...].reshape(step_rows, width)
        unit, inverse = norm_unit(x_ref[at, :].astype(jnp.float32))
        norm_s[0:1, :] += jnp.sum(dh * unit, axis=0, keepdims=True)
        norm_s[1:2, :] += jnp.sum(dh, axis=0, keepdims=True)
        value = dy1_ref[at, :] + norm_back(dh * gain_ref[...], unit, inverse)
        per_step = step_rows // group_rows
        dx[pl.ds(i * per_step, per_step)] = value.astype(bf16).reshape(per_step, group_rows, width)
        return carry

    natural_own = norm_t
    lax.fori_loop(0, mine // step_rows, finish_step, 0)

    def send(d, carry):
        trade(d).start()
        return carry

    lax.fori_loop(1, size, send, 0)

    def send_small(d, carry):
        small(d).start()
        return carry

    lax.fori_loop(1, size, send_small, 0)
    keep = pltpu.make_async_copy(dx.at[me], rows_own.at[me], local.at[0])
    keep.start()
    keep_small = pltpu.make_async_copy(norm_s, norm_r.at[me], local.at[1])
    keep_small.start()

    for b in bits[1:]:
        reduce_step(1, b)
    for d in range(1, NEAR):
        part_copy(d).wait_recv()
    own_part = part.at[near_block(e)]
    for j in range(far):
        at = slice(j * share, (j + 1) * share)
        total = own_part[at, :].astype(jnp.float32)
        for d in range(1, NEAR):
            total = total + near_b[d, at, :].astype(jnp.float32)
        sum_b[j] = total.astype(bf16)
    reduce_start(2, 1)

    top = bits[-1]
    pass_on(0, 0)
    arrive(0, top, 0)
    pass_on(1, 0)
    reduce_step(2, 1)
    arrive(1, top, 0)
    for b, m in arrivals[1:]:
        arrive(0, b, m)
    for b in bits[1:]:
        reduce_step(2, b)
    for b, m in arrivals[1:]:
        arrive(1, b, m)
    for s in range(2):
        for b, m in arrivals:
            pass_on(s, m + b)
    pass_on(2, 0)
    for b, m in arrivals:
        arrive(2, b, m)
    for b, m in arrivals:
        pass_on(2, m + b)
    keep.wait()
    passing(0).start()

    def settle(d, carry):
        trade_arrival(d).wait_recv()
        passing(d).start()
        return carry

    lax.fori_loop(1, size, settle, 0)
    keep_small.wait()

    def settle_small(d, carry):
        small_arrival(d).wait_recv()
        return carry

    lax.fori_loop(1, size, settle_small, 0)

    def add(g, carry):
        return carry + norm_r[g]

    total = lax.fori_loop(0, size, add, jnp.zeros(norm_s.shape, jnp.float32))
    for d in range(1, size):
        small(d).wait_send()
    norm_s[...] = total
    last = beside(norm_s, norm_r.at[size], mp_s.at[1], mp_r.at[1])
    last.start()
    last.wait()
    norms_out[...] = norm_s[...] + norm_r[size]

    for s in range(3):
        for m in range(far):
            near_passed(s, m).wait_recv()
    half.wait_send()
    for d in range(1, NEAR):
        part_copy(d).wait_send()
    for s in range(3):
        for b in bits:
            for m in held[b]:
                reduce_copy(s, b, m).wait_send()
                spread_copy(s, b, m).wait_send()
        for m in range(far):
            near_copy(s, 1, m).wait_send()
            near_copy(s, 2, m).wait_send()
            near_pass(s, m).wait_send()

    passing(0).wait()

    def close(d, carry):
        trade(d).wait_send()
        passing(d).wait()
        return carry

    lax.fori_loop(1, size, close, 0)


def close(own, other, chunk, grads, ht, w, x, dy1, gain, norm2, size):
    far = size // NEAR
    a, width = chunk.shape
    rows, local = grads.shape[1:]
    b = padded(3 * width, size)
    n = x.shape[0] // size
    bf16, f32 = jnp.bfloat16, jnp.float32
    share_a, share_b = a // far, b // size
    dma = pltpu.SemaphoreType.DMA
    step = min(256, x.shape[0])
    first, second, rows_own, rows_other, norms = pl.pallas_call(
        functools.partial(close_kernel, size),
        out_shape=[
            struct((NEAR, far, share_a, width), bf16),
            struct((NEAR, far, share_b, local), bf16),
            struct((size, n, width), bf16),
            struct((size, n, width), bf16),
            struct((8, width), f32),
        ],
        in_specs=[SMEM, SMEM] + [VMEM] * 8,
        out_specs=[VMEM] * 5,
        scratch_shapes=[
            pltpu.VMEM((b, local), bf16),
            pltpu.VMEM((rows // PIECE, PIECE, width), f32),
            pltpu.VMEM((x.shape[0] // PIECE, PIECE, width), bf16),
            pltpu.VMEM((x.shape[0] // PIECE, PIECE, width), bf16),
            pltpu.VMEM((size, n, width), bf16),
            pltpu.VMEM((far, share_a, width), bf16),
            pltpu.VMEM((far, share_b, local), bf16),
            pltpu.VMEM((far, share_a, width), bf16),
            pltpu.VMEM((far, share_b, local), bf16),
            pltpu.VMEM((NEAR, b // NEAR, local), bf16),
            pltpu.VMEM((far, share_b, local), bf16),
            pltpu.VMEM((8, width), f32),
            pltpu.VMEM((size + 1, 8, width), f32),
            pltpu.VMEM((step // PIECE, PIECE, width), f32),
            dma((3, NEAR, far)),
            dma((3, NEAR, far)),
            dma((6, far)),
            dma((6, far)),
            dma((NEAR,)),
            dma((NEAR,)),
            dma((size,)),
            dma((size,)),
            dma((size,)),
            dma((size,)),
            dma((size,)),
            dma((size,)),
            dma((2,)),
            dma((2,)),
            dma((2,)),
        ],
        compiler_params=pltpu.CompilerParams(
            collective_id=0, has_side_effects=True, vmem_limit_bytes=60 * MIB
        ),
        cost_estimate=cost(8 * rows * width * local, 1e8),
        name="close",
    )(own, other, chunk.reshape(far, share_a, width), grads, ht, w, x, dy1, gain, norm2)
    return (
        first.reshape(NEAR * a, width),
        second.reshape(b, local),
        rows_own.reshape(-1, width),
        rows_other.reshape(-1, width),
        norms,
    )


def widen_kernel(first_ref, second_ref, up_ref, down_ref, out_ref, qkv_ref):
    f32 = jnp.float32
    count = first_ref.shape[0]
    up_rows = up_ref.shape[1] // count
    down_rows = down_ref.shape[0] // (count - 1)
    for e in range(count):
        up_ref[:, e * up_rows : (e + 1) * up_rows] = first_ref[e, :up_rows, :].astype(f32).T
    for e in range(count - 1):
        at = slice(e * down_rows, (e + 1) * down_rows)
        down_ref[at, :] = first_ref[e, up_rows : up_rows + down_rows, :].astype(f32)
    out_ref[...] = first_ref[count - 1, up_rows : up_rows + out_ref.shape[0], :].astype(f32)
    qkv_ref[...] = second_ref[: qkv_ref.shape[0], :].astype(f32)


def widen(first, second, hidden, local, rows):
    width = first.shape[2]
    f32 = jnp.float32
    return pl.pallas_call(
        widen_kernel,
        out_shape=[
            struct((width, hidden), f32),
            struct((hidden, width), f32),
            struct((local, width), f32),
            struct((rows, second.shape[1]), f32),
        ],
        in_specs=[VMEM] * 2,
        out_specs=[VMEM] * 4,
        compiler_params=params(40),
        cost_estimate=cost(0, 22e6),
        name="widen",
    )(first, second)


def swap(value):
    return lax.ppermute(value, "mp", [(0, 1), (1, 0)])


def exchange(value):
    return lax.all_to_all(value, "dp", split_axis=0, concat_axis=0, tiled=True)


def body(
    tokens, out_grad, lengths, counts, dest_slot, qkv_weight, out_weight, up_weight, down_weight,
    norm1_gain, norm1_shift, norm2_gain, norm2_shift,
):
    groups = lax.axis_size("dp")
    me = lax.axis_index("dp")
    core = lax.axis_index("mp")
    rows, width = tokens.shape
    per = rows // PIECE
    capacity = per // groups
    half = capacity // 2
    local = qkv_weight.shape[2]
    bf16 = jnp.bfloat16

    slots = dest_slot.reshape(groups, per)
    my_slots = lax.dynamic_index_in_dim(slots, me, 0, keepdims=True)
    group_ids = jnp.arange(groups, dtype=jnp.int32)[:, None]
    piece_ids = jnp.broadcast_to(jnp.arange(per, dtype=jnp.int32)[None, :], (groups, per))
    source = slot_table(my_slots // per == group_ids, piece_ids, capacity)
    target = slot_table(slots // per == me, slots - me * per, capacity)

    def halves(table):
        own = lax.dynamic_slice_in_dim(table, core * half, half, 1)
        other = lax.dynamic_slice_in_dim(table, (1 - core) * half, half, 1)
        return own.reshape(-1), other.reshape(-1)

    src_own, src_other = halves(source)
    own, other = halves(target)

    x_own = exchange(gather_pieces(src_own, tokens))
    dy_send = gather_pieces(src_own, out_grad)
    scaled = jnp.concatenate(
        [qkv_weight[0] * jnp.asarray(HEAD_DIM**-0.5, bf16), qkv_weight[1], qkv_weight[2]], axis=1
    )
    scaled_t = scaled.T
    wo_other, up_other, down_other = swap(out_weight), swap(up_weight), swap(down_weight)
    gain1, shift1 = norm1_gain[None], norm1_shift[None]
    gain2, shift2 = norm2_gain[None], norm2_shift[None]
    x_own, dy_send, scaled, scaled_t, wo_other, up_other, down_other, own, other, gain1, shift1, gain2, shift2 = (
        lax.optimization_barrier(
            (
                x_own, dy_send, scaled, scaled_t, wo_other, up_other, down_other,
                own, other, gain1, shift1, gain2, shift2,
            )
        )
    )
    wo, up, down = (out_weight, wo_other), (up_weight, up_other), (down_weight, down_other)
    x_other = swap(x_own)

    h1_t, q, k, v, qt, kt, vt = project(own, other, x_own, x_other, gain1, shift1, scaled, scaled_t)

    dy_own = exchange(dy_send)
    ot, o_own, o_send, lse = attend(own, other, lengths, counts, k, qt, vt)
    o_other = swap(o_send)

    place = (own[:, None] * PIECE + jnp.arange(PIECE, dtype=jnp.int32)[None, :]).reshape(-1, 1)
    real, start = jnp.zeros(place.shape, jnp.bool_), jnp.int32(0)
    for c in range(lengths.shape[1]):
        live = start + jnp.minimum(lengths[0, c], counts[0, c])
        real, start = real | ((place >= start) & (place < live)), start + lengths[0, c]
    real = real.astype(jnp.float32)

    out_rows, up_own, up_other_left, down_own, down_other_left, h2, right, do_own, do_send, dy1, norm2 = feed(
        x_own, o_own, o_other, dy_own, real, wo, up, down, gain2, shift2
    )
    do_other = swap(do_send)
    out_back = exchange(out_rows)

    e = me % NEAR
    natural_order = jnp.arange(NEAR, dtype=jnp.int32)
    order = natural_order ^ e
    up_more = swap(weight_grads(up_other_left, h2[None], natural_order))
    down_send = weight_grads(down_other_left, right, natural_order)
    up_blocks = weight_grads(up_own, h2[None], order, up_more)
    down_own, up_blocks = lax.optimization_barrier((down_own, up_blocks))
    up_got = [near_send(up_blocks[d], d, groups) for d in (1, 2)]
    down_blocks = weight_grads(down_own, right, order, swap(down_send))
    down_blocks, do_own, do_other = lax.optimization_barrier((down_blocks, do_own, do_other))
    down_got = [near_send(down_blocks[d], d, groups) for d in (1, 2)]
    both_got = near_send(jnp.concatenate([up_blocks[3], down_blocks[3]], axis=0), 3, groups)
    grads = attend_back(own, other, lengths, counts, q, k, v, qt, kt, ot, lse, do_own, do_other)
    up_got, down_got, both_got, grads, out_back = lax.optimization_barrier(
        (up_got, down_got, both_got, grads, out_back)
    )
    up_rows = up_blocks.shape[1]
    chunk = jnp.concatenate(
        [
            add_up([up_blocks[0], *up_got, both_got[:up_rows]]),
            add_up([down_blocks[0], *down_got, both_got[up_rows:]]),
        ],
        axis=0,
    )
    used = chunk.shape[0]
    chunk = jnp.pad(chunk, ((0, -used % (32 * (groups // NEAR))), (0, 0)))
    weights, qkv_grad, dx_own, dx_other, norms = close(
        own, other, chunk, grads, h1_t, qkv_weight, x_own, dy1, gain1, norm2, groups
    )
    weights, qkv_grad, dx_own, dx_other, norms, out_back = lax.optimization_barrier(
        (weights, qkv_grad, dx_own, dx_other, norms, out_back)
    )
    hidden = up_weight.shape[1]
    up_grad, down_grad, wo_grad, qkv_grad = widen(
        weights.reshape(NEAR, -1, width), qkv_grad, hidden, local, 3 * width
    )
    qkv_grad = qkv_grad.reshape(3, width, local)

    mixed_out = merge_pieces(src_own, src_other, out_back, swap(out_back))
    input_grad = merge_pieces(src_own, src_other, dx_own, dx_other)
    return (
        mixed_out, input_grad, qkv_grad, wo_grad, up_grad, down_grad,
        norms[0], norms[1], norms[2], norms[3],
    )


def solution(mesh):
    in_specs = (
        P("dp", None), P("dp", None), P("dp", None), P("dp", None), P(),
        P(None, None, "mp"), P("mp", None), P(None, "mp"), P("mp", None), P(), P(), P(), P(),
    )
    out_specs = (
        P("dp", None), P("dp", None), P(None, None, "mp"), P("mp", None), P(None, "mp"), P("mp", None),
        P(), P(), P(), P(),
    )
    return jax.shard_map(body, mesh=mesh, in_specs=in_specs, out_specs=out_specs, check_vma=False)
```

```python
import functools

import jax
import jax.numpy as jnp
from jax import lax
from jax.experimental import pallas as pl
from jax.experimental.pallas import tpu as pltpu
from jax.sharding import PartitionSpec as P

HEAD_DIM = 64
PIECE = 8
NORM_EPS = 1e-05
MASKED = -1e30
MIB = 2**20
VMEM = pl.BlockSpec(memory_space=pltpu.VMEM)
SMEM = pl.BlockSpec(memory_space=pltpu.SMEM)
NEAR = 4
MESH = pl.DeviceIdType.MESH
ANYWHERE = pl.BlockSpec(memory_space=pl.ANY)
NT = (((1,), (1,)), ((), ()))
TN = (((0,), (0,)), ((), ()))


def params(mib):
    return pltpu.CompilerParams(vmem_limit_bytes=mib * MIB)


def cost(flops, nbytes, transcendentals=0):
    return pl.CostEstimate(
        flops=int(flops), bytes_accessed=int(nbytes), transcendentals=int(transcendentals)
    )


def struct(shape, dtype):
    return jax.ShapeDtypeStruct(shape, dtype)


def dot(a, b, dims=None):
    if dims is None:
        return jnp.dot(a, b, preferred_element_type=jnp.float32)
    return lax.dot_general(a, b, dims, preferred_element_type=jnp.float32)


def norm_unit(values):
    mean = jnp.mean(values, axis=-1, keepdims=True)
    centred = values - mean
    variance = jnp.mean(centred * centred, axis=-1, keepdims=True)
    inverse = lax.rsqrt(variance + NORM_EPS)
    return centred * inverse, inverse


def norm_back(grad_unit, unit, inverse):
    first = jnp.mean(grad_unit, axis=-1, keepdims=True)
    second = jnp.mean(grad_unit * unit, axis=-1, keepdims=True)
    return inverse * (grad_unit - first - unit * second)


def slot_table(chosen, values, capacity):
    per = chosen.shape[1]
    place = lax.broadcasted_iota(jnp.int32, (per, per), 0)
    earlier = place < lax.broadcasted_iota(jnp.int32, (per, per), 1)
    rank = dot(chosen.astype(jnp.bfloat16), earlier.astype(jnp.bfloat16)).astype(jnp.int32)
    rank = jnp.where(chosen, rank, -1)
    ranks = jnp.arange(capacity, dtype=jnp.int32)
    hit = rank[:, None, :] == ranks[None, :, None]
    return jnp.sum(jnp.where(hit, values[:, None, :], 0), axis=2)


def gather_kernel(index_ref, source_ref, out_ref):
    def step(j, carry):
        out_ref[j] = source_ref[index_ref[j]]
        return carry

    lax.fori_loop(0, out_ref.shape[0], step, 0, unroll=8)


def gather_pieces(index, source):
    rows, width = source.shape
    count = index.shape[0]
    out = pl.pallas_call(
        gather_kernel,
        out_shape=struct((count, PIECE, width), source.dtype),
        in_specs=[SMEM, VMEM],
        out_specs=VMEM,
        compiler_params=params(60),
        cost_estimate=cost(0, 3 * rows * width),
        name="gather_pieces",
    )(index, source.reshape(rows // PIECE, PIECE, width))
    return out.reshape(count * PIECE, width)


def split_kernel(own_ref, other_ref, source_ref, own_out, other_out):
    def step(j, carry):
        own_out[j] = source_ref[own_ref[j]]
        other_out[j] = source_ref[other_ref[j]]
        return carry

    lax.fori_loop(0, own_out.shape[0], step, 0, unroll=8)


def split_pieces(own, other, source):
    rows, width = source.shape
    count = own.shape[0]
    outs = pl.pallas_call(
        split_kernel,
        out_shape=[struct((count, PIECE, width), source.dtype)] * 2,
        in_specs=[SMEM, SMEM, VMEM],
        out_specs=[VMEM, VMEM],
        compiler_params=params(60),
        cost_estimate=cost(0, 4 * rows * width),
        name="split_pieces",
    )(own, other, source.reshape(rows // PIECE, PIECE, width))
    return tuple(o.reshape(count * PIECE, width) for o in outs)


def merge_kernel(own_ref, other_ref, own_in, other_in, out_ref):
    def step(j, carry):
        out_ref[own_ref[j]] = own_in[j]
        out_ref[other_ref[j]] = other_in[j]
        return carry

    lax.fori_loop(0, own_in.shape[0], step, 0, unroll=8)


def merge_pieces(own, other, own_rows, other_rows):
    rows, width = own_rows.shape
    out = pl.pallas_call(
        merge_kernel,
        out_shape=struct((2 * rows // PIECE, PIECE, width), own_rows.dtype),
        in_specs=[SMEM, SMEM, VMEM, VMEM],
        out_specs=VMEM,
        compiler_params=params(60),
        cost_estimate=cost(0, 8 * rows * width),
        name="merge_pieces",
    )(
        own,
        other,
        own_rows.reshape(rows // PIECE, PIECE, width),
        other_rows.reshape(rows // PIECE, PIECE, width),
    )
    return out.reshape(2 * rows, width)


def project_kernel(
    own_ref, other_ref, own_in, other_in, gain_ref, shift_ref, w_ref, wt_ref,
    ht_ref, q_ref, k_ref, v_ref, qt_ref, kt_ref, vt_ref, x_all,
):
    @pl.when(pl.program_id(0) == 0)
    def _():
        def step(j, carry):
            x_all[own_ref[j]] = own_in[j]
            x_all[other_ref[j]] = other_in[j]
            return carry

        lax.fori_loop(0, own_in.shape[0], step, 0, unroll=8)

    block, local = q_ref.shape
    pieces = block // PIECE
    x = x_all[pl.ds(pl.program_id(0) * pieces, pieces)].astype(jnp.float32).reshape(block, -1)
    unit, _ = norm_unit(x)
    h = (unit * gain_ref[...] + shift_ref[...]).astype(jnp.bfloat16)
    ht_ref[...] = h.T
    for i, (n_ref, t_ref) in enumerate(((q_ref, qt_ref), (k_ref, kt_ref), (v_ref, vt_ref))):
        scale = HEAD_DIM**-0.5 if i == 0 else 1.0
        n_ref[...] = (dot(h, w_ref[i]) * scale).astype(jnp.bfloat16)
        t_ref[...] = (dot(wt_ref[i], h, NT) * scale).astype(jnp.bfloat16)


def project(own, other, x_own, x_other, gain, shift, w, wt):
    half, width = x_own.shape
    rows, local = 2 * half, w.shape[2]
    outs = 3 * local
    pieces = half // PIECE
    block = min(256, rows)
    bf16 = jnp.bfloat16

    def whole(shape):
        return pl.BlockSpec(shape, lambda i: (0,) * len(shape), pipeline_mode=pl.Buffered(1))

    natural = pl.BlockSpec((block, local), lambda i: (i, 0))
    turned = pl.BlockSpec((local, block), lambda i: (0, i))
    return pl.pallas_call(
        project_kernel,
        grid=(rows // block,),
        out_shape=[struct((width, rows), bf16)] + [struct((rows, local), bf16)] * 3 + [struct((local, rows), bf16)] * 3,
        in_specs=[SMEM, SMEM]
        + [whole((pieces, PIECE, width))] * 2
        + [whole((1, width))] * 2
        + [whole(w.shape), whole(wt.shape)],
        out_specs=[pl.BlockSpec((width, block), lambda i: (0, i))] + [natural] * 3 + [turned] * 3,
        scratch_shapes=[pltpu.VMEM((rows // PIECE, PIECE, width), bf16)],
        compiler_params=params(60),
        cost_estimate=cost(4 * rows * width * outs, 20e6),
        name="project",
    )(own, other, x_own.reshape(pieces, PIECE, width), x_other.reshape(pieces, PIECE, width), gain, shift, w, wt)


def cell_bounds(len_ref, cnt_ref):
    cells = len_ref.shape[1]
    starts, lives, start = [], [], jnp.int32(0)
    for c in range(cells):
        length = len_ref[0, c]
        starts.append(start)
        lives.append(start + jnp.minimum(length, cnt_ref[0, c]))
        start = start + length
    return starts, lives


def key_range(pos, starts, lives):
    low = jnp.zeros_like(pos) + starts[0]
    high = jnp.zeros_like(pos) + lives[0]
    for start, live in zip(starts[1:], lives[1:]):
        inside = pos >= start
        low = jnp.where(inside, start, low)
        high = jnp.where(inside, live, high)
    return low, high


def load_all(sems, *pairs):
    loads = [pltpu.make_async_copy(source, target, sems.at[i]) for i, (source, target) in enumerate(pairs)]
    for one in loads:
        one.start()
    for one in loads:
        one.wait()


def attend_kernel(
    own_ref, other_ref, len_ref, cnt_ref, k_in, qt_in, vt_in,
    ot_ref, own_out, other_out, lse_ref,
    k_ref, qt_ref, vt_ref, natural, bias, top, total, acc, load,
):
    load_all(load, (k_in, k_ref), (qt_in, qt_ref), (vt_in, vt_ref))
    rows, width = k_ref.shape
    heads = width // HEAD_DIM
    bk, bq = bias.shape
    starts, lives = cell_bounds(len_ref, cnt_ref)
    zeros = jnp.zeros((HEAD_DIM, bq), jnp.bfloat16)
    ones = jnp.ones((16, bk), jnp.bfloat16)

    def query_step(i, carry):
        q0 = pl.multiple_of(i * bq, bq)
        cols = pl.ds(q0, bq)
        low, high = key_range(q0 + lax.broadcasted_iota(jnp.int32, (1, bq), 1), starts, lives)
        first, _ = key_range(q0, starts, lives)
        _, last = key_range(q0 + bq - 1, starts, lives)
        origin = first // 128 * 128
        top[...] = jnp.full_like(top, MASKED)
        total[...] = jnp.zeros_like(total)
        acc[...] = jnp.zeros_like(acc)

        def key_step(j, carry):
            begin = origin + j * bk
            k0 = pl.multiple_of(jnp.minimum(begin, rows - bk), 128)
            keys = pl.ds(k0, bk)
            kpos = k0 + lax.broadcasted_iota(jnp.int32, (bk, bq), 0)
            bias[...] = jnp.where((kpos >= jnp.maximum(low, begin)) & (kpos < high), 0.0, MASKED)

            def score(h):
                lanes = slice(h // 2 * 128, h // 2 * 128 + 128)
                q = qt_ref[h * HEAD_DIM : (h + 1) * HEAD_DIM, cols]
                q = jnp.concatenate([q, zeros] if h % 2 == 0 else [zeros, q], axis=0)
                return dot(k_ref[keys, lanes], q)

            s = [score(0), score(1)]
            ps = {}

            def mix(h):
                p, decay = ps.pop(h)
                sub = slice(h * HEAD_DIM, (h + 1) * HEAD_DIM)
                v = jnp.concatenate([vt_ref[sub, keys], ones], axis=0)
                r = dot(v, p)
                acc[sub, :] = acc[sub, :] * decay + r[:HEAD_DIM]
                total[h : h + 1, :] = total[h : h + 1, :] * decay + r[HEAD_DIM : HEAD_DIM + 1]

            for h in range(heads):
                if h + 2 < heads:
                    s.append(score(h + 2))
                x = s[h] + bias[...]
                old = top[h : h + 1, :]
                new = jnp.maximum(old, jnp.max(x, axis=0, keepdims=True))
                p = jnp.exp(x - new).astype(jnp.bfloat16)
                ps[h] = (p, jnp.exp(old - new))
                top[h : h + 1, :] = new
                if h >= 1:
                    mix(h - 1)
            mix(heads - 1)
            return carry

        lax.fori_loop(0, (last - origin + bk - 1) // bk, key_step, 0)
        for h in range(heads):
            sub = slice(h * HEAD_DIM, (h + 1) * HEAD_DIM)
            acc[sub, :] = acc[sub, :] / total[h : h + 1, :]
            lse_ref[h : h + 1, cols] = top[h : h + 1, :] + jnp.log(total[h : h + 1, :])
        mixed = acc[...]
        ot_ref[:, cols] = mixed.astype(jnp.bfloat16)
        natural[pl.ds(i * (bq // PIECE), bq // PIECE)] = mixed.T.reshape(bq // PIECE, PIECE, width)
        return carry

    lax.fori_loop(0, rows // bq, query_step, 0)

    def step(j, carry):
        own_out[j] = natural[own_ref[j]].astype(jnp.bfloat16)
        other_out[j] = natural[other_ref[j]].astype(jnp.bfloat16)
        return carry

    lax.fori_loop(0, own_out.shape[0], step, 0, unroll=8)


def attend(own, other, lengths, counts, k, qt, vt):
    rows, width = k.shape
    count = own.shape[0]
    bk, bq = min(640, rows), min(256, rows)
    heads = width // HEAD_DIM
    ot, o_own, o_other, lse = pl.pallas_call(
        attend_kernel,
        out_shape=[
            struct((width, rows), jnp.bfloat16),
            struct((count, PIECE, width), jnp.bfloat16),
            struct((count, PIECE, width), jnp.bfloat16),
            struct((8, rows), jnp.float32),
        ],
        in_specs=[SMEM] * 4 + [ANYWHERE] * 3,
        out_specs=[VMEM] * 4,
        scratch_shapes=[
            *[pltpu.VMEM(one.shape, one.dtype) for one in (k, qt, vt)],
            pltpu.VMEM((rows // PIECE, PIECE, width), jnp.float32),
            pltpu.VMEM((bk, bq), jnp.float32),
            pltpu.VMEM((8, bq), jnp.float32),
            pltpu.VMEM((8, bq), jnp.float32),
            pltpu.VMEM((width, bq), jnp.float32),
            pltpu.SemaphoreType.DMA((3,)),
        ],
        compiler_params=params(60),
        cost_estimate=cost(2e10, 10e6, heads * rows * rows // 2),
        name="attend",
    )(own, other, lengths, counts, k, qt, vt)
    return ot, o_own.reshape(count * PIECE, width), o_other.reshape(count * PIECE, width), lse


def attend_back_kernel(
    own_ref, other_ref, len_ref, cnt_ref, q_in, k_in, v_in, qt_in, kt_in, ot_in, lse_in,
    do_own, do_other, out_ref,
    own_in, other_in, q_ref, ot_ref, k_ref, v_ref, qt_ref, kt_ref, lse_ref, natural, do_t, do_m, q_m, delta, dq_t, dk_acc, dv_acc, bias, load,
):
    load_all(
        load, (do_own, own_in), (do_other, other_in), (q_in, q_ref), (ot_in, ot_ref),
        (k_in, k_ref), (v_in, v_ref), (qt_in, qt_ref), (kt_in, kt_ref), (lse_in, lse_ref),
    )
    rows, width = k_ref.shape
    heads = width // HEAD_DIM
    bk, bq = bias.shape
    pieces = bq // PIECE
    starts, lives = cell_bounds(len_ref, cnt_ref)
    zeros = jnp.zeros((HEAD_DIM, bq), jnp.bfloat16)

    def place(j, carry):
        natural[own_ref[j]] = own_in[j].astype(jnp.float32)
        natural[other_ref[j]] = other_in[j].astype(jnp.float32)
        return carry

    lax.fori_loop(0, own_in.shape[0], place, 0, unroll=8)
    lane = lax.broadcasted_iota(jnp.int32, (bq, 128), 1)

    def prepare(i, carry):
        q0 = pl.multiple_of(i * bq, bq)
        at = pl.ds(q0, bq)
        do = natural[pl.ds(i * pieces, pieces)].reshape(bq, width)
        dot_t = do.T
        do_t[:, at] = dot_t.astype(jnp.bfloat16)
        for h in range(heads):
            sub = slice(h * HEAD_DIM, (h + 1) * HEAD_DIM)
            delta[h : h + 1, at] = jnp.sum(
                dot_t[sub, :] * ot_ref[sub, at].astype(jnp.float32), axis=0, keepdims=True
            )
            lanes = slice(h // 2 * 128, h // 2 * 128 + 128)
            mine = (lane < HEAD_DIM) if h % 2 == 0 else (lane >= HEAD_DIM)
            do_m[h, at, :] = jnp.where(mine, do[:, lanes], 0.0).astype(jnp.bfloat16)
            q_m[h, at, :] = jnp.where(mine, q_ref[at, lanes].astype(jnp.float32), 0.0).astype(jnp.bfloat16)
        dq_t[:, at] = jnp.zeros((width, bq), jnp.float32)
        return carry

    lax.fori_loop(0, rows // bq, prepare, 0)

    def key_step(j, carry):
        k0 = pl.multiple_of(j * bk, bk)
        keys = pl.ds(k0, bk)
        first, last = jnp.int32(rows), jnp.int32(0)
        for start, live in zip(starts, lives):
            met = (start < k0 + bk) & (live > k0)
            first = jnp.where(met, jnp.minimum(first, start), first)
            last = jnp.where(met, live, last)
        origin = first // 128 * 128
        dk_acc[...] = jnp.zeros_like(dk_acc)
        dv_acc[...] = jnp.zeros_like(dv_acc)

        def query_step(i, carry):
            begin = origin + i * bq
            q0 = pl.multiple_of(jnp.minimum(begin, rows - bq), 128)
            cols = pl.ds(q0, bq)
            qpos = q0 + lax.broadcasted_iota(jnp.int32, (1, bq), 1)
            low, high = key_range(qpos, starts, lives)
            low = jnp.where(qpos < begin, rows, low)
            kpos = k0 + lax.broadcasted_iota(jnp.int32, (bk, bq), 0)
            bias[...] = jnp.where((kpos >= low) & (kpos < high), 0.0, MASKED)

            def first_half(g):
                lanes = slice(g // 2 * 128, g // 2 * 128 + 128)
                sub = slice(g * HEAD_DIM, (g + 1) * HEAD_DIM)
                q, d = qt_ref[sub, cols], do_t[sub, cols]
                order = (lambda t: [t, zeros]) if g % 2 == 0 else (lambda t: [zeros, t])
                s = dot(k_ref[keys, lanes], jnp.concatenate(order(q), axis=0))
                dp = dot(v_ref[keys, lanes], jnp.concatenate(order(d), axis=0))
                return s, dp

            def second_half(g, p, ds):
                lanes = slice(g // 2 * 128, g // 2 * 128 + 128)
                sub = slice(g * HEAD_DIM, (g + 1) * HEAD_DIM)
                dv_acc[:, lanes] += dot(p, do_m[g, cols, :])
                dk_acc[:, lanes] += dot(ds, q_m[g, cols, :])
                dq_t[sub, cols] += dot(kt_ref[sub, keys], ds)

            ready = [first_half(0)]
            last_pair = None
            for g in range(heads):
                if g + 1 < heads:
                    ready.append(first_half(g + 1))
                s, dp = ready[g]
                p = jnp.exp(s + bias[...] - lse_ref[g : g + 1, cols])
                ds = (p * (dp - delta[g : g + 1, cols])).astype(jnp.bfloat16)
                if last_pair is not None:
                    second_half(*last_pair)
                last_pair = (g, p.astype(jnp.bfloat16), ds)
            second_half(*last_pair)
            return carry

        lax.fori_loop(0, (last - origin + bq - 1) // bq, query_step, 0)
        out_ref[1, keys, :] = dk_acc[...].astype(jnp.bfloat16)
        out_ref[2, keys, :] = dv_acc[...].astype(jnp.bfloat16)
        return carry

    lax.fori_loop(0, rows // bk, key_step, 0)

    def finish(i, carry):
        at = pl.ds(pl.multiple_of(i * bq, bq), bq)
        out_ref[0, at, :] = (dq_t[:, at].T * HEAD_DIM**-0.5).astype(jnp.bfloat16)
        return carry

    lax.fori_loop(0, rows // bq, finish, 0)


def attend_back(own, other, lengths, counts, q, k, v, qt, kt, ot, lse, do_own, do_other):
    rows, width = k.shape
    count = own.shape[0]
    bk = bq = min(256, rows)
    heads = width // HEAD_DIM
    return pl.pallas_call(
        attend_back_kernel,
        out_shape=struct((3, rows, width), jnp.bfloat16),
        in_specs=[SMEM] * 4 + [ANYWHERE] * 9,
        out_specs=VMEM,
        scratch_shapes=[
            *[pltpu.VMEM((count, PIECE, width), jnp.bfloat16)] * 2,
            *[pltpu.VMEM(one.shape, one.dtype) for one in (q, ot, k, v, qt, kt, lse)],
            pltpu.VMEM((rows // PIECE, PIECE, width), jnp.float32),
            pltpu.VMEM((width, rows), jnp.bfloat16),
            pltpu.VMEM((heads, rows, 128), jnp.bfloat16),
            pltpu.VMEM((heads, rows, 128), jnp.bfloat16),
            pltpu.VMEM((8, rows), jnp.float32),
            pltpu.VMEM((width, rows), jnp.float32),
            pltpu.VMEM((bk, width), jnp.float32),
            pltpu.VMEM((bk, width), jnp.float32),
            pltpu.VMEM((bk, bq), jnp.float32),
            pltpu.SemaphoreType.DMA((9,)),
        ],
        compiler_params=params(60),
        cost_estimate=cost(5e10, 20e6, heads * rows * rows // 2),
        name="attend_back",
    )(
        own, other, lengths, counts, q, k, v, qt, kt, ot, lse,
        do_own.reshape(count, PIECE, width), do_other.reshape(count, PIECE, width),
    )


def feed_kernel(
    x_ref, oa_ref, ob_ref, dy_ref, real_ref, gain_ref, shift_ref, *refs,
):
    weights, (out_ref, y1_ref, gr_ref, act_a, act_b, slope_a, slope_b), held = refs[:6], refs[6:13], refs[13:19]
    wo_a, wo_b, up_a, down_a, up_b, down_b = held
    ready = resident([pltpu.make_async_copy(w, h, refs[19].at[i]) for i, (w, h) in enumerate(zip(weights, held))])
    ready(0)
    ready(1)
    x = x_ref[...].astype(jnp.float32)
    y1 = x + dot(oa_ref[...], wo_a[...]) + dot(ob_ref[...], wo_b[...])
    y1_ref[...] = y1
    unit, _ = norm_unit(y1)
    h = (unit * gain_ref[...] + shift_ref[...]).astype(jnp.bfloat16)
    gr_ref[...] = (dy_ref[...].astype(jnp.float32) * real_ref[...]).astype(jnp.bfloat16)
    mlp = None
    for n, up, down, act_ref, slope_ref in ((2, up_a, down_a, act_a, slope_a), (4, up_b, down_b, act_b, slope_b)):
        ready(n)
        ready(n + 1)
        hidden = up.shape[1]
        part = min(768, hidden)
        for at in range(0, hidden, part):
            cols = slice(at, at + part)
            u = dot(h, up[:, cols])
            phi = 0.5 * (1.0 + lax.erf(u * 0.7071067811865476))
            act = (u * phi).astype(jnp.bfloat16)
            act_ref[:, cols] = act
            slope_ref[:, cols] = (phi + u * 0.3989422804014327 * jnp.exp(-0.5 * u * u)).astype(jnp.bfloat16)
            m = dot(act, down[cols, :])
            mlp = m if mlp is None else mlp + m
    out_ref[...] = (y1 + mlp).astype(jnp.bfloat16)


def feed_back_kernel(
    y1_ref, gr_ref, slope_a, slope_b, oa_ref, ob_ref, gain_ref, shift_ref, blocks_ref, *refs,
):
    weights, (left_a, left_b, right_ref, doa_ref, dob_ref, dy1_ref, norm_ref, sum_ref) = refs[:6], refs[6:14]
    held = refs[14:20]
    load, sent, got, more, send_sem, recv_sem = refs[20:]
    wo_a, wo_b, up_a, down_a, up_b, down_b = held
    loads = [pltpu.make_async_copy(w, h, load.at[i]) for i, (w, h) in enumerate(zip(weights, held))]
    loads.append(pltpu.make_async_copy(blocks_ref, sent, load.at[6]))
    ready = resident(loads)
    me = lax.axis_index("dp")
    e = me % NEAR
    step = pl.program_id(0)
    last = pl.num_programs(0) - 1
    cut = sum_ref.shape[0] // 2
    first, second = slice(0, cut), slice(cut, 2 * cut)

    def flip(d):
        return (e // 2 + d // 2) % 2 * 2 + (e % 2 + d % 2) % 2

    def trade(n):
        source, d = (
            (sent.at[flip(1), first], 1),
            (sent.at[flip(3), first], 1),
            (sent.at[flip(2), second], 2),
            (sent.at[flip(3), second], 2),
            (more.at[0], 2),
            (more.at[1], 1),
        )[n]
        return pltpu.make_async_remote_copy(
            source, got.at[n], send_sem.at[n], recv_sem.at[n],
            device_id={"dp": me // NEAR * NEAR + flip(d)}, device_id_type=MESH,
        )

    @pl.when(step == 0)
    def _():
        barrier = pltpu.get_barrier_semaphore()
        for d in (1, 2):
            to = me // NEAR * NEAR + flip(d)
            pl.semaphore_signal(barrier, inc=1, device_id={"dp": to}, device_id_type=MESH)
        pl.semaphore_wait(barrier, 2)

    ready(6)

    @pl.when(step == 0)
    def _():
        for n in (1, 3, 0, 2):
            trade(n).start()

    def second_trades():
        @pl.when(step == jnp.maximum(last - 1, 0))
        def _():
            f32 = jnp.float32
            for n, source in ((1, sent.at[flip(2), first]), (3, sent.at[flip(1), second])):
                trade(n).wait()
                more[n // 2] = (source[...].astype(f32) + got[n].astype(f32)).astype(jnp.bfloat16)
                trade(4 + n // 2).start()

    unit, inverse = norm_unit(y1_ref[...])
    right_ref[0] = (unit * gain_ref[...] + shift_ref[...]).astype(jnp.bfloat16)
    gr = gr_ref[...]
    dh = None
    for n, up, down, slope_ref, left, o_ref in (
        (2, up_a, down_a, slope_a, left_a, oa_ref),
        (4, up_b, down_b, slope_b, left_b, ob_ref),
    ):
        ready(n)
        ready(n + 1)
        hidden = up.shape[1]
        part = min(768, hidden)
        for at in range(0, hidden, part):
            cols = slice(at, at + part)
            slope = slope_ref[:, cols].astype(jnp.float32)
            du = (dot(gr, down[cols, :], NT) * slope).astype(jnp.bfloat16)
            left[:, cols] = du
            d = dot(du, up[:, cols], NT)
            dh = d if dh is None else dh + d
        if n == 2:
            second_trades()
        local = o_ref.shape[1]
        left[:, hidden : hidden + local] = o_ref[...]
        left[:, hidden + local :] = jnp.zeros_like(left[:, hidden + local :])
    sums = jnp.concatenate(
        [jnp.sum(dh * unit, axis=0, keepdims=True), jnp.sum(dh, axis=0, keepdims=True)], axis=0
    )

    @pl.when(pl.program_id(0) == 0)
    def _():
        norm_ref[...] = sums

    @pl.when(pl.program_id(0) > 0)
    def _():
        norm_ref[...] += sums

    ready(0)
    ready(1)
    dy1 = gr.astype(jnp.float32) + norm_back(dh * gain_ref[...], unit, inverse)
    dy1_ref[...] = dy1
    dar = dy1.astype(jnp.bfloat16)
    right_ref[1] = dar
    doa_ref[...] = dot(dar, wo_a[...], NT).astype(jnp.bfloat16)
    dob_ref[...] = dot(dar, wo_b[...], NT).astype(jnp.bfloat16)

    @pl.when(step == last)
    def _():
        for at, n in ((first, 0), (second, 2)):
            trade(n).wait()
            trade(4 + n // 2).wait()
            total = sent[e, at].astype(jnp.float32) + got[n].astype(jnp.float32)
            sum_ref[at, :] = (total + got[4 + n // 2].astype(jnp.float32)).astype(jnp.bfloat16)


def feed_specs(rows):
    block = min(256, rows)

    def tall(cols):
        return pl.BlockSpec((block, cols), lambda i: (i, 0))

    return block, tall


def resident(loads):
    @pl.when(pl.program_id(0) == 0)
    def _():
        for one in loads:
            one.start()

    def ready(i):
        @pl.when(pl.program_id(0) == 0)
        def _():
            loads[i].wait()

    return ready


def feed(x, o_own, o_other, dy, real, wo, up, down, gain, shift):
    rows, width = x.shape
    local = o_own.shape[1]
    hidden = up[0].shape[1]
    block, tall = feed_specs(rows)
    weights = (*wo, up[0], down[0], up[1], down[1])
    bf16 = jnp.bfloat16
    return pl.pallas_call(
        feed_kernel,
        grid=(rows // block,),
        out_shape=[struct((rows, width), bf16), struct((rows, width), jnp.float32), struct((rows, width), bf16)]
        + [struct((rows, hidden), bf16)] * 4,
        in_specs=[tall(width), tall(local), tall(local), tall(width), tall(1)] + [VMEM] * 2 + [ANYWHERE] * 6,
        out_specs=[tall(width)] * 3 + [tall(hidden)] * 4,
        scratch_shapes=[pltpu.VMEM(w.shape, bf16) for w in weights] + [pltpu.SemaphoreType.DMA((6,))],
        compiler_params=params(60),
        cost_estimate=cost(2 * rows * width * (hidden * 4 + local * 2), 45e6, rows * hidden * 4),
        name="feed",
    )(x, o_own, o_other, dy, real, gain, shift, *weights)


def feed_back(y1, gr, slope, o_own, o_other, wo, up, down, gain, shift, blocks):
    rows, width = y1.shape
    local = o_own.shape[1]
    hidden = up[0].shape[1]
    block, tall = feed_specs(rows)
    weights = (*wo, up[0], down[0], up[1], down[1])
    bf16 = jnp.bfloat16
    lefts = hidden // 3 * 4
    return pl.pallas_call(
        feed_back_kernel,
        grid=(rows // block,),
        out_shape=[
            struct((rows, lefts), bf16),
            struct((rows, lefts), bf16),
            struct((2, rows, width), bf16),
            struct((rows, local), bf16),
            struct((rows, local), bf16),
            struct((rows, width), jnp.float32),
            struct((2, width), jnp.float32),
            struct(blocks.shape[1:], bf16),
        ],
        in_specs=[tall(width), tall(width), tall(hidden), tall(hidden), tall(local), tall(local)]
        + [VMEM] * 2
        + [ANYWHERE] * 7,
        out_specs=[
            tall(lefts),
            tall(lefts),
            pl.BlockSpec((2, block, width), lambda i: (0, i, 0)),
            tall(local),
            tall(local),
            tall(width),
            pl.BlockSpec((2, width), lambda i: (0, 0)),
            pl.BlockSpec(blocks.shape[1:], lambda i: (0, 0)),
        ],
        scratch_shapes=[pltpu.VMEM(w.shape, bf16) for w in weights]
        + [
            pltpu.SemaphoreType.DMA((7,)),
            pltpu.VMEM(blocks.shape, bf16),
            pltpu.VMEM((6, blocks.shape[1] // 2, width), bf16),
            pltpu.VMEM((2, blocks.shape[1] // 2, width), bf16),
            pltpu.SemaphoreType.DMA((6,)),
            pltpu.SemaphoreType.DMA((6,)),
        ],
        compiler_params=pltpu.CompilerParams(collective_id=1, has_side_effects=True, vmem_limit_bytes=60 * MIB),
        cost_estimate=cost(2 * rows * width * (hidden * 4 + local * 2), 45e6),
        name="feed_back",
    )(y1, gr, *slope, o_own, o_other, gain, shift, blocks, *weights)


def weight_kernel(size, hosted, other_ref, own_ref, right_ref, *refs):
    if hosted:
        chunk_ref, out_ref, share_ref, send, recv, send_sem, recv_sem, chunk, land, far_s, far_r, load = refs
    else:
        out_ref, send, recv, send_sem, recv_sem = refs
    step = pl.program_id(0)
    core = lax.axis_index("mp")
    me = lax.axis_index("dp")
    far = size // NEAR
    f, e = me // NEAR, me % NEAR

    def swapped(i):
        return pltpu.make_async_remote_copy(
            send.at[i], recv.at[i], send_sem.at[i], recv_sem.at[i],
            device_id={"mp": 1 - core}, device_id_type=MESH,
        )

    def spread(d):
        to = (f + d) % far
        return pltpu.make_async_remote_copy(
            chunk.at[to], land.at[d], far_s.at[d], far_r.at[d],
            device_id={"dp": to * NEAR + e}, device_id_type=MESH,
        )

    @pl.when(step == 0)
    def _():
        barrier = pltpu.get_barrier_semaphore()
        pl.semaphore_signal(barrier, inc=1, device_id={"mp": 1 - core}, device_id_type=MESH)
        if hosted:
            fetch = pltpu.make_async_copy(chunk_ref, chunk, load)
            fetch.start()
            for d in range(1, far):
                to = (f + d) % far * NEAR + e
                pl.semaphore_signal(barrier, inc=1, device_id={"dp": to}, device_id_type=MESH)
            fetch.wait()
        pl.semaphore_wait(barrier, far if hosted else 1)
        if hosted:
            for d in range(1, far):
                spread(d).start()

    @pl.when(step < NEAR)
    def _():
        send[step] = dot(other_ref[...], right_ref[0], TN).astype(jnp.bfloat16)
        swapped(step).start()

    @pl.when(step >= NEAR)
    def _():
        total = dot(own_ref[...], right_ref[0], TN)
        swapped(step - NEAR).wait_recv()
        out_ref[0] = (total + recv[step - NEAR].astype(jnp.float32)).astype(jnp.bfloat16)

    @pl.when(step == 2 * NEAR - 1)
    def _():
        for i in range(NEAR):
            swapped(i).wait_send()
        if hosted:
            total = chunk[f].astype(jnp.float32)
            for d in range(1, far):
                spread(d).wait()
                total = total + land[d].astype(jnp.float32)
            share_ref[...] = total.astype(jnp.bfloat16)


def weight_grads(own, other, right, size, chunk=None):
    rows, lefts = own.shape
    count, _, width = right.shape
    block = lefts // NEAR
    far = size // NEAR
    bf16 = jnp.bfloat16
    dma = pltpu.SemaphoreType.DMA

    def pick(i):
        return (i % NEAR // (NEAR - 1) if count == 2 else 0, 0, 0)

    out_shape = [struct((NEAR, block, width), bf16)]
    in_specs = [
        pl.BlockSpec((rows, block), lambda i: (0, jnp.minimum(i, NEAR - 1))),
        pl.BlockSpec((rows, block), lambda i: (0, jnp.maximum(i - NEAR, 0))),
        pl.BlockSpec((1, rows, width), pick),
    ]
    out_specs = [pl.BlockSpec((1, block, width), lambda i: (jnp.maximum(i - NEAR, 0), 0, 0))]
    scratch = [pltpu.VMEM((NEAR, block, width), bf16)] * 2 + [dma((NEAR,))] * 2
    operands = [other, own, right]
    if chunk is not None:
        share = chunk.shape[0] // far
        out_shape.append(struct((share, width), bf16))
        in_specs.append(ANYWHERE)
        out_specs.append(pl.BlockSpec((share, width), lambda i: (0, 0)))
        scratch += [pltpu.VMEM((far, share, width), bf16)] * 2 + [dma((far,))] * 2 + [dma]
        operands.append(chunk.reshape(far, share, width))
    return pl.pallas_call(
        functools.partial(weight_kernel, size, chunk is not None),
        grid=(2 * NEAR,),
        out_shape=out_shape,
        in_specs=in_specs,
        out_specs=out_specs,
        scratch_shapes=scratch,
        compiler_params=pltpu.CompilerParams(
            collective_id=2 if chunk is None else 3, has_side_effects=True, vmem_limit_bytes=60 * MIB
        ),
        cost_estimate=cost(4 * rows * width * lefts, 20e6),
        name="weight_grads",
    )(*operands)


def padded(rows, size):
    return -(-rows // (16 * size)) * 16 * size


def near_send(block, d, size):
    return lax.ppermute(block, "dp", [(i, i ^ d) for i in range(size)])


def add_up(blocks):
    total = blocks[0].astype(jnp.float32)
    for block in blocks[1:]:
        total = total + block.astype(jnp.float32)
    return total.astype(jnp.bfloat16)


def close_kernel(
    size, own_ref, other_ref, up_in, down_in, gain_ref, norm2_ref, grads_in, ht_in, w_in, dy1_in, x_in,
    up_out, down_out, second_out, rows_own, rows_other, norms_out,
    grads_ref, ht_ref, w_ref, dy1_ref, x_ref, mine_a, mine_c, part, natural, swap_s, swap_r, dx, acc_a, acc_c, land_a, land_c, near_b, sum_b, norm_s, norm_r, norm_t,
    near_sem_s, near_sem_r, far_sem_s, far_sem_r, part_s, part_r, trade_s, trade_r, pass_s, pass_r,
    small_s, small_r, mp_s, mp_r, local, load, store,
):
    far = size // NEAR
    bits = [1 << b for b in range(far.bit_length() - 1)]
    me = lax.axis_index("dp")
    core = lax.axis_index("mp")
    f, e = me // NEAR, me % NEAR
    rows_all, local_width = grads_ref.shape[1:]
    width = w_ref.shape[1]
    block = min(256, rows_all)
    bf16 = jnp.bfloat16

    def flip(value, mask, top):
        out, b = 0, 1
        while b < top:
            out = out + b * ((value // b + mask // b) % 2)
            b *= 2
        return out

    loads = [
        pltpu.make_async_copy(source, target, load.at[i])
        for i, (source, target) in enumerate(
            ((grads_in, grads_ref), (ht_in, ht_ref), (w_in, w_ref), (dy1_in, dy1_ref), (x_in, x_ref))
        )
    ]
    for i in (0, 2, 1, 3, 4):
        loads[i].start()

    barrier = pltpu.get_barrier_semaphore()

    def greet(d, carry):
        pl.semaphore_signal(barrier, inc=1, device_id={"dp": (me + d) % size}, device_id_type=MESH)
        return carry

    lax.fori_loop(1, size, greet, 0)
    pl.semaphore_signal(barrier, inc=1, device_id={"mp": 1 - core}, device_id_type=MESH)
    pl.semaphore_wait(barrier, size)

    def remote(source, target, send, recv, device):
        return pltpu.make_async_remote_copy(
            source, target, send, recv, device_id={"dp": device}, device_id_type=MESH
        )

    def beside(source, target, send, recv):
        return pltpu.make_async_remote_copy(
            source, target, send, recv, device_id={"mp": 1 - core}, device_id_type=MESH
        )

    def views(*refs):
        return lambda s, *at: refs[s].at[at]

    inputs, accs = views(up_in, None, sum_b), views(acc_a, None, acc_c)
    lands, outs = views(land_a, None, land_c), views(up_out, down_out, second_out)
    mines = (mine_a, down_in, mine_c)
    held = {b: [m for m in range(far) if m % (2 * b) == 0] for b in bits}
    slot = {}
    for b in bits:
        for m in held[b]:
            slot[b, m] = len(slot)
    arrivals = [(b, m) for b in reversed(bits) for m in held[b]]

    def reduce_copy(s, b, m):
        source = inputs(s, flip(f, m + b, far)) if b == 1 else accs(s, m + b)
        k = slot[b, m]
        return remote(source, lands(s, k), far_sem_s.at[s, k], far_sem_r.at[s, k], flip(f, b, far) * NEAR + e)

    def reduce_start(s, b):
        for m in held[b]:
            reduce_copy(s, b, m).start()

    def reduce_step(s, b):
        for m in held[b]:
            reduce_copy(s, b, m).wait_recv()
            base = inputs(s, flip(f, m, far)) if b == 1 else accs(s, m)
            total = (base[...].astype(jnp.float32) + lands(s, slot[b, m])[...].astype(jnp.float32)).astype(bf16)
            if 2 * b == far:
                mines[s][...] = total
            else:
                accs(s, m)[...] = total
        if 2 * b < far:
            reduce_start(s, 2 * b)
        else:
            kept(s).start()
            available(s, 0)

    def kept(s):
        return pltpu.make_async_copy(mines[s], outs(s, e, f), store.at[s])

    def held_at(s, m):
        return mines[s] if m == 0 else outs(s, e, flip(f, m, far))

    def spread_copy(s, b, m):
        piece = outs(s, e, flip(f, m, far))
        k = slot[b, m]
        return remote(held_at(s, m), piece, far_sem_s.at[3 + s, k], far_sem_r.at[3 + s, k], flip(f, b, far) * NEAR + e)

    def spread_arrival(s, b, m):
        piece = outs(s, e, flip(f, m + b, far))
        k = slot[b, m]
        return remote(piece, piece, far_sem_s.at[3 + s, k], far_sem_r.at[3 + s, k], flip(f, b, far) * NEAR + e)

    def near_copy(s, d, m):
        piece = outs(s, e, flip(f, m, far))
        return remote(held_at(s, m), piece, near_sem_s.at[s, d, m], near_sem_r.at[s, d, m], f * NEAR + flip(e, d, NEAR))

    def near_arrival(s, d, m):
        piece = outs(s, flip(e, d, NEAR), flip(f, m, far))
        return remote(piece, piece, near_sem_s.at[s, d, m], near_sem_r.at[s, d, m], f * NEAR + flip(e, d, NEAR))

    def near_pass(s, m):
        source, to = (1, 2) if m % 2 == 0 else (2, 1)
        piece = outs(s, flip(e, source, NEAR), flip(f, m, far))
        return remote(piece, piece, near_sem_s.at[s, 3, m], near_sem_r.at[s, 3, m], f * NEAR + flip(e, to, NEAR))

    def near_passed(s, m):
        to = 2 if m % 2 == 0 else 1
        piece = outs(s, flip(e, 3, NEAR), flip(f, m, far))
        return remote(piece, piece, near_sem_s.at[s, 3, m], near_sem_r.at[s, 3, m], f * NEAR + flip(e, to, NEAR))

    def available(s, m):
        for b in reversed(bits):
            if m % (2 * b) == 0:
                spread_copy(s, b, m).start()
        for d in (1, 2):
            near_copy(s, d, m).start()

    def arrive(s, b, m):
        spread_arrival(s, b, m).wait_recv()
        available(s, m + b)

    def pass_on(s, m):
        for d in (1, 2):
            near_arrival(s, d, m).wait_recv()
        near_pass(s, m).start()

    share = land_c.shape[1]

    def near_block(index):
        return pl.ds(pl.multiple_of(index * (far * share), 16), far * share)

    def part_copy(d):
        to = flip(e, d, NEAR)
        return remote(part.at[near_block(to)], near_b.at[d], part_s.at[d], part_r.at[d], f * NEAR + to)

    def trade(d):
        to = (me + d) % size
        return remote(dx.at[to], rows_own.at[me], trade_s.at[d], trade_r.at[d], to)

    def trade_arrival(d):
        source = (me - d + size) % size
        return remote(dx.at[source], rows_own.at[source], trade_s.at[d], trade_r.at[d], source)

    def passing(d):
        source = (me - d + size) % size
        return beside(rows_own.at[source], rows_other.at[source], pass_s.at[d], pass_r.at[d])

    def small(d):
        to = (me + d) % size
        return remote(norm_s, norm_r.at[me], small_s.at[d], small_r.at[d], to)

    def small_arrival(d):
        source = (me - d + size) % size
        return remote(norm_s, norm_r.at[source], small_s.at[d], small_r.at[d], source)

    reduce_start(0, 1)
    kept(1).start()
    available(1, 0)

    pieces = block // PIECE

    def grad_step(i, carry):
        at = pl.ds(pl.multiple_of(i * block, block), block)
        value = dot(grads_ref[0, at, :], w_ref[0], NT)
        value += dot(grads_ref[1, at, :], w_ref[1], NT)
        value += dot(grads_ref[2, at, :], w_ref[2], NT)
        natural[pl.ds(i * pieces, pieces)] = value.reshape(pieces, PIECE, width)
        return carry

    loads[0].wait()
    loads[2].wait()
    lax.fori_loop(0, rows_all // block, grad_step, 0)

    def pack(j, carry):
        swap_s[j] = natural[other_ref[j]].astype(bf16)
        return carry

    lax.fori_loop(0, swap_s.shape[0], pack, 0, unroll=8)
    half = beside(swap_s, swap_r, mp_s.at[0], mp_r.at[0])
    half.start()
    reduce_step(0, 1)

    tall = width // 4

    def part_step(i, carry):
        for c in range(4):
            value = dot(ht_ref[c * tall : (c + 1) * tall, :], grads_ref[i])
            at = pl.multiple_of(i * width + c * tall, 16)
            part[pl.ds(at, tall), :] = value.astype(bf16)
        return carry

    loads[1].wait()
    lax.fori_loop(0, 3, part_step, 0)
    used = 3 * width
    if part.shape[0] > used:
        part[used:, :] = jnp.zeros((part.shape[0] - used, local_width), bf16)
    for d in range(1, NEAR):
        part_copy(d).start()
    for b in bits[1:]:
        reduce_step(0, b)

    half.wait_recv()
    loads[3].wait()
    loads[4].wait()
    group_rows = dx.shape[1]
    norm_s[...] = jnp.zeros_like(norm_s)
    norm_s[2:4, :] = norm2_ref[...]
    mine = x_ref.shape[0]
    step_rows = min(256, mine)
    step_pieces = step_rows // PIECE

    def finish_step(i, carry):
        def take(j, inner):
            k = i * step_pieces + j
            natural_own[j] = natural[own_ref[k]] + swap_r[k].astype(jnp.float32)
            return inner

        lax.fori_loop(0, step_pieces, take, 0, unroll=8)
        at = pl.ds(pl.multiple_of(i * step_rows, step_rows), step_rows)
        dh = natural_own[...].reshape(step_rows, width)
        unit, inverse = norm_unit(x_ref[at, :].astype(jnp.float32))
        norm_s[0:1, :] += jnp.sum(dh * unit, axis=0, keepdims=True)
        norm_s[1:2, :] += jnp.sum(dh, axis=0, keepdims=True)
        value = dy1_ref[at, :] + norm_back(dh * gain_ref[...], unit, inverse)
        per_step = step_rows // group_rows
        dx[pl.ds(i * per_step, per_step)] = value.astype(bf16).reshape(per_step, group_rows, width)
        return carry

    natural_own = norm_t
    lax.fori_loop(0, mine // step_rows, finish_step, 0)

    def send(d, carry):
        trade(d).start()
        return carry

    lax.fori_loop(1, size, send, 0)

    def send_small(d, carry):
        small(d).start()
        return carry

    lax.fori_loop(1, size, send_small, 0)
    keep = pltpu.make_async_copy(dx.at[me], rows_own.at[me], local.at[0])
    keep.start()
    keep_small = pltpu.make_async_copy(norm_s, norm_r.at[me], local.at[1])
    keep_small.start()

    for d in range(1, NEAR):
        part_copy(d).wait_recv()
    own_part = part.at[near_block(e)]
    for j in range(far):
        at = slice(j * share, (j + 1) * share)
        total = own_part[at, :].astype(jnp.float32)
        for d in range(1, NEAR):
            total = total + near_b[d, at, :].astype(jnp.float32)
        sum_b[j] = total.astype(bf16)
    reduce_start(2, 1)

    pass_on(1, 0)
    for b, m in arrivals:
        arrive(1, b, m)
    for b, m in arrivals:
        pass_on(1, m + b)
    reduce_step(2, 1)
    pass_on(0, 0)
    arrive(0, *arrivals[0])
    for b in bits[1:]:
        reduce_step(2, b)
    for b, m in arrivals[1:]:
        arrive(0, b, m)
    for b, m in arrivals:
        pass_on(0, m + b)
    pass_on(2, 0)
    for b, m in arrivals:
        arrive(2, b, m)
    for b, m in arrivals:
        pass_on(2, m + b)
    keep.wait()
    passing(0).start()

    def settle(d, carry):
        trade_arrival(d).wait_recv()
        passing(d).start()
        return carry

    lax.fori_loop(1, size, settle, 0)
    keep_small.wait()

    def settle_small(d, carry):
        small_arrival(d).wait_recv()
        return carry

    lax.fori_loop(1, size, settle_small, 0)

    def add(g, carry):
        return carry + norm_r[g]

    total = lax.fori_loop(0, size, add, jnp.zeros(norm_s.shape, jnp.float32))
    for d in range(1, size):
        small(d).wait_send()
    norm_s[...] = total
    last = beside(norm_s, norm_r.at[size], mp_s.at[1], mp_r.at[1])
    last.start()
    last.wait()
    norms_out[...] = norm_s[...] + norm_r[size]

    for s in range(3):
        for m in range(far):
            near_passed(s, m).wait_recv()
    half.wait_send()
    for s in range(3):
        kept(s).wait()
    for d in range(1, NEAR):
        part_copy(d).wait_send()
    for s in range(3):
        for b in bits:
            for m in held[b]:
                if s != 1:
                    reduce_copy(s, b, m).wait_send()
                spread_copy(s, b, m).wait_send()
        for m in range(far):
            near_copy(s, 1, m).wait_send()
            near_copy(s, 2, m).wait_send()
            near_pass(s, m).wait_send()

    passing(0).wait()

    def close(d, carry):
        trade(d).wait_send()
        passing(d).wait()
        return carry

    lax.fori_loop(1, size, close, 0)


def close(own, other, up_chunk, down_share, grads, ht, w, x, dy1, gain, norm2, size):
    far = size // NEAR
    rows, local = grads.shape[1:]
    width = w.shape[1]
    b = padded(3 * width, size)
    n = x.shape[0] // size
    bf16, f32 = jnp.bfloat16, jnp.float32
    shares = (up_chunk.shape[0] // far, down_share.shape[0])
    share_b = b // size
    dma = pltpu.SemaphoreType.DMA
    step = min(256, x.shape[0])
    up_sum, down_sum, second, rows_own, rows_other, norms = pl.pallas_call(
        functools.partial(close_kernel, size),
        out_shape=[
            struct((NEAR, far, shares[0], width), bf16),
            struct((NEAR, far, shares[1], width), bf16),
            struct((NEAR, far, share_b, local), bf16),
            struct((size, n, width), bf16),
            struct((size, n, width), bf16),
            struct((8, width), f32),
        ],
        in_specs=[SMEM, SMEM] + [VMEM] * 4 + [ANYWHERE] * 5,
        out_specs=[ANYWHERE] * 5 + [VMEM],
        scratch_shapes=[
            pltpu.VMEM(grads.shape, bf16),
            pltpu.VMEM(ht.shape, bf16),
            pltpu.VMEM(w.shape, bf16),
            pltpu.VMEM(dy1.shape, f32),
            pltpu.VMEM(x.shape, bf16),
            pltpu.VMEM((shares[0], width), bf16),
            pltpu.VMEM((share_b, local), bf16),
            pltpu.VMEM((b, local), bf16),
            pltpu.VMEM((rows // PIECE, PIECE, width), f32),
            pltpu.VMEM((x.shape[0] // PIECE, PIECE, width), bf16),
            pltpu.VMEM((x.shape[0] // PIECE, PIECE, width), bf16),
            pltpu.VMEM((size, n, width), bf16),
            pltpu.VMEM((far, shares[0], width), bf16),
            pltpu.VMEM((far, share_b, local), bf16),
            pltpu.VMEM((far, shares[0], width), bf16),
            pltpu.VMEM((far, share_b, local), bf16),
            pltpu.VMEM((NEAR, b // NEAR, local), bf16),
            pltpu.VMEM((far, share_b, local), bf16),
            pltpu.VMEM((8, width), f32),
            pltpu.VMEM((size + 1, 8, width), f32),
            pltpu.VMEM((step // PIECE, PIECE, width), f32),
            dma((3, NEAR, far)),
            dma((3, NEAR, far)),
            dma((6, far)),
            dma((6, far)),
            dma((NEAR,)),
            dma((NEAR,)),
            dma((size,)),
            dma((size,)),
            dma((size,)),
            dma((size,)),
            dma((size,)),
            dma((size,)),
            dma((2,)),
            dma((2,)),
            dma((2,)),
            dma((5,)),
            dma((3,)),
        ],
        compiler_params=pltpu.CompilerParams(
            collective_id=0, has_side_effects=True, vmem_limit_bytes=60 * MIB
        ),
        cost_estimate=cost(8 * rows * width * local, 1e8),
        name="close",
    )(
        own, other, up_chunk.reshape(far, shares[0], width), down_share, gain, norm2,
        grads, ht, w, dy1, x,
    )
    return (
        up_sum.reshape(NEAR, -1, width),
        down_sum.reshape(NEAR, -1, width),
        second.reshape(b, local),
        rows_own.reshape(-1, width),
        rows_other.reshape(-1, width),
        norms,
    )


def widen_kernel(up_in, down_in, second_ref, up_ref, down_ref, out_ref, qkv_ref):
    f32 = jnp.float32
    down_ref[...] = down_in[0, : down_ref.shape[0], :].astype(f32)
    qkv_ref[...] = second_ref[...].astype(f32)

    @pl.when(pl.program_id(0) < NEAR - 1)
    def _():
        up_ref[...] = up_in[0, : up_ref.shape[1], :].astype(f32).T

    @pl.when(pl.program_id(0) == NEAR - 1)
    def _():
        out_ref[...] = up_in[0, : out_ref.shape[0], :].astype(f32)


def widen(up_sum, down_sum, second, hidden, local, rows):
    width = up_sum.shape[2]
    f32 = jnp.float32
    up_rows, down_rows, part = hidden // (NEAR - 1), hidden // NEAR, rows // NEAR
    return pl.pallas_call(
        widen_kernel,
        grid=(NEAR,),
        out_shape=[
            struct((width, hidden), f32),
            struct((hidden, width), f32),
            struct((local, width), f32),
            struct((rows, second.shape[1]), f32),
        ],
        in_specs=[
            pl.BlockSpec((1, *up_sum.shape[1:]), lambda i: (i, 0, 0)),
            pl.BlockSpec((1, *down_sum.shape[1:]), lambda i: (i, 0, 0)),
            pl.BlockSpec((part, second.shape[1]), lambda i: (i, 0)),
        ],
        out_specs=[
            pl.BlockSpec((width, up_rows), lambda i: (0, jnp.minimum(i, NEAR - 2))),
            pl.BlockSpec((down_rows, width), lambda i: (i, 0)),
            pl.BlockSpec((local, width), lambda i: (0, 0)),
            pl.BlockSpec((part, second.shape[1]), lambda i: (i, 0)),
        ],
        compiler_params=params(60),
        cost_estimate=cost(0, 22e6),
        name="widen",
    )(up_sum, down_sum, second)


def swap(value):
    return lax.ppermute(value, "mp", [(0, 1), (1, 0)])


def exchange(value):
    return lax.all_to_all(value, "dp", split_axis=0, concat_axis=0, tiled=True)


def body(
    tokens, out_grad, lengths, counts, dest_slot, qkv_weight, out_weight, up_weight, down_weight,
    norm1_gain, norm1_shift, norm2_gain, norm2_shift,
):
    groups = lax.axis_size("dp")
    me = lax.axis_index("dp")
    core = lax.axis_index("mp")
    rows, width = tokens.shape
    per = rows // PIECE
    capacity = per // groups
    half = capacity // 2
    local = qkv_weight.shape[2]
    bf16 = jnp.bfloat16

    slots = dest_slot.reshape(groups, per)
    my_slots = lax.dynamic_index_in_dim(slots, me, 0, keepdims=True)
    group_ids = jnp.arange(groups, dtype=jnp.int32)[:, None]
    piece_ids = jnp.broadcast_to(jnp.arange(per, dtype=jnp.int32)[None, :], (groups, per))
    source = slot_table(my_slots // per == group_ids, piece_ids, capacity)
    target = slot_table(slots // per == me, slots - me * per, capacity)

    def halves(table):
        own = lax.dynamic_slice_in_dim(table, core * half, half, 1)
        other = lax.dynamic_slice_in_dim(table, (1 - core) * half, half, 1)
        return own.reshape(-1), other.reshape(-1)

    src_own, src_other = halves(source)
    own, other = halves(target)

    x_own = exchange(gather_pieces(src_own, tokens))
    dy_send = gather_pieces(src_own, out_grad)
    place = (own[:, None] * PIECE + jnp.arange(PIECE, dtype=jnp.int32)[None, :]).reshape(-1, 1)
    real, start = jnp.zeros(place.shape, jnp.bool_), jnp.int32(0)
    for c in range(lengths.shape[1]):
        live = start + jnp.minimum(lengths[0, c], counts[0, c])
        real, start = real | ((place >= start) & (place < live)), start + lengths[0, c]
    real = real.astype(jnp.float32)
    turned_weight = jnp.swapaxes(qkv_weight, 1, 2)
    wo_other, up_other, down_other = swap(out_weight), swap(up_weight), swap(down_weight)
    gain1, shift1 = norm1_gain[None], norm1_shift[None]
    gain2, shift2 = norm2_gain[None], norm2_shift[None]
    x_own, dy_send, real, turned_weight, wo_other, up_other, down_other, own, other, gain1, shift1, gain2, shift2 = (
        lax.optimization_barrier(
            (
                x_own, dy_send, real, turned_weight, wo_other, up_other, down_other,
                own, other, gain1, shift1, gain2, shift2,
            )
        )
    )
    wo, up, down = (out_weight, wo_other), (up_weight, up_other), (down_weight, down_other)
    x_other = swap(x_own)

    h1_t, q, k, v, qt, kt, vt = project(own, other, x_own, x_other, gain1, shift1, qkv_weight, turned_weight)

    dy_own = exchange(dy_send)
    ot, o_own, o_send, lse = attend(own, other, lengths, counts, k, qt, vt)
    o_other = swap(o_send)

    out_rows, y1, gr, act_own, act_other, slope_own, slope_other = feed(
        x_own, o_own, o_other, dy_own, real, wo, up, down, gain2, shift2
    )
    [down_blocks] = weight_grads(act_own, act_other, gr[None], groups)
    left_own, left_other, right, do_own, do_send, dy1, norm2, down_chunk = feed_back(
        y1, gr, (slope_own, slope_other), o_own, o_other, wo, up, down, gain2, shift2, down_blocks
    )
    do_other = swap(do_send)
    unit = 16 * (groups // NEAR)
    down_chunk = jnp.pad(down_chunk, ((0, -down_chunk.shape[0] % unit), (0, 0)))
    up_blocks, down_share = weight_grads(left_own, left_other, right, groups, down_chunk)
    up_blocks, do_own, do_other, out_rows = lax.optimization_barrier((up_blocks, do_own, do_other, out_rows))
    out_back = exchange(out_rows)
    e = me % NEAR
    up_mine = lax.dynamic_index_in_dim(up_blocks, e, 0, keepdims=False)
    up_got = [
        near_send(lax.dynamic_index_in_dim(up_blocks, e ^ d, 0, keepdims=False), d, groups) for d in range(1, NEAR)
    ]
    grads = attend_back(own, other, lengths, counts, q, k, v, qt, kt, ot, lse, do_own, do_other)
    up_got, grads, out_back = lax.optimization_barrier((up_got, grads, out_back))
    up_chunk = add_up([up_mine, *up_got])
    up_chunk = jnp.pad(up_chunk, ((0, -up_chunk.shape[0] % unit), (0, 0)))
    up_sum, down_sum, qkv_grad, dx_own, dx_other, norms = close(
        own, other, up_chunk, down_share, grads, h1_t, qkv_weight, x_own, dy1, gain1, norm2, groups
    )
    up_sum, down_sum, qkv_grad, dx_own, dx_other, norms, out_back = lax.optimization_barrier(
        (up_sum, down_sum, qkv_grad, dx_own, dx_other, norms, out_back)
    )
    up_grad, down_grad, wo_grad, qkv_grad = widen(
        up_sum, down_sum, qkv_grad, up_weight.shape[1], local, 3 * width
    )
    qkv_grad = qkv_grad.reshape(3, width, local)

    mixed_out = merge_pieces(src_own, src_other, out_back, swap(out_back))
    input_grad = merge_pieces(src_own, src_other, dx_own, dx_other)
    return (
        mixed_out, input_grad, qkv_grad, wo_grad, up_grad, down_grad,
        norms[0], norms[1], norms[2], norms[3],
    )


def solution(mesh):
    in_specs = (
        P("dp", None), P("dp", None), P("dp", None), P("dp", None), P(),
        P(None, None, "mp"), P("mp", None), P(None, "mp"), P("mp", None), P(), P(), P(), P(),
    )
    out_specs = (
        P("dp", None), P("dp", None), P(None, None, "mp"), P("mp", None), P(None, "mp"), P("mp", None),
        P(), P(), P(), P(),
    )
    return jax.shard_map(body, mesh=mesh, in_specs=in_specs, out_specs=out_specs, check_vma=False)
```

```python
import functools

import jax
import jax.numpy as jnp
from jax import lax
from jax.experimental import pallas as pl
from jax.experimental.pallas import tpu as pltpu
from jax.sharding import PartitionSpec as P

HEAD_DIM = 64
PIECE = 8
NORM_EPS = 1e-05
MASKED = -1e30
MIB = 2**20
VMEM = pl.BlockSpec(memory_space=pltpu.VMEM)
SMEM = pl.BlockSpec(memory_space=pltpu.SMEM)
NEAR = 4
MESH = pl.DeviceIdType.MESH
ANYWHERE = pl.BlockSpec(memory_space=pl.ANY)
NT = (((1,), (1,)), ((), ()))
TN = (((0,), (0,)), ((), ()))


def params(mib):
    return pltpu.CompilerParams(vmem_limit_bytes=mib * MIB)


def cost(flops, nbytes, transcendentals=0):
    return pl.CostEstimate(
        flops=int(flops), bytes_accessed=int(nbytes), transcendentals=int(transcendentals)
    )


def struct(shape, dtype):
    return jax.ShapeDtypeStruct(shape, dtype)


def dot(a, b, dims=None):
    if dims is None:
        return jnp.dot(a, b, preferred_element_type=jnp.float32)
    return lax.dot_general(a, b, dims, preferred_element_type=jnp.float32)


def norm_unit(values):
    mean = jnp.mean(values, axis=-1, keepdims=True)
    centred = values - mean
    variance = jnp.mean(centred * centred, axis=-1, keepdims=True)
    inverse = lax.rsqrt(variance + NORM_EPS)
    return centred * inverse, inverse


def norm_back(grad_unit, unit, inverse):
    first = jnp.mean(grad_unit, axis=-1, keepdims=True)
    second = jnp.mean(grad_unit * unit, axis=-1, keepdims=True)
    return inverse * (grad_unit - first - unit * second)


def slot_table(chosen, values, capacity):
    per = chosen.shape[1]
    place = lax.broadcasted_iota(jnp.int32, (per, per), 0)
    earlier = place < lax.broadcasted_iota(jnp.int32, (per, per), 1)
    rank = dot(chosen.astype(jnp.bfloat16), earlier.astype(jnp.bfloat16)).astype(jnp.int32)
    rank = jnp.where(chosen, rank, -1)
    ranks = jnp.arange(capacity, dtype=jnp.int32)
    hit = rank[:, None, :] == ranks[None, :, None]
    return jnp.sum(jnp.where(hit, values[:, None, :], 0), axis=2)


def gather_kernel(index_ref, source_ref, out_ref):
    def step(j, carry):
        out_ref[j] = source_ref[index_ref[j]]
        return carry

    lax.fori_loop(0, out_ref.shape[0], step, 0, unroll=8)


def gather_pieces(index, source):
    rows, width = source.shape
    count = index.shape[0]
    out = pl.pallas_call(
        gather_kernel,
        out_shape=struct((count, PIECE, width), source.dtype),
        in_specs=[SMEM, VMEM],
        out_specs=VMEM,
        compiler_params=params(60),
        cost_estimate=cost(0, 3 * rows * width),
        name="gather_pieces",
    )(index, source.reshape(rows // PIECE, PIECE, width))
    return out.reshape(count * PIECE, width)


def project_kernel(
    own_ref, other_ref, own_in, other_in, gain_ref, shift_ref, w_ref,
    ht_ref, q_ref, k_ref, v_ref, qt_ref, kt_ref, vt_ref, x_all,
):
    @pl.when(pl.program_id(0) == 0)
    def _():
        def step(j, carry):
            x_all[own_ref[j]] = own_in[j]
            x_all[other_ref[j]] = other_in[j]
            return carry

        lax.fori_loop(0, own_in.shape[0], step, 0, unroll=8)

    block, local = q_ref.shape
    pieces = block // PIECE
    x = x_all[pl.ds(pl.program_id(0) * pieces, pieces)].astype(jnp.float32).reshape(block, -1)
    unit, _ = norm_unit(x)
    h = (unit * gain_ref[...] + shift_ref[...]).astype(jnp.bfloat16)
    ht_ref[...] = h.T
    for i, (n_ref, t_ref) in enumerate(((q_ref, qt_ref), (k_ref, kt_ref), (v_ref, vt_ref))):
        scale = HEAD_DIM**-0.5 if i == 0 else 1.0
        value = (dot(h, w_ref[i]) * scale).astype(jnp.bfloat16)
        n_ref[...] = value
        t_ref[...] = value.T


def project(own, other, x_own, x_other, gain, shift, w):
    half, width = x_own.shape
    rows, local = 2 * half, w.shape[2]
    outs = 3 * local
    pieces = half // PIECE
    block = min(512, rows)
    bf16 = jnp.bfloat16

    def whole(shape):
        return pl.BlockSpec(shape, lambda i: (0,) * len(shape), pipeline_mode=pl.Buffered(1))

    natural = pl.BlockSpec((block, local), lambda i: (i, 0))
    turned = pl.BlockSpec((local, block), lambda i: (0, i))
    return pl.pallas_call(
        project_kernel,
        grid=(rows // block,),
        out_shape=[struct((width, rows), bf16)] + [struct((rows, local), bf16)] * 3 + [struct((local, rows), bf16)] * 3,
        in_specs=[SMEM, SMEM]
        + [whole((pieces, PIECE, width))] * 2
        + [whole((1, width))] * 2
        + [whole(w.shape)],
        out_specs=[pl.BlockSpec((width, block), lambda i: (0, i))] + [natural] * 3 + [turned] * 3,
        scratch_shapes=[pltpu.VMEM((rows // PIECE, PIECE, width), bf16)],
        compiler_params=params(60),
        cost_estimate=cost(2 * rows * width * outs, 20e6),
        name="project",
    )(own, other, x_own.reshape(pieces, PIECE, width), x_other.reshape(pieces, PIECE, width), gain, shift, w)


def cell_bounds(len_ref, cnt_ref):
    cells = len_ref.shape[1]
    starts, lives, start = [], [], jnp.int32(0)
    for c in range(cells):
        length = len_ref[0, c]
        starts.append(start)
        lives.append(start + jnp.minimum(length, cnt_ref[0, c]))
        start = start + length
    return starts, lives


def key_range(pos, starts, lives):
    low = jnp.zeros_like(pos) + starts[0]
    high = jnp.zeros_like(pos) + lives[0]
    for start, live in zip(starts[1:], lives[1:]):
        inside = pos >= start
        low = jnp.where(inside, start, low)
        high = jnp.where(inside, live, high)
    return low, high


def load_all(sems, *pairs):
    loads = [pltpu.make_async_copy(source, target, sems.at[i]) for i, (source, target) in enumerate(pairs)]
    for one in loads:
        one.start()
    for one in loads:
        one.wait()


def attend_kernel(
    own_ref, other_ref, len_ref, cnt_ref, k_in, qt_in, vt_in,
    ot_ref, own_out, other_out, lse_ref,
    k_ref, qt_ref, vt_ref, natural, bias, top, total, acc, load,
):
    load_all(load, (k_in, k_ref), (qt_in, qt_ref), (vt_in, vt_ref))
    rows, width = k_ref.shape
    heads = width // HEAD_DIM
    bk, bq = bias.shape
    starts, lives = cell_bounds(len_ref, cnt_ref)
    zeros = jnp.zeros((HEAD_DIM, bq), jnp.bfloat16)
    ones = jnp.ones((16, bk), jnp.bfloat16)

    def query_step(i, carry):
        q0 = pl.multiple_of(i * bq, bq)
        cols = pl.ds(q0, bq)
        low, high = key_range(q0 + lax.broadcasted_iota(jnp.int32, (1, bq), 1), starts, lives)
        first, _ = key_range(q0, starts, lives)
        _, last = key_range(q0 + bq - 1, starts, lives)
        origin = first // 128 * 128
        top[...] = jnp.full_like(top, MASKED)
        total[...] = jnp.zeros_like(total)
        acc[...] = jnp.zeros_like(acc)

        def key_step(j, carry):
            begin = origin + j * bk
            k0 = pl.multiple_of(jnp.minimum(begin, rows - bk), 128)
            keys = pl.ds(k0, bk)
            kpos = k0 + lax.broadcasted_iota(jnp.int32, (bk, bq), 0)
            bias[...] = jnp.where((kpos >= jnp.maximum(low, begin)) & (kpos < high), 0.0, MASKED)

            def score(h):
                lanes = slice(h // 2 * 128, h // 2 * 128 + 128)
                q = qt_ref[h * HEAD_DIM : (h + 1) * HEAD_DIM, cols]
                q = jnp.concatenate([q, zeros] if h % 2 == 0 else [zeros, q], axis=0)
                return dot(k_ref[keys, lanes], q)

            s = [score(0), score(1)]
            ps = {}

            def mix(h):
                p, decay = ps.pop(h)
                sub = slice(h * HEAD_DIM, (h + 1) * HEAD_DIM)
                v = jnp.concatenate([vt_ref[sub, keys], ones], axis=0)
                r = dot(v, p)
                acc[sub, :] = acc[sub, :] * decay + r[:HEAD_DIM]
                total[h : h + 1, :] = total[h : h + 1, :] * decay + r[HEAD_DIM : HEAD_DIM + 1]

            for h in range(heads):
                if h + 2 < heads:
                    s.append(score(h + 2))
                x = s[h] + bias[...]
                old = top[h : h + 1, :]
                new = jnp.maximum(old, jnp.max(x, axis=0, keepdims=True))
                p = jnp.exp(x - new).astype(jnp.bfloat16)
                ps[h] = (p, jnp.exp(old - new))
                top[h : h + 1, :] = new
                if h >= 1:
                    mix(h - 1)
            mix(heads - 1)
            return carry

        lax.fori_loop(0, (last - origin + bk - 1) // bk, key_step, 0)
        for h in range(heads):
            sub = slice(h * HEAD_DIM, (h + 1) * HEAD_DIM)
            acc[sub, :] = acc[sub, :] / total[h : h + 1, :]
            lse_ref[h : h + 1, cols] = top[h : h + 1, :] + jnp.log(total[h : h + 1, :])
        mixed = acc[...]
        ot_ref[:, cols] = mixed.astype(jnp.bfloat16)
        natural[pl.ds(i * (bq // PIECE), bq // PIECE)] = mixed.T.reshape(bq // PIECE, PIECE, width)
        return carry

    lax.fori_loop(0, rows // bq, query_step, 0)

    def step(j, carry):
        own_out[j] = natural[own_ref[j]].astype(jnp.bfloat16)
        other_out[j] = natural[other_ref[j]].astype(jnp.bfloat16)
        return carry

    lax.fori_loop(0, own_out.shape[0], step, 0, unroll=8)


def attend(own, other, lengths, counts, k, qt, vt):
    rows, width = k.shape
    count = own.shape[0]
    bk, bq = min(640, rows), min(256, rows)
    heads = width // HEAD_DIM
    ot, o_own, o_other, lse = pl.pallas_call(
        attend_kernel,
        out_shape=[
            struct((width, rows), jnp.bfloat16),
            struct((count, PIECE, width), jnp.bfloat16),
            struct((count, PIECE, width), jnp.bfloat16),
            struct((8, rows), jnp.float32),
        ],
        in_specs=[SMEM] * 4 + [ANYWHERE] * 3,
        out_specs=[VMEM] * 4,
        scratch_shapes=[
            *[pltpu.VMEM(one.shape, one.dtype) for one in (k, qt, vt)],
            pltpu.VMEM((rows // PIECE, PIECE, width), jnp.float32),
            pltpu.VMEM((bk, bq), jnp.float32),
            pltpu.VMEM((8, bq), jnp.float32),
            pltpu.VMEM((8, bq), jnp.float32),
            pltpu.VMEM((width, bq), jnp.float32),
            pltpu.SemaphoreType.DMA((3,)),
        ],
        compiler_params=params(60),
        cost_estimate=cost(2e10, 10e6, heads * rows * rows // 2),
        name="attend",
    )(own, other, lengths, counts, k, qt, vt)
    return ot, o_own.reshape(count * PIECE, width), o_other.reshape(count * PIECE, width), lse


def attend_back_kernel(
    own_ref, other_ref, len_ref, cnt_ref, q_in, k_in, v_in, qt_in, kt_in, ot_in, lse_in,
    do_own, do_other, out_ref,
    own_in, other_in, q_ref, ot_ref, k_ref, v_ref, qt_ref, kt_ref, lse_ref, natural, do_t, do_m, q_m, delta, dq_t, dk_acc, dv_acc, bias, load,
):
    load_all(
        load, (do_own, own_in), (do_other, other_in), (q_in, q_ref), (ot_in, ot_ref),
        (k_in, k_ref), (v_in, v_ref), (qt_in, qt_ref), (kt_in, kt_ref), (lse_in, lse_ref),
    )
    rows, width = k_ref.shape
    heads = width // HEAD_DIM
    bk, bq = bias.shape
    pieces = bq // PIECE
    starts, lives = cell_bounds(len_ref, cnt_ref)
    zeros = jnp.zeros((HEAD_DIM, bq), jnp.bfloat16)

    def place(j, carry):
        natural[own_ref[j]] = own_in[j].astype(jnp.float32)
        natural[other_ref[j]] = other_in[j].astype(jnp.float32)
        return carry

    lax.fori_loop(0, own_in.shape[0], place, 0, unroll=8)
    lane = lax.broadcasted_iota(jnp.int32, (bq, 128), 1)

    def prepare(i, carry):
        q0 = pl.multiple_of(i * bq, bq)
        at = pl.ds(q0, bq)
        do = natural[pl.ds(i * pieces, pieces)].reshape(bq, width)
        dot_t = do.T
        do_t[:, at] = dot_t.astype(jnp.bfloat16)
        for h in range(heads):
            sub = slice(h * HEAD_DIM, (h + 1) * HEAD_DIM)
            delta[h : h + 1, at] = jnp.sum(
                dot_t[sub, :] * ot_ref[sub, at].astype(jnp.float32), axis=0, keepdims=True
            )
            lanes = slice(h // 2 * 128, h // 2 * 128 + 128)
            mine = (lane < HEAD_DIM) if h % 2 == 0 else (lane >= HEAD_DIM)
            do_m[h, at, :] = jnp.where(mine, do[:, lanes], 0.0).astype(jnp.bfloat16)
            q_m[h, at, :] = jnp.where(mine, q_ref[at, lanes].astype(jnp.float32), 0.0).astype(jnp.bfloat16)
        dq_t[:, at] = jnp.zeros((width, bq), jnp.float32)
        return carry

    lax.fori_loop(0, rows // bq, prepare, 0)

    def key_step(j, carry):
        k0 = pl.multiple_of(j * bk, bk)
        keys = pl.ds(k0, bk)
        first, last = jnp.int32(rows), jnp.int32(0)
        for start, live in zip(starts, lives):
            met = (start < k0 + bk) & (live > k0)
            first = jnp.where(met, jnp.minimum(first, start), first)
            last = jnp.where(met, live, last)
        origin = first // 128 * 128
        dk_acc[...] = jnp.zeros_like(dk_acc)
        dv_acc[...] = jnp.zeros_like(dv_acc)

        def query_step(i, carry):
            begin = origin + i * bq
            q0 = pl.multiple_of(jnp.minimum(begin, rows - bq), 128)
            cols = pl.ds(q0, bq)
            qpos = q0 + lax.broadcasted_iota(jnp.int32, (1, bq), 1)
            low, high = key_range(qpos, starts, lives)
            low = jnp.where(qpos < begin, rows, low)
            kpos = k0 + lax.broadcasted_iota(jnp.int32, (bk, bq), 0)
            bias[...] = jnp.where((kpos >= low) & (kpos < high), 0.0, MASKED)

            def first_half(g):
                lanes = slice(g // 2 * 128, g // 2 * 128 + 128)
                sub = slice(g * HEAD_DIM, (g + 1) * HEAD_DIM)
                q, d = qt_ref[sub, cols], do_t[sub, cols]
                order = (lambda t: [t, zeros]) if g % 2 == 0 else (lambda t: [zeros, t])
                s = dot(k_ref[keys, lanes], jnp.concatenate(order(q), axis=0))
                dp = dot(v_ref[keys, lanes], jnp.concatenate(order(d), axis=0))
                return s, dp

            def second_half(g, p, ds):
                lanes = slice(g // 2 * 128, g // 2 * 128 + 128)
                sub = slice(g * HEAD_DIM, (g + 1) * HEAD_DIM)
                dv_acc[:, lanes] += dot(p, do_m[g, cols, :])
                dk_acc[:, lanes] += dot(ds, q_m[g, cols, :])
                dq_t[sub, cols] += dot(kt_ref[sub, keys], ds)

            ready = [first_half(0)]
            last_pair = None
            for g in range(heads):
                if g + 1 < heads:
                    ready.append(first_half(g + 1))
                s, dp = ready[g]
                p = jnp.exp(s + bias[...] - lse_ref[g : g + 1, cols])
                ds = (p * (dp - delta[g : g + 1, cols])).astype(jnp.bfloat16)
                if last_pair is not None:
                    second_half(*last_pair)
                last_pair = (g, p.astype(jnp.bfloat16), ds)
            second_half(*last_pair)
            return carry

        lax.fori_loop(0, (last - origin + bq - 1) // bq, query_step, 0)
        out_ref[1, keys, :] = dk_acc[...].astype(jnp.bfloat16)
        out_ref[2, keys, :] = dv_acc[...].astype(jnp.bfloat16)
        return carry

    lax.fori_loop(0, rows // bk, key_step, 0)

    def finish(i, carry):
        at = pl.ds(pl.multiple_of(i * bq, bq), bq)
        out_ref[0, at, :] = (dq_t[:, at].T * HEAD_DIM**-0.5).astype(jnp.bfloat16)
        return carry

    lax.fori_loop(0, rows // bq, finish, 0)


def attend_back(own, other, lengths, counts, q, k, v, qt, kt, ot, lse, do_own, do_other):
    rows, width = k.shape
    count = own.shape[0]
    bk = bq = min(256, rows)
    heads = width // HEAD_DIM
    return pl.pallas_call(
        attend_back_kernel,
        out_shape=struct((3, rows, width), jnp.bfloat16),
        in_specs=[SMEM] * 4 + [ANYWHERE] * 9,
        out_specs=VMEM,
        scratch_shapes=[
            *[pltpu.VMEM((count, PIECE, width), jnp.bfloat16)] * 2,
            *[pltpu.VMEM(one.shape, one.dtype) for one in (q, ot, k, v, qt, kt, lse)],
            pltpu.VMEM((rows // PIECE, PIECE, width), jnp.float32),
            pltpu.VMEM((width, rows), jnp.bfloat16),
            pltpu.VMEM((heads, rows, 128), jnp.bfloat16),
            pltpu.VMEM((heads, rows, 128), jnp.bfloat16),
            pltpu.VMEM((8, rows), jnp.float32),
            pltpu.VMEM((width, rows), jnp.float32),
            pltpu.VMEM((bk, width), jnp.float32),
            pltpu.VMEM((bk, width), jnp.float32),
            pltpu.VMEM((bk, bq), jnp.float32),
            pltpu.SemaphoreType.DMA((9,)),
        ],
        compiler_params=params(60),
        cost_estimate=cost(5e10, 20e6, heads * rows * rows // 2),
        name="attend_back",
    )(
        own, other, lengths, counts, q, k, v, qt, kt, ot, lse,
        do_own.reshape(count, PIECE, width), do_other.reshape(count, PIECE, width),
    )


def feed_kernel(
    x_ref, oa_ref, ob_ref, dy_ref, real_ref, gain_ref, shift_ref, *refs,
):
    weights, outs, held, load = refs[:6], refs[6:14], refs[14:20], refs[20]
    out_ref, y1_ref, gr_ref, turned_ref, act_a, act_b, slope_a, slope_b = outs
    wo_a, wo_b, up_a, down_a, up_b, down_b = held
    ready = resident([pltpu.make_async_copy(w, h, load.at[i]) for i, (w, h) in enumerate(zip(weights, held))])
    ready(0)
    ready(1)
    x = x_ref[...].astype(jnp.float32)
    y1 = x + dot(oa_ref[...], wo_a[...]) + dot(ob_ref[...], wo_b[...])
    y1_ref[...] = y1
    unit, _ = norm_unit(y1)
    h = (unit * gain_ref[...] + shift_ref[...]).astype(jnp.bfloat16)
    gr = (dy_ref[...].astype(jnp.float32) * real_ref[...]).astype(jnp.bfloat16)
    gr_ref[...] = gr
    turned_ref[0] = gr.T
    mlp = None
    for n, up, down, act_ref, slope_ref in ((2, up_a, down_a, act_a, slope_a), (4, up_b, down_b, act_b, slope_b)):
        ready(n)
        ready(n + 1)
        hidden = up.shape[1]
        part = min(768, hidden)
        for at in range(0, hidden, part):
            cols = slice(at, at + part)
            u = dot(h, up[:, cols])
            phi = 0.5 * (1.0 + lax.erf(u * 0.7071067811865476))
            act = (u * phi).astype(jnp.bfloat16)
            act_ref[:, cols] = act
            slope_ref[:, cols] = (phi + u * 0.3989422804014327 * jnp.exp(-0.5 * u * u)).astype(jnp.bfloat16)
            m = dot(act, down[cols, :])
            mlp = m if mlp is None else mlp + m
    out_ref[...] = (y1 + mlp).astype(jnp.bfloat16)


def feed_back_kernel(
    y1_ref, gr_ref, slope_a, slope_b, oa_ref, ob_ref, gain_ref, shift_ref, blocks_ref, *refs,
):
    weights, (left_a, left_b, right_ref, doa_ref, dob_ref, dy1_ref, norm_ref, sum_ref) = refs[:6], refs[6:14]
    held = refs[14:20]
    load, sent, got, more, send_sem, recv_sem = refs[20:]
    wo_a, wo_b, up_a, down_a, up_b, down_b = held
    loads = [pltpu.make_async_copy(w, h, load.at[i]) for i, (w, h) in enumerate(zip(weights, held))]
    loads.append(pltpu.make_async_copy(blocks_ref, sent, load.at[6]))
    ready = resident(loads)
    me = lax.axis_index("dp")
    e = me % NEAR
    step = pl.program_id(0)
    last = pl.num_programs(0) - 1
    cut = sum_ref.shape[0] // 2
    first, second = slice(0, cut), slice(cut, 2 * cut)

    def flip(d):
        return (e // 2 + d // 2) % 2 * 2 + (e % 2 + d % 2) % 2

    def trade(n):
        source, d = (
            (sent.at[flip(1), first], 1),
            (sent.at[flip(3), first], 1),
            (sent.at[flip(2), second], 2),
            (sent.at[flip(3), second], 2),
            (more.at[0], 2),
            (more.at[1], 1),
        )[n]
        return pltpu.make_async_remote_copy(
            source, got.at[n], send_sem.at[n], recv_sem.at[n],
            device_id={"dp": me // NEAR * NEAR + flip(d)}, device_id_type=MESH,
        )

    @pl.when(step == 0)
    def _():
        barrier = pltpu.get_barrier_semaphore()
        for d in (1, 2):
            to = me // NEAR * NEAR + flip(d)
            pl.semaphore_signal(barrier, inc=1, device_id={"dp": to}, device_id_type=MESH)
        pl.semaphore_wait(barrier, 2)

    ready(6)

    @pl.when(step == 0)
    def _():
        for n in (1, 3, 0, 2):
            trade(n).start()

    def second_trades():
        @pl.when(step == jnp.maximum(last - 1, 0))
        def _():
            f32 = jnp.float32
            for n, source in ((1, sent.at[flip(2), first]), (3, sent.at[flip(1), second])):
                trade(n).wait()
                more[n // 2] = (source[...].astype(f32) + got[n].astype(f32)).astype(jnp.bfloat16)
                trade(4 + n // 2).start()

    unit, inverse = norm_unit(y1_ref[...])
    right_ref[0] = (unit * gain_ref[...] + shift_ref[...]).astype(jnp.bfloat16).T
    gr = gr_ref[...]
    dh = None
    for n, up, down, slope_ref, left, o_ref in (
        (2, up_a, down_a, slope_a, left_a, oa_ref),
        (4, up_b, down_b, slope_b, left_b, ob_ref),
    ):
        ready(n)
        ready(n + 1)
        hidden = up.shape[1]
        part = min(768, hidden)
        for at in range(0, hidden, part):
            cols = slice(at, at + part)
            slope = slope_ref[:, cols].astype(jnp.float32)
            du = (dot(gr, down[cols, :], NT) * slope).astype(jnp.bfloat16)
            left[:, cols] = du
            d = dot(du, up[:, cols], NT)
            dh = d if dh is None else dh + d
        if n == 2:
            second_trades()
        local = o_ref.shape[1]
        left[:, hidden : hidden + local] = o_ref[...]
        left[:, hidden + local :] = jnp.zeros_like(left[:, hidden + local :])
    sums = jnp.concatenate(
        [jnp.sum(dh * unit, axis=0, keepdims=True), jnp.sum(dh, axis=0, keepdims=True)], axis=0
    )

    @pl.when(pl.program_id(0) == 0)
    def _():
        norm_ref[...] = sums

    @pl.when(pl.program_id(0) > 0)
    def _():
        norm_ref[...] += sums

    ready(0)
    ready(1)
    dy1 = gr.astype(jnp.float32) + norm_back(dh * gain_ref[...], unit, inverse)
    dy1_ref[...] = dy1
    dar = dy1.astype(jnp.bfloat16)
    right_ref[1] = dar.T
    doa_ref[...] = dot(dar, wo_a[...], NT).astype(jnp.bfloat16)
    dob_ref[...] = dot(dar, wo_b[...], NT).astype(jnp.bfloat16)

    @pl.when(step == last)
    def _():
        for at, n in ((first, 0), (second, 2)):
            trade(n).wait()
            trade(4 + n // 2).wait()
            total = sent[e, at].astype(jnp.float32) + got[n].astype(jnp.float32)
            sum_ref[at, :] = (total + got[4 + n // 2].astype(jnp.float32)).astype(jnp.bfloat16)


def feed_specs(rows):
    block = min(256, rows)

    def tall(cols):
        return pl.BlockSpec((block, cols), lambda i: (i, 0))

    return block, tall


def resident(loads):
    @pl.when(pl.program_id(0) == 0)
    def _():
        for one in loads:
            one.start()

    def ready(i):
        @pl.when(pl.program_id(0) == 0)
        def _():
            loads[i].wait()

    return ready


def feed(x, o_own, o_other, dy, real, wo, up, down, gain, shift):
    rows, width = x.shape
    local = o_own.shape[1]
    hidden = up[0].shape[1]
    block, tall = feed_specs(rows)
    weights = (*wo, up[0], down[0], up[1], down[1])
    bf16 = jnp.bfloat16
    return pl.pallas_call(
        feed_kernel,
        grid=(rows // block,),
        out_shape=[
            struct((rows, width), bf16),
            struct((rows, width), jnp.float32),
            struct((rows, width), bf16),
            struct((1, width, rows), bf16),
        ]
        + [struct((rows, hidden), bf16)] * 4,
        in_specs=[tall(width), tall(local), tall(local), tall(width), tall(1)] + [VMEM] * 2 + [ANYWHERE] * 6,
        out_specs=[tall(width)] * 3 + [pl.BlockSpec((1, width, block), lambda i: (0, 0, i))] + [tall(hidden)] * 4,
        scratch_shapes=[pltpu.VMEM(w.shape, bf16) for w in weights] + [pltpu.SemaphoreType.DMA((6,))],
        compiler_params=params(60),
        cost_estimate=cost(2 * rows * width * (hidden * 4 + local * 2), 45e6, rows * hidden * 4),
        name="feed",
    )(x, o_own, o_other, dy, real, gain, shift, *weights)


def feed_back(y1, gr, slope, o_own, o_other, wo, up, down, gain, shift, blocks):
    rows, width = y1.shape
    local = o_own.shape[1]
    hidden = up[0].shape[1]
    block, tall = feed_specs(rows)
    weights = (*wo, up[0], down[0], up[1], down[1])
    bf16 = jnp.bfloat16
    lefts = hidden // 3 * 4
    return pl.pallas_call(
        feed_back_kernel,
        grid=(rows // block,),
        out_shape=[
            struct((rows, lefts), bf16),
            struct((rows, lefts), bf16),
            struct((2, width, rows), bf16),
            struct((rows, local), bf16),
            struct((rows, local), bf16),
            struct((rows, width), jnp.float32),
            struct((2, width), jnp.float32),
            struct(blocks.shape[1:], bf16),
        ],
        in_specs=[tall(width), tall(width), tall(hidden), tall(hidden), tall(local), tall(local)]
        + [VMEM] * 2
        + [ANYWHERE] * 7,
        out_specs=[
            tall(lefts),
            tall(lefts),
            pl.BlockSpec((2, width, block), lambda i: (0, 0, i)),
            tall(local),
            tall(local),
            tall(width),
            pl.BlockSpec((2, width), lambda i: (0, 0)),
            pl.BlockSpec(blocks.shape[1:], lambda i: (0, 0)),
        ],
        scratch_shapes=[pltpu.VMEM(w.shape, bf16) for w in weights]
        + [
            pltpu.SemaphoreType.DMA((7,)),
            pltpu.VMEM(blocks.shape, bf16),
            pltpu.VMEM((6, blocks.shape[1] // 2, blocks.shape[2]), bf16),
            pltpu.VMEM((2, blocks.shape[1] // 2, blocks.shape[2]), bf16),
            pltpu.SemaphoreType.DMA((6,)),
            pltpu.SemaphoreType.DMA((6,)),
        ],
        compiler_params=pltpu.CompilerParams(collective_id=1, has_side_effects=True, vmem_limit_bytes=60 * MIB),
        cost_estimate=cost(2 * rows * width * (hidden * 4 + local * 2), 45e6),
        name="feed_back",
    )(y1, gr, *slope, o_own, o_other, gain, shift, blocks, *weights)


def weight_kernel(size, hosted, other_ref, own_ref, right_ref, *refs):
    if hosted:
        chunk_ref, *outs = refs[:5]
        share_ref, send, recv, send_sem, recv_sem, chunk, land, far_s, far_r, load, tiles, store = refs[5:]
    else:
        out_ref, send, recv, send_sem, recv_sem = refs
    step = pl.program_id(0)
    core = lax.axis_index("mp")
    me = lax.axis_index("dp")
    far = size // NEAR
    f, e = me // NEAR, me % NEAR

    def swapped(i):
        return pltpu.make_async_remote_copy(
            send.at[i], recv.at[i], send_sem.at[i], recv_sem.at[i],
            device_id={"mp": 1 - core}, device_id_type=MESH,
        )

    def spread(d):
        to = (f + d) % far
        return pltpu.make_async_remote_copy(
            chunk.at[to], land.at[d], far_s.at[d], far_r.at[d],
            device_id={"dp": to * NEAR + e}, device_id_type=MESH,
        )

    def flip(d):
        return (e // 2 + d // 2) % 2 * 2 + (e % 2 + d % 2) % 2

    def kept(d):
        return pltpu.make_async_copy(tiles.at[flip(d)], outs[d], store.at[d])

    @pl.when(step == 0)
    def _():
        barrier = pltpu.get_barrier_semaphore()
        pl.semaphore_signal(barrier, inc=1, device_id={"mp": 1 - core}, device_id_type=MESH)
        if hosted:
            fetch = pltpu.make_async_copy(chunk_ref, chunk, load)
            fetch.start()
            for d in range(1, far):
                to = (f + d) % far * NEAR + e
                pl.semaphore_signal(barrier, inc=1, device_id={"dp": to}, device_id_type=MESH)
            fetch.wait()
        pl.semaphore_wait(barrier, far if hosted else 1)
        if hosted:
            for d in range(1, far):
                spread(d).start()

    @pl.when(step < NEAR)
    def _():
        send[step] = dot(right_ref[0], other_ref[...]).astype(jnp.bfloat16)
        swapped(step).start()

    @pl.when(step >= NEAR)
    def _():
        total = dot(right_ref[0], own_ref[...])
        tile = step - NEAR
        swapped(tile).wait_recv()
        value = (total + recv[tile].astype(jnp.float32)).astype(jnp.bfloat16)
        if hosted:
            tiles[tile] = value
            for d in range(NEAR):

                @pl.when(flip(d) == tile)
                def _(d=d):
                    kept(d).start()

        else:
            out_ref[0] = value

    @pl.when(step == 2 * NEAR - 1)
    def _():
        for i in range(NEAR):
            swapped(i).wait_send()
        if hosted:
            for d in range(NEAR):
                kept(d).wait()
            total = chunk[f].astype(jnp.float32)
            for d in range(1, far):
                spread(d).wait()
                total = total + land[d].astype(jnp.float32)
            share_ref[...] = total.astype(jnp.bfloat16)


def weight_grads(own, other, right, size, chunk=None):
    rows, lefts = own.shape
    count, width, _ = right.shape
    block = lefts // NEAR
    far = size // NEAR
    bf16 = jnp.bfloat16
    dma = pltpu.SemaphoreType.DMA

    def pick(i):
        return (i % NEAR // (NEAR - 1) if count == 2 else 0, 0, 0)

    out_shape = [struct((NEAR, width, block), bf16)]
    in_specs = [
        pl.BlockSpec((rows, block), lambda i: (0, jnp.minimum(i, NEAR - 1))),
        pl.BlockSpec((rows, block), lambda i: (0, jnp.maximum(i - NEAR, 0))),
        pl.BlockSpec((1, width, rows), pick),
    ]
    out_specs = [pl.BlockSpec((1, width, block), lambda i: (jnp.maximum(i - NEAR, 0), 0, 0))]
    scratch = [pltpu.VMEM((NEAR, width, block), bf16)] * 2 + [dma((NEAR,))] * 2
    operands = [other, own, right]
    if chunk is not None:
        share, cols = chunk.shape[0] // far, chunk.shape[1]
        out_shape = [struct((width, block), bf16)] * NEAR + [struct((share, cols), bf16)]
        out_specs = [ANYWHERE] * NEAR
        in_specs.append(ANYWHERE)
        out_specs.append(pl.BlockSpec((share, cols), lambda i: (0, 0)))
        scratch += [pltpu.VMEM((far, share, cols), bf16)] * 2 + [dma((far,))] * 2 + [dma]
        scratch += [pltpu.VMEM((NEAR, width, block), bf16), dma((NEAR,))]
        operands.append(chunk.reshape(far, share, cols))
    return pl.pallas_call(
        functools.partial(weight_kernel, size, chunk is not None),
        grid=(2 * NEAR,),
        out_shape=out_shape,
        in_specs=in_specs,
        out_specs=out_specs,
        scratch_shapes=scratch,
        compiler_params=pltpu.CompilerParams(
            collective_id=2 if chunk is None else 3, has_side_effects=True, vmem_limit_bytes=60 * MIB
        ),
        cost_estimate=cost(4 * rows * width * lefts, 20e6),
        name="weight_grads",
    )(*operands)


def padded(rows, size):
    return -(-rows // (16 * size)) * 16 * size


def near_send(block, d, size):
    return lax.ppermute(block, "dp", [(i, i ^ d) for i in range(size)])


def add_up(blocks):
    total = blocks[0].astype(jnp.float32)
    for block in blocks[1:]:
        total = total + block.astype(jnp.float32)
    return total.astype(jnp.bfloat16)


def close_kernel(
    size, own_ref, other_ref, up_in, down_in, gain_ref, norm2_ref, grads_in, ht_in, w_in, dy1_in, x_in,
    up_out, down_out, second_out, rows_own, rows_other, norms_out,
    grads_ref, ht_ref, w_ref, dy1_ref, x_ref, mine_a, mine_c, part, natural, swap_s, swap_r, dx, acc_a, acc_c, land_a, land_c, near_b, near_m, sum_b, norm_s, norm_r, norm_t,
    near_sem_s, near_sem_r, far_sem_s, far_sem_r, part_s, part_r, trade_s, trade_r, pass_s, pass_r,
    small_s, small_r, mp_s, mp_r, local, load, store,
):
    far = size // NEAR
    bits = [1 << b for b in range(far.bit_length() - 1)]
    me = lax.axis_index("dp")
    core = lax.axis_index("mp")
    f, e = me // NEAR, me % NEAR
    rows_all, local_width = grads_ref.shape[1:]
    width = w_ref.shape[1]
    block = min(256, rows_all)
    bf16 = jnp.bfloat16

    def flip(value, mask, top):
        out, b = 0, 1
        while b < top:
            out = out + b * ((value // b + mask // b) % 2)
            b *= 2
        return out

    loads = [
        pltpu.make_async_copy(source, target, load.at[i])
        for i, (source, target) in enumerate(
            ((grads_in, grads_ref), (ht_in, ht_ref), (w_in, w_ref), (dy1_in, dy1_ref), (x_in, x_ref))
        )
    ]
    for i in (0, 1, 2, 3, 4):
        loads[i].start()

    barrier = pltpu.get_barrier_semaphore()

    def greet(d, carry):
        pl.semaphore_signal(barrier, inc=1, device_id={"dp": (me + d) % size}, device_id_type=MESH)
        return carry

    lax.fori_loop(1, size, greet, 0)
    pl.semaphore_signal(barrier, inc=1, device_id={"mp": 1 - core}, device_id_type=MESH)
    pl.semaphore_wait(barrier, size)

    def remote(source, target, send, recv, device):
        return pltpu.make_async_remote_copy(
            source, target, send, recv, device_id={"dp": device}, device_id_type=MESH
        )

    def beside(source, target, send, recv):
        return pltpu.make_async_remote_copy(
            source, target, send, recv, device_id={"mp": 1 - core}, device_id_type=MESH
        )

    def views(*refs):
        return lambda s, *at: refs[s].at[at]

    inputs, accs = views(up_in, None, sum_b), views(acc_a, None, acc_c)
    lands, outs = views(land_a, None, land_c), views(up_out, down_out, second_out)
    mines = (mine_a, down_in, mine_c)
    held = {b: [m for m in range(far) if m % (2 * b) == 0] for b in bits}
    slot = {}
    for b in bits:
        for m in held[b]:
            slot[b, m] = len(slot)
    arrivals = [(b, m) for b in reversed(bits) for m in held[b]]

    def reduce_copy(s, b, m):
        source = inputs(s, flip(f, m + b, far)) if b == 1 else accs(s, m + b)
        k = slot[b, m]
        return remote(source, lands(s, k), far_sem_s.at[s, k], far_sem_r.at[s, k], flip(f, b, far) * NEAR + e)

    def reduce_start(s, b):
        for m in held[b]:
            reduce_copy(s, b, m).start()

    def reduce_step(s, b):
        for m in held[b]:
            reduce_copy(s, b, m).wait_recv()
            base = inputs(s, flip(f, m, far)) if b == 1 else accs(s, m)
            total = (base[...].astype(jnp.float32) + lands(s, slot[b, m])[...].astype(jnp.float32)).astype(bf16)
            if 2 * b == far:
                mines[s][...] = total
            else:
                accs(s, m)[...] = total
        if 2 * b < far:
            reduce_start(s, 2 * b)
        else:
            kept(s).start()
            available(s, 0)

    def kept(s):
        return pltpu.make_async_copy(mines[s], outs(s, e, f), store.at[s])

    def held_at(s, m):
        return mines[s] if m == 0 else outs(s, e, flip(f, m, far))

    def spread_copy(s, b, m):
        piece = outs(s, e, flip(f, m, far))
        k = slot[b, m]
        return remote(held_at(s, m), piece, far_sem_s.at[3 + s, k], far_sem_r.at[3 + s, k], flip(f, b, far) * NEAR + e)

    def spread_arrival(s, b, m):
        piece = outs(s, e, flip(f, m + b, far))
        k = slot[b, m]
        return remote(piece, piece, far_sem_s.at[3 + s, k], far_sem_r.at[3 + s, k], flip(f, b, far) * NEAR + e)

    def near_copy(s, d, m):
        piece = outs(s, e, flip(f, m, far))
        return remote(held_at(s, m), piece, near_sem_s.at[s, d, m], near_sem_r.at[s, d, m], f * NEAR + flip(e, d, NEAR))

    def near_arrival(s, d, m):
        piece = outs(s, flip(e, d, NEAR), flip(f, m, far))
        return remote(piece, piece, near_sem_s.at[s, d, m], near_sem_r.at[s, d, m], f * NEAR + flip(e, d, NEAR))

    def near_pass(s, m):
        source, to = (1, 2) if m % 2 == 0 else (2, 1)
        piece = outs(s, flip(e, source, NEAR), flip(f, m, far))
        return remote(piece, piece, near_sem_s.at[s, 3, m], near_sem_r.at[s, 3, m], f * NEAR + flip(e, to, NEAR))

    def near_passed(s, m):
        to = 2 if m % 2 == 0 else 1
        piece = outs(s, flip(e, 3, NEAR), flip(f, m, far))
        return remote(piece, piece, near_sem_s.at[s, 3, m], near_sem_r.at[s, 3, m], f * NEAR + flip(e, to, NEAR))

    def available(s, m):
        for b in reversed(bits):
            if m % (2 * b) == 0:
                spread_copy(s, b, m).start()
        for d in (1, 2):
            near_copy(s, d, m).start()

    def arrive(s, b, m):
        spread_arrival(s, b, m).wait_recv()
        available(s, m + b)

    def pass_on(s, m):
        for d in (1, 2):
            near_arrival(s, d, m).wait_recv()
        near_pass(s, m).start()

    share = land_c.shape[1]

    half_block = far * share // 2

    def near_half(index, h):
        return pl.ds(pl.multiple_of(index * (2 * half_block) + h * half_block, 16), half_block)

    def part_copy(n):
        source, d = (
            (part.at[near_half(flip(e, 1, NEAR), 0)], 1),
            (part.at[near_half(flip(e, 3, NEAR), 0)], 1),
            (part.at[near_half(flip(e, 2, NEAR), 1)], 2),
            (part.at[near_half(flip(e, 3, NEAR), 1)], 2),
            (near_m.at[0], 2),
            (near_m.at[1], 1),
        )[n]
        return remote(source, near_b.at[n], part_s.at[n], part_r.at[n], f * NEAR + flip(e, d, NEAR))

    def trade(d):
        to = (me + d) % size
        return remote(dx.at[to], rows_own.at[me], trade_s.at[d], trade_r.at[d], to)

    def trade_arrival(d):
        source = (me - d + size) % size
        return remote(dx.at[source], rows_own.at[source], trade_s.at[d], trade_r.at[d], source)

    def passing(d):
        source = (me - d + size) % size
        return beside(rows_own.at[source], rows_other.at[source], pass_s.at[d], pass_r.at[d])

    def small(d):
        to = (me + d) % size
        return remote(norm_s, norm_r.at[me], small_s.at[d], small_r.at[d], to)

    def small_arrival(d):
        source = (me - d + size) % size
        return remote(norm_s, norm_r.at[source], small_s.at[d], small_r.at[d], source)

    reduce_start(0, 1)
    kept(1).start()
    available(1, 0)

    tall = width // 4

    def part_step(i, carry):
        for c in range(4):
            value = dot(ht_ref[c * tall : (c + 1) * tall, :], grads_ref[i])
            at = pl.multiple_of(i * width + c * tall, 16)
            part[pl.ds(at, tall), :] = value.astype(bf16)
        return carry

    loads[0].wait()
    loads[1].wait()
    lax.fori_loop(0, 3, part_step, 0)
    used = 3 * width
    if part.shape[0] > used:
        part[used:, :] = jnp.zeros((part.shape[0] - used, local_width), bf16)
    for n in (1, 3, 0, 2):
        part_copy(n).start()

    pieces = block // PIECE

    def grad_step(i, carry):
        at = pl.ds(pl.multiple_of(i * block, block), block)
        value = dot(grads_ref[0, at, :], w_ref[0], NT)
        value += dot(grads_ref[1, at, :], w_ref[1], NT)
        value += dot(grads_ref[2, at, :], w_ref[2], NT)
        natural[pl.ds(i * pieces, pieces)] = value.reshape(pieces, PIECE, width)
        return carry

    loads[2].wait()
    lax.fori_loop(0, rows_all // block, grad_step, 0)

    def pack(j, carry):
        swap_s[j] = natural[other_ref[j]].astype(bf16)
        return carry

    lax.fori_loop(0, swap_s.shape[0], pack, 0, unroll=8)
    half = beside(swap_s, swap_r, mp_s.at[0], mp_r.at[0])
    half.start()
    reduce_step(0, 1)
    for b, m in arrivals[:1]:
        arrive(1, b, m)

    half.wait_recv()
    loads[3].wait()
    loads[4].wait()
    group_rows = dx.shape[1]
    norm_s[...] = jnp.zeros_like(norm_s)
    norm_s[2:4, :] = norm2_ref[...]
    mine = x_ref.shape[0]
    step_rows = min(256, mine)
    step_pieces = step_rows // PIECE

    def finish_step(i, carry):
        def take(j, inner):
            k = i * step_pieces + j
            natural_own[j] = natural[own_ref[k]] + swap_r[k].astype(jnp.float32)
            return inner

        lax.fori_loop(0, step_pieces, take, 0, unroll=8)
        at = pl.ds(pl.multiple_of(i * step_rows, step_rows), step_rows)
        dh = natural_own[...].reshape(step_rows, width)
        unit, inverse = norm_unit(x_ref[at, :].astype(jnp.float32))
        norm_s[0:1, :] += jnp.sum(dh * unit, axis=0, keepdims=True)
        norm_s[1:2, :] += jnp.sum(dh, axis=0, keepdims=True)
        value = dy1_ref[at, :] + norm_back(dh * gain_ref[...], unit, inverse)
        per_step = step_rows // group_rows
        dx[pl.ds(i * per_step, per_step)] = value.astype(bf16).reshape(per_step, group_rows, width)
        return carry

    natural_own = norm_t
    lax.fori_loop(0, mine // step_rows, finish_step, 0)

    def send(d, carry):
        trade(d).start()
        return carry

    lax.fori_loop(1, size, send, 0)

    def send_small(d, carry):
        small(d).start()
        return carry

    lax.fori_loop(1, size, send_small, 0)
    keep = pltpu.make_async_copy(dx.at[me], rows_own.at[me], local.at[0])
    keep.start()
    keep_small = pltpu.make_async_copy(norm_s, norm_r.at[me], local.at[1])
    keep_small.start()

    for b in bits[1:]:
        reduce_step(0, b)
    f32 = jnp.float32
    for h, n in ((0, 1), (1, 3)):
        part_copy(n).wait_recv()
        base = part[near_half(flip(e, 2 - h, NEAR), h), :]
        near_m[h] = (base.astype(f32) + near_b[n].astype(f32)).astype(bf16)
        part_copy(4 + h).start()
    for h, n in ((0, 0), (1, 2)):
        part_copy(n).wait_recv()
        part_copy(4 + h).wait_recv()
        base = part[near_half(e, h), :]
        total = base.astype(f32) + near_b[n].astype(f32) + near_b[4 + h].astype(f32)
        for j in range(far // 2):
            sum_b[h * (far // 2) + j] = total[j * share : (j + 1) * share].astype(bf16)
    reduce_start(2, 1)

    pass_on(1, 0)
    for b, m in arrivals[1:]:
        arrive(1, b, m)
    for b, m in arrivals:
        pass_on(1, m + b)
    reduce_step(2, 1)
    pass_on(0, 0)
    arrive(0, *arrivals[0])
    for b in bits[1:]:
        reduce_step(2, b)
    for b, m in arrivals[1:]:
        arrive(0, b, m)
    for b, m in arrivals:
        pass_on(0, m + b)
    pass_on(2, 0)
    for b, m in arrivals:
        arrive(2, b, m)
    keep.wait()
    passing(0).start()

    def settle(d, carry):
        trade_arrival(d).wait_recv()
        passing(d).start()
        return carry

    lax.fori_loop(1, size, settle, 0)
    keep_small.wait()

    def settle_small(d, carry):
        small_arrival(d).wait_recv()
        return carry

    lax.fori_loop(1, size, settle_small, 0)

    def add(g, carry):
        return carry + norm_r[g]

    total = lax.fori_loop(0, size, add, jnp.zeros(norm_s.shape, jnp.float32))
    for d in range(1, size):
        small(d).wait_send()
    norm_s[...] = total
    last = beside(norm_s, norm_r.at[size], mp_s.at[1], mp_r.at[1])
    last.start()
    last.wait()
    norms_out[...] = norm_s[...] + norm_r[size]

    for b, m in arrivals:
        pass_on(2, m + b)
    for s in range(3):
        for m in range(far):
            near_passed(s, m).wait_recv()
    half.wait_send()
    for s in range(3):
        kept(s).wait()
    for n in range(6):
        part_copy(n).wait_send()
    for s in range(3):
        for b in bits:
            for m in held[b]:
                if s != 1:
                    reduce_copy(s, b, m).wait_send()
                spread_copy(s, b, m).wait_send()
        for m in range(far):
            near_copy(s, 1, m).wait_send()
            near_copy(s, 2, m).wait_send()
            near_pass(s, m).wait_send()

    passing(0).wait()

    def close(d, carry):
        trade(d).wait_send()
        passing(d).wait()
        return carry

    lax.fori_loop(1, size, close, 0)


def close(own, other, up_chunk, down_share, grads, ht, w, x, dy1, gain, norm2, size):
    far = size // NEAR
    rows, local = grads.shape[1:]
    width = w.shape[1]
    b = padded(3 * width, size)
    n = x.shape[0] // size
    bf16, f32 = jnp.bfloat16, jnp.float32
    shares = (up_chunk.shape[0] // far, down_share.shape[0])
    cols = (up_chunk.shape[1], down_share.shape[1])
    share_b = b // size
    dma = pltpu.SemaphoreType.DMA
    step = min(256, x.shape[0])
    up_sum, down_sum, second, rows_own, rows_other, norms = pl.pallas_call(
        functools.partial(close_kernel, size),
        out_shape=[
            struct((NEAR, far, shares[0], cols[0]), bf16),
            struct((NEAR, far, shares[1], cols[1]), bf16),
            struct((NEAR, far, share_b, local), bf16),
            struct((size, n, width), bf16),
            struct((size, n, width), bf16),
            struct((8, width), f32),
        ],
        in_specs=[SMEM, SMEM] + [VMEM] * 4 + [ANYWHERE] * 5,
        out_specs=[ANYWHERE] * 5 + [VMEM],
        scratch_shapes=[
            pltpu.VMEM(grads.shape, bf16),
            pltpu.VMEM(ht.shape, bf16),
            pltpu.VMEM(w.shape, bf16),
            pltpu.VMEM(dy1.shape, f32),
            pltpu.VMEM(x.shape, bf16),
            pltpu.VMEM((shares[0], cols[0]), bf16),
            pltpu.VMEM((share_b, local), bf16),
            pltpu.VMEM((b, local), bf16),
            pltpu.VMEM((rows // PIECE, PIECE, width), f32),
            pltpu.VMEM((x.shape[0] // PIECE, PIECE, width), bf16),
            pltpu.VMEM((x.shape[0] // PIECE, PIECE, width), bf16),
            pltpu.VMEM((size, n, width), bf16),
            pltpu.VMEM((far, shares[0], cols[0]), bf16),
            pltpu.VMEM((far, share_b, local), bf16),
            pltpu.VMEM((far, shares[0], cols[0]), bf16),
            pltpu.VMEM((far, share_b, local), bf16),
            pltpu.VMEM((6, b // NEAR // 2, local), bf16),
            pltpu.VMEM((2, b // NEAR // 2, local), bf16),
            pltpu.VMEM((far, share_b, local), bf16),
            pltpu.VMEM((8, width), f32),
            pltpu.VMEM((size + 1, 8, width), f32),
            pltpu.VMEM((step // PIECE, PIECE, width), f32),
            dma((3, NEAR, far)),
            dma((3, NEAR, far)),
            dma((6, far)),
            dma((6, far)),
            dma((6,)),
            dma((6,)),
            dma((size,)),
            dma((size,)),
            dma((size,)),
            dma((size,)),
            dma((size,)),
            dma((size,)),
            dma((2,)),
            dma((2,)),
            dma((2,)),
            dma((5,)),
            dma((3,)),
        ],
        compiler_params=pltpu.CompilerParams(
            collective_id=0, has_side_effects=True, vmem_limit_bytes=60 * MIB
        ),
        cost_estimate=cost(8 * rows * width * local, 1e8),
        name="close",
    )(
        own, other, up_chunk.reshape(far, shares[0], cols[0]), down_share, gain, norm2,
        grads, ht, w, dy1, x,
    )
    return (
        up_sum.reshape(NEAR, -1, cols[0]),
        down_sum.reshape(NEAR, -1, cols[1]),
        second.reshape(b, local),
        rows_own.reshape(-1, width),
        rows_other.reshape(-1, width),
        norms,
    )


def settle_kernel(
    own_ref, other_ref, mixed_a, mixed_b, dx_a, dx_b, up_in, down_in, qkv_in,
    mixed_out, dx_out, up_out, down_out, wo_out, qkv_out,
    halves, mixed, dx, up_v, down_v, qkv_v, up, down, wo, qkv, load, store,
):
    f32 = jnp.float32
    sources = (mixed_a, mixed_b, dx_a, dx_b)
    loads = [pltpu.make_async_copy(one, halves.at[i], load.at[i]) for i, one in enumerate(sources)]
    more = ((up_in, up_v), (down_in, down_v), (qkv_in, qkv_v))
    loads += [pltpu.make_async_copy(one, to, load.at[4 + i]) for i, (one, to) in enumerate(more)]
    for one in loads:
        one.start()
    stores = []

    def keep(source, target):
        stores.append(pltpu.make_async_copy(source, target, store.at[len(stores)]))
        stores[-1].start()

    for i, (merged, target) in enumerate(((mixed, mixed_out), (dx, dx_out))):
        loads[2 * i].wait()
        loads[2 * i + 1].wait()

        def step(j, carry):
            merged[own_ref[j]] = halves[2 * i, j]
            merged[other_ref[j]] = halves[2 * i + 1, j]
            return carry

        lax.fori_loop(0, halves.shape[1], step, 0, unroll=8)
        keep(merged, target)
    loads[4].wait()
    width = up.shape[0]
    cols = up.shape[1] // (NEAR - 1)
    for e in range(NEAR - 1):
        up[:, e * cols : (e + 1) * cols] = up_v[e, :width, :].astype(f32)
    keep(up, up_out)
    wo[...] = up_v[NEAR - 1, :width, : wo.shape[0]].astype(f32).T
    keep(wo, wo_out)
    loads[5].wait()
    cols = down.shape[0] // NEAR
    for e in range(NEAR):
        down[e * cols : (e + 1) * cols, :] = down_v[e, :width, :].astype(f32).T
    keep(down, down_out)
    loads[6].wait()
    qkv[...] = qkv_v[: qkv.shape[0], :].astype(f32)
    keep(qkv, qkv_out)
    for one in stores:
        one.wait()


def settle(own, other, mixed, dx, up_sum, down_sum, qkv_sum, hidden, local):
    rows, width = mixed[0].shape
    count = rows // PIECE
    pieces = (count, PIECE, width)
    f32, bf16 = jnp.float32, jnp.bfloat16
    outs = [
        struct((2 * count, PIECE, width), bf16),
        struct((2 * count, PIECE, width), bf16),
        struct((width, hidden), f32),
        struct((hidden, width), f32),
        struct((local, width), f32),
        struct((3 * width, local), f32),
    ]
    held = [pltpu.VMEM(one.shape, one.dtype) for one in outs]
    sums = [pltpu.VMEM(one.shape, bf16) for one in (up_sum, down_sum, qkv_sum)]
    mixed_out, dx_out, *grads = pl.pallas_call(
        settle_kernel,
        out_shape=outs,
        in_specs=[SMEM] * 2 + [ANYWHERE] * 7,
        out_specs=[ANYWHERE] * 6,
        scratch_shapes=[
            pltpu.VMEM((4, *pieces), bf16),
            *held[:2],
            *sums,
            *held[2:],
            pltpu.SemaphoreType.DMA((7,)),
            pltpu.SemaphoreType.DMA((6,)),
        ],
        compiler_params=params(60),
        cost_estimate=cost(0, 34e6),
        name="settle",
    )(own, other, *[one.reshape(pieces) for one in (*mixed, *dx)], up_sum, down_sum, qkv_sum)
    return mixed_out.reshape(2 * rows, width), dx_out.reshape(2 * rows, width), *grads


def swap(value):
    return lax.ppermute(value, "mp", [(0, 1), (1, 0)])


def held_kernel(value_ref, after_ref, out_ref):
    del value_ref, after_ref, out_ref


def held_until(value, after):
    return pl.pallas_call(
        held_kernel,
        out_shape=struct(value.shape, value.dtype),
        in_specs=[ANYWHERE] * 2,
        out_specs=ANYWHERE,
        input_output_aliases={0: 0},
        name="held_until",
    )(value, after)


def exchange(value):
    return lax.all_to_all(value, "dp", split_axis=0, concat_axis=0, tiled=True)


def body(
    tokens, out_grad, lengths, counts, dest_slot, qkv_weight, out_weight, up_weight, down_weight,
    norm1_gain, norm1_shift, norm2_gain, norm2_shift,
):
    groups = lax.axis_size("dp")
    me = lax.axis_index("dp")
    core = lax.axis_index("mp")
    rows, width = tokens.shape
    per = rows // PIECE
    capacity = per // groups
    half = capacity // 2
    local = qkv_weight.shape[2]
    bf16 = jnp.bfloat16

    slots = dest_slot.reshape(groups, per)
    my_slots = lax.dynamic_index_in_dim(slots, me, 0, keepdims=True)
    group_ids = jnp.arange(groups, dtype=jnp.int32)[:, None]
    piece_ids = jnp.broadcast_to(jnp.arange(per, dtype=jnp.int32)[None, :], (groups, per))
    source = slot_table(my_slots // per == group_ids, piece_ids, capacity)
    target = slot_table(slots // per == me, slots - me * per, capacity)

    def halves(table):
        own = lax.dynamic_slice_in_dim(table, core * half, half, 1)
        other = lax.dynamic_slice_in_dim(table, (1 - core) * half, half, 1)
        return own.reshape(-1), other.reshape(-1)

    src_own, src_other = halves(source)
    own, other = halves(target)

    x_own = exchange(gather_pieces(src_own, tokens))
    dy_send = gather_pieces(src_own, out_grad)
    place = (own[:, None] * PIECE + jnp.arange(PIECE, dtype=jnp.int32)[None, :]).reshape(-1, 1)
    real, start = jnp.zeros(place.shape, jnp.bool_), jnp.int32(0)
    for c in range(lengths.shape[1]):
        live = start + jnp.minimum(lengths[0, c], counts[0, c])
        real, start = real | ((place >= start) & (place < live)), start + lengths[0, c]
    real = real.astype(jnp.float32)
    wo_other, up_other, down_other = swap(out_weight), swap(up_weight), swap(down_weight)
    gain1, shift1 = norm1_gain[None], norm1_shift[None]
    gain2, shift2 = norm2_gain[None], norm2_shift[None]
    x_own, dy_send, real, wo_other, up_other, down_other, own, other, gain1, shift1, gain2, shift2 = (
        lax.optimization_barrier(
            (
                x_own, dy_send, real, wo_other, up_other, down_other,
                own, other, gain1, shift1, gain2, shift2,
            )
        )
    )
    wo, up, down = (out_weight, wo_other), (up_weight, up_other), (down_weight, down_other)
    x_other = swap(x_own)

    h1_t, q, k, v, qt, kt, vt = project(own, other, x_own, x_other, gain1, shift1, qkv_weight)

    dy_own = exchange(dy_send)
    ot, o_own, o_send, lse = attend(own, other, lengths, counts, k, qt, vt)
    o_other = swap(o_send)

    out_rows, y1, gr, gr_turned, act_own, act_other, slope_own, slope_other = feed(
        x_own, o_own, o_other, dy_own, real, wo, up, down, gain2, shift2
    )
    [down_blocks] = weight_grads(act_own, act_other, gr_turned, groups)
    left_own, left_other, right, do_own, do_send, dy1, norm2, down_chunk = feed_back(
        y1, gr, (slope_own, slope_other), o_own, o_other, wo, up, down, gain2, shift2, down_blocks
    )
    do_other = swap(do_send)
    unit = 16 * (groups // NEAR)
    down_chunk = jnp.pad(down_chunk, ((0, -down_chunk.shape[0] % unit), (0, 0)))
    *up_blocks, down_share = weight_grads(left_own, left_other, right, groups, down_chunk)
    up_blocks, do_own, do_other = lax.optimization_barrier((up_blocks, do_own, do_other))
    up_got = [near_send(up_blocks[d], d, groups) for d in range(1, NEAR)]
    out_back = exchange(held_until(out_rows, swap(up_blocks[0][:16, :128])))
    grads = attend_back(own, other, lengths, counts, q, k, v, qt, kt, ot, lse, do_own, do_other)
    up_got, grads, out_back = lax.optimization_barrier((up_got, grads, out_back))
    out_other = swap(out_back)
    up_chunk = add_up([up_blocks[0], *up_got])
    up_chunk = jnp.pad(up_chunk, ((0, -up_chunk.shape[0] % unit), (0, 0)))
    up_sum, down_sum, qkv_grad, dx_own, dx_other, norms = close(
        own, other, up_chunk, down_share, grads, h1_t, qkv_weight, x_own, dy1, gain1, norm2, groups
    )
    mixed_out, input_grad, up_grad, down_grad, wo_grad, qkv_grad = settle(
        src_own, src_other, (out_back, out_other), (dx_own, dx_other), up_sum, down_sum, qkv_grad,
        up_weight.shape[1], local,
    )
    qkv_grad = qkv_grad.reshape(3, width, local)

    return (
        mixed_out, input_grad, qkv_grad, wo_grad, up_grad, down_grad,
        norms[0], norms[1], norms[2], norms[3],
    )


def solution(mesh):
    in_specs = (
        P("dp", None), P("dp", None), P("dp", None), P("dp", None), P(),
        P(None, None, "mp"), P("mp", None), P(None, "mp"), P("mp", None), P(), P(), P(), P(),
    )
    out_specs = (
        P("dp", None), P("dp", None), P(None, None, "mp"), P("mp", None), P(None, "mp"), P("mp", None),
        P(), P(), P(), P(),
    )
    return jax.shard_map(body, mesh=mesh, in_specs=in_specs, out_specs=out_specs, check_vma=False)
```

```python
import functools

import jax
import jax.numpy as jnp
from jax import lax
from jax.experimental import pallas as pl
from jax.experimental.pallas import tpu as pltpu
from jax.sharding import PartitionSpec as P

HEAD_DIM = 64
PIECE = 8
NORM_EPS = 1e-05
MASKED = -1e30
MIB = 2**20
VMEM = pl.BlockSpec(memory_space=pltpu.VMEM)
SMEM = pl.BlockSpec(memory_space=pltpu.SMEM)
NEAR = 4
MESH = pl.DeviceIdType.MESH
ANYWHERE = pl.BlockSpec(memory_space=pl.ANY)
NT = (((1,), (1,)), ((), ()))
TN = (((0,), (0,)), ((), ()))


def params(mib):
    return pltpu.CompilerParams(vmem_limit_bytes=mib * MIB)


def cost(flops, nbytes, transcendentals=0):
    return pl.CostEstimate(
        flops=int(flops), bytes_accessed=int(nbytes), transcendentals=int(transcendentals)
    )


def struct(shape, dtype):
    return jax.ShapeDtypeStruct(shape, dtype)


def dot(a, b, dims=None):
    if dims is None:
        return jnp.dot(a, b, preferred_element_type=jnp.float32)
    return lax.dot_general(a, b, dims, preferred_element_type=jnp.float32)


def norm_unit(values):
    mean = jnp.mean(values, axis=-1, keepdims=True)
    centred = values - mean
    variance = jnp.mean(centred * centred, axis=-1, keepdims=True)
    inverse = lax.rsqrt(variance + NORM_EPS)
    return centred * inverse, inverse


def norm_back(grad_unit, unit, inverse):
    first = jnp.mean(grad_unit, axis=-1, keepdims=True)
    second = jnp.mean(grad_unit * unit, axis=-1, keepdims=True)
    return inverse * (grad_unit - first - unit * second)


def slot_table(chosen, values, capacity):
    per = chosen.shape[1]
    place = lax.broadcasted_iota(jnp.int32, (per, per), 0)
    earlier = place < lax.broadcasted_iota(jnp.int32, (per, per), 1)
    rank = dot(chosen.astype(jnp.bfloat16), earlier.astype(jnp.bfloat16)).astype(jnp.int32)
    rank = jnp.where(chosen, rank, -1)
    ranks = jnp.arange(capacity, dtype=jnp.int32)
    hit = rank[:, None, :] == ranks[None, :, None]
    return jnp.sum(jnp.where(hit, values[:, None, :], 0), axis=2)


def gather_kernel(index_ref, source_ref, out_ref):
    def step(j, carry):
        out_ref[j] = source_ref[index_ref[j]]
        return carry

    lax.fori_loop(0, out_ref.shape[0], step, 0, unroll=8)


def gather_pieces(index, source):
    rows, width = source.shape
    count = index.shape[0]
    out = pl.pallas_call(
        gather_kernel,
        out_shape=struct((count, PIECE, width), source.dtype),
        in_specs=[SMEM, VMEM],
        out_specs=VMEM,
        compiler_params=params(60),
        cost_estimate=cost(0, 3 * rows * width),
        name="gather_pieces",
    )(index, source.reshape(rows // PIECE, PIECE, width))
    return out.reshape(count * PIECE, width)


def project_kernel(
    own_ref, other_ref, own_in, other_in, gain_ref, shift_ref, w_ref,
    ht_ref, q_ref, k_ref, v_ref, qt_ref, kt_ref, vt_ref, x_all,
):
    @pl.when(pl.program_id(0) == 0)
    def _():
        def step(j, carry):
            x_all[own_ref[j]] = own_in[j]
            x_all[other_ref[j]] = other_in[j]
            return carry

        lax.fori_loop(0, own_in.shape[0], step, 0, unroll=8)

    block, local = q_ref.shape
    pieces = block // PIECE
    x = x_all[pl.ds(pl.program_id(0) * pieces, pieces)].astype(jnp.float32).reshape(block, -1)
    unit, _ = norm_unit(x)
    h = (unit * gain_ref[...] + shift_ref[...]).astype(jnp.bfloat16)
    ht_ref[...] = h.T
    for i, (n_ref, t_ref) in enumerate(((q_ref, qt_ref), (k_ref, kt_ref), (v_ref, vt_ref))):
        scale = HEAD_DIM**-0.5 if i == 0 else 1.0
        value = (dot(h, w_ref[i]) * scale).astype(jnp.bfloat16)
        n_ref[...] = value
        t_ref[...] = value.T


def project(own, other, x_own, x_other, gain, shift, w):
    half, width = x_own.shape
    rows, local = 2 * half, w.shape[2]
    outs = 3 * local
    pieces = half // PIECE
    block = min(512, rows)
    bf16 = jnp.bfloat16

    def whole(shape):
        return pl.BlockSpec(shape, lambda i: (0,) * len(shape), pipeline_mode=pl.Buffered(1))

    natural = pl.BlockSpec((block, local), lambda i: (i, 0))
    turned = pl.BlockSpec((local, block), lambda i: (0, i))
    return pl.pallas_call(
        project_kernel,
        grid=(rows // block,),
        out_shape=[struct((width, rows), bf16)] + [struct((rows, local), bf16)] * 3 + [struct((local, rows), bf16)] * 3,
        in_specs=[SMEM, SMEM]
        + [whole((pieces, PIECE, width))] * 2
        + [whole((1, width))] * 2
        + [whole(w.shape)],
        out_specs=[pl.BlockSpec((width, block), lambda i: (0, i))] + [natural] * 3 + [turned] * 3,
        scratch_shapes=[pltpu.VMEM((rows // PIECE, PIECE, width), bf16)],
        compiler_params=params(60),
        cost_estimate=cost(2 * rows * width * outs, 20e6),
        name="project",
    )(own, other, x_own.reshape(pieces, PIECE, width), x_other.reshape(pieces, PIECE, width), gain, shift, w)


def cell_bounds(len_ref, cnt_ref):
    cells = len_ref.shape[1]
    starts, lives, start = [], [], jnp.int32(0)
    for c in range(cells):
        length = len_ref[0, c]
        starts.append(start)
        lives.append(start + jnp.minimum(length, cnt_ref[0, c]))
        start = start + length
    return starts, lives


def key_range(pos, starts, lives):
    low = jnp.zeros_like(pos) + starts[0]
    high = jnp.zeros_like(pos) + lives[0]
    for start, live in zip(starts[1:], lives[1:]):
        inside = pos >= start
        low = jnp.where(inside, start, low)
        high = jnp.where(inside, live, high)
    return low, high


def load_all(sems, *pairs):
    loads = [pltpu.make_async_copy(source, target, sems.at[i]) for i, (source, target) in enumerate(pairs)]
    for one in loads:
        one.start()
    for one in loads:
        one.wait()


def attend_kernel(
    own_ref, other_ref, len_ref, cnt_ref, k_in, qt_in, vt_in,
    ot_ref, own_out, other_out, lse_ref,
    k_ref, qt_ref, vt_ref, natural, bias, top, total, acc, load,
):
    load_all(load, (k_in, k_ref), (qt_in, qt_ref), (vt_in, vt_ref))
    rows, width = k_ref.shape
    heads = width // HEAD_DIM
    bk, bq = bias.shape
    starts, lives = cell_bounds(len_ref, cnt_ref)
    zeros = jnp.zeros((HEAD_DIM, bq), jnp.bfloat16)
    ones = jnp.ones((16, bk), jnp.bfloat16)

    def query_step(i, carry):
        q0 = pl.multiple_of(i * bq, bq)
        cols = pl.ds(q0, bq)
        low, high = key_range(q0 + lax.broadcasted_iota(jnp.int32, (1, bq), 1), starts, lives)
        first, _ = key_range(q0, starts, lives)
        _, last = key_range(q0 + bq - 1, starts, lives)
        origin = first // 128 * 128
        top[...] = jnp.full_like(top, MASKED)
        total[...] = jnp.zeros_like(total)
        acc[...] = jnp.zeros_like(acc)

        def key_step(j, carry):
            begin = origin + j * bk
            k0 = pl.multiple_of(jnp.minimum(begin, rows - bk), 128)
            keys = pl.ds(k0, bk)
            kpos = k0 + lax.broadcasted_iota(jnp.int32, (bk, bq), 0)
            bias[...] = jnp.where((kpos >= jnp.maximum(low, begin)) & (kpos < high), 0.0, MASKED)

            def score(h):
                lanes = slice(h // 2 * 128, h // 2 * 128 + 128)
                q = qt_ref[h * HEAD_DIM : (h + 1) * HEAD_DIM, cols]
                q = jnp.concatenate([q, zeros] if h % 2 == 0 else [zeros, q], axis=0)
                return dot(k_ref[keys, lanes], q)

            s = [score(0), score(1)]
            ps = {}

            def mix(h):
                p, decay = ps.pop(h)
                sub = slice(h * HEAD_DIM, (h + 1) * HEAD_DIM)
                v = jnp.concatenate([vt_ref[sub, keys], ones], axis=0)
                r = dot(v, p)
                acc[sub, :] = acc[sub, :] * decay + r[:HEAD_DIM]
                total[h : h + 1, :] = total[h : h + 1, :] * decay + r[HEAD_DIM : HEAD_DIM + 1]

            for h in range(heads):
                if h + 2 < heads:
                    s.append(score(h + 2))
                x = s[h] + bias[...]
                old = top[h : h + 1, :]
                new = jnp.maximum(old, jnp.max(x, axis=0, keepdims=True))
                p = jnp.exp(x - new).astype(jnp.bfloat16)
                ps[h] = (p, jnp.exp(old - new))
                top[h : h + 1, :] = new
                if h >= 1:
                    mix(h - 1)
            mix(heads - 1)
            return carry

        lax.fori_loop(0, (last - origin + bk - 1) // bk, key_step, 0)
        for h in range(heads):
            sub = slice(h * HEAD_DIM, (h + 1) * HEAD_DIM)
            acc[sub, :] = acc[sub, :] / total[h : h + 1, :]
            lse_ref[h : h + 1, cols] = top[h : h + 1, :] + jnp.log(total[h : h + 1, :])
        mixed = acc[...]
        ot_ref[:, cols] = mixed.astype(jnp.bfloat16)
        natural[pl.ds(i * (bq // PIECE), bq // PIECE)] = mixed.T.reshape(bq // PIECE, PIECE, width)
        return carry

    lax.fori_loop(0, rows // bq, query_step, 0)

    def step(j, carry):
        own_out[j] = natural[own_ref[j]].astype(jnp.bfloat16)
        other_out[j] = natural[other_ref[j]].astype(jnp.bfloat16)
        return carry

    lax.fori_loop(0, own_out.shape[0], step, 0, unroll=8)


def attend(own, other, lengths, counts, k, qt, vt):
    rows, width = k.shape
    count = own.shape[0]
    bk, bq = min(640, rows), min(256, rows)
    heads = width // HEAD_DIM
    ot, o_own, o_other, lse = pl.pallas_call(
        attend_kernel,
        out_shape=[
            struct((width, rows), jnp.bfloat16),
            struct((count, PIECE, width), jnp.bfloat16),
            struct((count, PIECE, width), jnp.bfloat16),
            struct((8, rows), jnp.float32),
        ],
        in_specs=[SMEM] * 4 + [ANYWHERE] * 3,
        out_specs=[VMEM] * 4,
        scratch_shapes=[
            *[pltpu.VMEM(one.shape, one.dtype) for one in (k, qt, vt)],
            pltpu.VMEM((rows // PIECE, PIECE, width), jnp.float32),
            pltpu.VMEM((bk, bq), jnp.float32),
            pltpu.VMEM((8, bq), jnp.float32),
            pltpu.VMEM((8, bq), jnp.float32),
            pltpu.VMEM((width, bq), jnp.float32),
            pltpu.SemaphoreType.DMA((3,)),
        ],
        compiler_params=params(60),
        cost_estimate=cost(2e10, 10e6, heads * rows * rows // 2),
        name="attend",
    )(own, other, lengths, counts, k, qt, vt)
    return ot, o_own.reshape(count * PIECE, width), o_other.reshape(count * PIECE, width), lse


def attend_back_kernel(
    own_ref, other_ref, len_ref, cnt_ref, q_in, k_in, v_in, qt_in, kt_in, ot_in, lse_in,
    do_own, do_other, out_ref,
    own_in, other_in, q_ref, ot_ref, k_ref, v_ref, qt_ref, kt_ref, lse_ref, natural, do_t, do_m, q_m, delta, dq_t, dk_acc, dv_acc, bias, load,
):
    load_all(
        load, (do_own, own_in), (do_other, other_in), (q_in, q_ref), (ot_in, ot_ref),
        (k_in, k_ref), (v_in, v_ref), (qt_in, qt_ref), (kt_in, kt_ref), (lse_in, lse_ref),
    )
    rows, width = k_ref.shape
    heads = width // HEAD_DIM
    bk, bq = bias.shape
    pieces = bq // PIECE
    starts, lives = cell_bounds(len_ref, cnt_ref)
    zeros = jnp.zeros((HEAD_DIM, bq), jnp.bfloat16)

    def place(j, carry):
        natural[own_ref[j]] = own_in[j].astype(jnp.float32)
        natural[other_ref[j]] = other_in[j].astype(jnp.float32)
        return carry

    lax.fori_loop(0, own_in.shape[0], place, 0, unroll=8)
    lane = lax.broadcasted_iota(jnp.int32, (bq, 128), 1)

    def prepare(i, carry):
        q0 = pl.multiple_of(i * bq, bq)
        at = pl.ds(q0, bq)
        do = natural[pl.ds(i * pieces, pieces)].reshape(bq, width)
        dot_t = do.T
        do_t[:, at] = dot_t.astype(jnp.bfloat16)
        for h in range(heads):
            sub = slice(h * HEAD_DIM, (h + 1) * HEAD_DIM)
            delta[h : h + 1, at] = jnp.sum(
                dot_t[sub, :] * ot_ref[sub, at].astype(jnp.float32), axis=0, keepdims=True
            )
            lanes = slice(h // 2 * 128, h // 2 * 128 + 128)
            mine = (lane < HEAD_DIM) if h % 2 == 0 else (lane >= HEAD_DIM)
            do_m[h, at, :] = jnp.where(mine, do[:, lanes], 0.0).astype(jnp.bfloat16)
            q_m[h, at, :] = jnp.where(mine, q_ref[at, lanes].astype(jnp.float32), 0.0).astype(jnp.bfloat16)
        dq_t[:, at] = jnp.zeros((width, bq), jnp.float32)
        return carry

    lax.fori_loop(0, rows // bq, prepare, 0)

    def key_step(j, carry):
        k0 = pl.multiple_of(j * bk, bk)
        keys = pl.ds(k0, bk)
        first, last = jnp.int32(rows), jnp.int32(0)
        for start, live in zip(starts, lives):
            met = (start < k0 + bk) & (live > k0)
            first = jnp.where(met, jnp.minimum(first, start), first)
            last = jnp.where(met, live, last)
        origin = first // 128 * 128
        dk_acc[...] = jnp.zeros_like(dk_acc)
        dv_acc[...] = jnp.zeros_like(dv_acc)

        def query_step(i, carry):
            begin = origin + i * bq
            q0 = pl.multiple_of(jnp.minimum(begin, rows - bq), 128)
            cols = pl.ds(q0, bq)
            qpos = q0 + lax.broadcasted_iota(jnp.int32, (1, bq), 1)
            low, high = key_range(qpos, starts, lives)
            low = jnp.where(qpos < begin, rows, low)
            kpos = k0 + lax.broadcasted_iota(jnp.int32, (bk, bq), 0)
            bias[...] = jnp.where((kpos >= low) & (kpos < high), 0.0, MASKED)

            def first_half(g):
                lanes = slice(g // 2 * 128, g // 2 * 128 + 128)
                sub = slice(g * HEAD_DIM, (g + 1) * HEAD_DIM)
                q, d = qt_ref[sub, cols], do_t[sub, cols]
                order = (lambda t: [t, zeros]) if g % 2 == 0 else (lambda t: [zeros, t])
                s = dot(k_ref[keys, lanes], jnp.concatenate(order(q), axis=0))
                dp = dot(v_ref[keys, lanes], jnp.concatenate(order(d), axis=0))
                return s, dp

            def second_half(g, p, ds):
                lanes = slice(g // 2 * 128, g // 2 * 128 + 128)
                sub = slice(g * HEAD_DIM, (g + 1) * HEAD_DIM)
                dv_acc[:, lanes] += dot(p, do_m[g, cols, :])
                dk_acc[:, lanes] += dot(ds, q_m[g, cols, :])
                dq_t[sub, cols] += dot(kt_ref[sub, keys], ds)

            ready = [first_half(0)]
            last_pair = None
            for g in range(heads):
                if g + 1 < heads:
                    ready.append(first_half(g + 1))
                s, dp = ready[g]
                p = jnp.exp(s + bias[...] - lse_ref[g : g + 1, cols])
                ds = (p * (dp - delta[g : g + 1, cols])).astype(jnp.bfloat16)
                if last_pair is not None:
                    second_half(*last_pair)
                last_pair = (g, p.astype(jnp.bfloat16), ds)
            second_half(*last_pair)
            return carry

        lax.fori_loop(0, (last - origin + bq - 1) // bq, query_step, 0)
        out_ref[1, keys, :] = dk_acc[...].astype(jnp.bfloat16)
        out_ref[2, keys, :] = dv_acc[...].astype(jnp.bfloat16)
        return carry

    lax.fori_loop(0, rows // bk, key_step, 0)

    def finish(i, carry):
        at = pl.ds(pl.multiple_of(i * bq, bq), bq)
        out_ref[0, at, :] = (dq_t[:, at].T * HEAD_DIM**-0.5).astype(jnp.bfloat16)
        return carry

    lax.fori_loop(0, rows // bq, finish, 0)


def attend_back(own, other, lengths, counts, q, k, v, qt, kt, ot, lse, do_own, do_other):
    rows, width = k.shape
    count = own.shape[0]
    bk = bq = min(256, rows)
    heads = width // HEAD_DIM
    return pl.pallas_call(
        attend_back_kernel,
        out_shape=struct((3, rows, width), jnp.bfloat16),
        in_specs=[SMEM] * 4 + [ANYWHERE] * 9,
        out_specs=VMEM,
        scratch_shapes=[
            *[pltpu.VMEM((count, PIECE, width), jnp.bfloat16)] * 2,
            *[pltpu.VMEM(one.shape, one.dtype) for one in (q, ot, k, v, qt, kt, lse)],
            pltpu.VMEM((rows // PIECE, PIECE, width), jnp.float32),
            pltpu.VMEM((width, rows), jnp.bfloat16),
            pltpu.VMEM((heads, rows, 128), jnp.bfloat16),
            pltpu.VMEM((heads, rows, 128), jnp.bfloat16),
            pltpu.VMEM((8, rows), jnp.float32),
            pltpu.VMEM((width, rows), jnp.float32),
            pltpu.VMEM((bk, width), jnp.float32),
            pltpu.VMEM((bk, width), jnp.float32),
            pltpu.VMEM((bk, bq), jnp.float32),
            pltpu.SemaphoreType.DMA((9,)),
        ],
        compiler_params=params(60),
        cost_estimate=cost(5e10, 20e6, heads * rows * rows // 2),
        name="attend_back",
    )(
        own, other, lengths, counts, q, k, v, qt, kt, ot, lse,
        do_own.reshape(count, PIECE, width), do_other.reshape(count, PIECE, width),
    )


def feed_kernel(
    x_ref, oa_ref, ob_ref, dy_ref, real_ref, gain_ref, shift_ref, *refs,
):
    weights, outs, held, load = refs[:6], refs[6:14], refs[14:20], refs[20]
    out_ref, y1_ref, gr_ref, turned_ref, act_a, act_b, slope_a, slope_b = outs
    wo_a, wo_b, up_a, down_a, up_b, down_b = held
    ready = resident([pltpu.make_async_copy(w, h, load.at[i]) for i, (w, h) in enumerate(zip(weights, held))])
    ready(0)
    ready(1)
    x = x_ref[...].astype(jnp.float32)
    y1 = x + dot(oa_ref[...], wo_a[...]) + dot(ob_ref[...], wo_b[...])
    y1_ref[...] = y1
    unit, _ = norm_unit(y1)
    h = (unit * gain_ref[...] + shift_ref[...]).astype(jnp.bfloat16)
    gr = (dy_ref[...].astype(jnp.float32) * real_ref[...]).astype(jnp.bfloat16)
    gr_ref[...] = gr
    turned_ref[0] = gr.T
    mlp = None
    for n, up, down, act_ref, slope_ref in ((2, up_a, down_a, act_a, slope_a), (4, up_b, down_b, act_b, slope_b)):
        ready(n)
        ready(n + 1)
        hidden = up.shape[1]
        part = min(768, hidden)
        for at in range(0, hidden, part):
            cols = slice(at, at + part)
            u = dot(h, up[:, cols])
            phi = 0.5 * (1.0 + lax.erf(u * 0.7071067811865476))
            act = (u * phi).astype(jnp.bfloat16)
            act_ref[:, cols] = act
            slope_ref[:, cols] = (phi + u * 0.3989422804014327 * jnp.exp(-0.5 * u * u)).astype(jnp.bfloat16)
            m = dot(act, down[cols, :])
            mlp = m if mlp is None else mlp + m
    out_ref[...] = (y1 + mlp).astype(jnp.bfloat16)


def feed_back_kernel(
    y1_ref, gr_ref, slope_a, slope_b, oa_ref, ob_ref, gain_ref, shift_ref, blocks_ref, *refs,
):
    weights, (left_a, left_b, right_ref, doa_ref, dob_ref, dy1_ref, norm_ref, sum_ref) = refs[:6], refs[6:14]
    held = refs[14:20]
    load, sent, got, more, send_sem, recv_sem = refs[20:]
    wo_a, wo_b, up_a, down_a, up_b, down_b = held
    loads = [pltpu.make_async_copy(w, h, load.at[i]) for i, (w, h) in enumerate(zip(weights, held))]
    loads.append(pltpu.make_async_copy(blocks_ref, sent, load.at[6]))
    ready = resident(loads)
    me = lax.axis_index("dp")
    e = me % NEAR
    step = pl.program_id(0)
    last = pl.num_programs(0) - 1
    cut = sum_ref.shape[0] // 2
    first, second = slice(0, cut), slice(cut, 2 * cut)

    def flip(d):
        return (e // 2 + d // 2) % 2 * 2 + (e % 2 + d % 2) % 2

    def trade(n):
        source, d = (
            (sent.at[flip(1), first], 1),
            (sent.at[flip(3), first], 1),
            (sent.at[flip(2), second], 2),
            (sent.at[flip(3), second], 2),
            (more.at[0], 2),
            (more.at[1], 1),
        )[n]
        return pltpu.make_async_remote_copy(
            source, got.at[n], send_sem.at[n], recv_sem.at[n],
            device_id={"dp": me // NEAR * NEAR + flip(d)}, device_id_type=MESH,
        )

    @pl.when(step == 0)
    def _():
        barrier = pltpu.get_barrier_semaphore()
        for d in (1, 2):
            to = me // NEAR * NEAR + flip(d)
            pl.semaphore_signal(barrier, inc=1, device_id={"dp": to}, device_id_type=MESH)
        pl.semaphore_wait(barrier, 2)

    ready(6)

    @pl.when(step == 0)
    def _():
        for n in (1, 3, 0, 2):
            trade(n).start()

    def second_trades():
        @pl.when(step == jnp.maximum(last - 1, 0))
        def _():
            f32 = jnp.float32
            for n, source in ((1, sent.at[flip(2), first]), (3, sent.at[flip(1), second])):
                trade(n).wait()
                more[n // 2] = (source[...].astype(f32) + got[n].astype(f32)).astype(jnp.bfloat16)
                trade(4 + n // 2).start()

    unit, inverse = norm_unit(y1_ref[...])
    right_ref[0] = (unit * gain_ref[...] + shift_ref[...]).astype(jnp.bfloat16).T
    gr = gr_ref[...]
    dh = None
    for n, up, down, slope_ref, left, o_ref in (
        (2, up_a, down_a, slope_a, left_a, oa_ref),
        (4, up_b, down_b, slope_b, left_b, ob_ref),
    ):
        ready(n)
        ready(n + 1)
        hidden = up.shape[1]
        part = min(768, hidden)
        for at in range(0, hidden, part):
            cols = slice(at, at + part)
            slope = slope_ref[:, cols].astype(jnp.float32)
            du = (dot(gr, down[cols, :], NT) * slope).astype(jnp.bfloat16)
            left[:, cols] = du
            d = dot(du, up[:, cols], NT)
            dh = d if dh is None else dh + d
        if n == 2:
            second_trades()
        local = o_ref.shape[1]
        left[:, hidden : hidden + local] = o_ref[...]
        left[:, hidden + local :] = jnp.zeros_like(left[:, hidden + local :])
    sums = jnp.concatenate(
        [jnp.sum(dh * unit, axis=0, keepdims=True), jnp.sum(dh, axis=0, keepdims=True)], axis=0
    )

    @pl.when(pl.program_id(0) == 0)
    def _():
        norm_ref[...] = sums

    @pl.when(pl.program_id(0) > 0)
    def _():
        norm_ref[...] += sums

    ready(0)
    ready(1)
    dy1 = gr.astype(jnp.float32) + norm_back(dh * gain_ref[...], unit, inverse)
    dy1_ref[...] = dy1
    dar = dy1.astype(jnp.bfloat16)
    right_ref[1] = dar.T
    doa_ref[...] = dot(dar, wo_a[...], NT).astype(jnp.bfloat16)
    dob_ref[...] = dot(dar, wo_b[...], NT).astype(jnp.bfloat16)

    @pl.when(step == last)
    def _():
        for at, n in ((first, 0), (second, 2)):
            trade(n).wait()
            trade(4 + n // 2).wait()
            total = sent[e, at].astype(jnp.float32) + got[n].astype(jnp.float32)
            sum_ref[at, :] = (total + got[4 + n // 2].astype(jnp.float32)).astype(jnp.bfloat16)


def feed_specs(rows):
    block = min(256, rows)

    def tall(cols):
        return pl.BlockSpec((block, cols), lambda i: (i, 0))

    return block, tall


def resident(loads):
    @pl.when(pl.program_id(0) == 0)
    def _():
        for one in loads:
            one.start()

    def ready(i):
        @pl.when(pl.program_id(0) == 0)
        def _():
            loads[i].wait()

    return ready


def feed(x, o_own, o_other, dy, real, wo, up, down, gain, shift):
    rows, width = x.shape
    local = o_own.shape[1]
    hidden = up[0].shape[1]
    block, tall = feed_specs(rows)
    row = pl.BlockSpec((1, width), lambda i: (0, 0))
    weights = (*wo, up[0], down[0], up[1], down[1])
    bf16 = jnp.bfloat16
    return pl.pallas_call(
        feed_kernel,
        grid=(rows // block,),
        out_shape=[
            struct((rows, width), bf16),
            struct((rows, width), jnp.float32),
            struct((rows, width), bf16),
            struct((1, width, rows), bf16),
        ]
        + [struct((rows, hidden), bf16)] * 4,
        in_specs=[tall(width), tall(local), tall(local), tall(width), tall(1)] + [row] * 2 + [ANYWHERE] * 6,
        out_specs=[tall(width)] * 3 + [pl.BlockSpec((1, width, block), lambda i: (0, 0, i))] + [tall(hidden)] * 4,
        scratch_shapes=[pltpu.VMEM(w.shape, bf16) for w in weights] + [pltpu.SemaphoreType.DMA((6,))],
        compiler_params=params(60),
        cost_estimate=cost(2 * rows * width * (hidden * 4 + local * 2), 45e6, rows * hidden * 4),
        name="feed",
    )(x, o_own, o_other, dy, real, gain, shift, *weights)


def feed_back(y1, gr, slope, o_own, o_other, wo, up, down, gain, shift, blocks):
    rows, width = y1.shape
    local = o_own.shape[1]
    hidden = up[0].shape[1]
    block, tall = feed_specs(rows)
    row = pl.BlockSpec((1, width), lambda i: (0, 0))
    weights = (*wo, up[0], down[0], up[1], down[1])
    bf16 = jnp.bfloat16
    lefts = hidden // 3 * 4
    return pl.pallas_call(
        feed_back_kernel,
        grid=(rows // block,),
        out_shape=[
            struct((rows, lefts), bf16),
            struct((rows, lefts), bf16),
            struct((2, width, rows), bf16),
            struct((rows, local), bf16),
            struct((rows, local), bf16),
            struct((rows, width), jnp.float32),
            struct((2, width), jnp.float32),
            struct(blocks.shape[1:], bf16),
        ],
        in_specs=[tall(width), tall(width), tall(hidden), tall(hidden), tall(local), tall(local)]
        + [row] * 2
        + [ANYWHERE] * 7,
        out_specs=[
            tall(lefts),
            tall(lefts),
            pl.BlockSpec((2, width, block), lambda i: (0, 0, i)),
            tall(local),
            tall(local),
            tall(width),
            pl.BlockSpec((2, width), lambda i: (0, 0)),
            pl.BlockSpec(blocks.shape[1:], lambda i: (0, 0)),
        ],
        scratch_shapes=[pltpu.VMEM(w.shape, bf16) for w in weights]
        + [
            pltpu.SemaphoreType.DMA((7,)),
            pltpu.VMEM(blocks.shape, bf16),
            pltpu.VMEM((6, blocks.shape[1] // 2, blocks.shape[2]), bf16),
            pltpu.VMEM((2, blocks.shape[1] // 2, blocks.shape[2]), bf16),
            pltpu.SemaphoreType.DMA((6,)),
            pltpu.SemaphoreType.DMA((6,)),
        ],
        compiler_params=pltpu.CompilerParams(collective_id=1, has_side_effects=True, vmem_limit_bytes=60 * MIB),
        cost_estimate=cost(2 * rows * width * (hidden * 4 + local * 2), 45e6),
        name="feed_back",
    )(y1, gr, *slope, o_own, o_other, gain, shift, blocks, *weights)


def weight_kernel(size, hosted, other_ref, own_ref, right_ref, *refs):
    if hosted:
        chunk_ref, *outs = refs[:5]
        share_ref, send, recv, send_sem, recv_sem, chunk, land, far_s, far_r, load, tiles, store = refs[5:]
    else:
        out_ref, send, recv, send_sem, recv_sem = refs
    step = pl.program_id(0)
    core = lax.axis_index("mp")
    me = lax.axis_index("dp")
    far = size // NEAR
    f, e = me // NEAR, me % NEAR

    def swapped(i):
        return pltpu.make_async_remote_copy(
            send.at[i], recv.at[i], send_sem.at[i], recv_sem.at[i],
            device_id={"mp": 1 - core}, device_id_type=MESH,
        )

    def spread(d):
        to = (f + d) % far
        return pltpu.make_async_remote_copy(
            chunk.at[to], land.at[d], far_s.at[d], far_r.at[d],
            device_id={"dp": to * NEAR + e}, device_id_type=MESH,
        )

    def flip(d):
        return (e // 2 + d // 2) % 2 * 2 + (e % 2 + d % 2) % 2

    def kept(d):
        return pltpu.make_async_copy(tiles.at[flip(d)], outs[d], store.at[d])

    @pl.when(step == 0)
    def _():
        barrier = pltpu.get_barrier_semaphore()
        pl.semaphore_signal(barrier, inc=1, device_id={"mp": 1 - core}, device_id_type=MESH)
        if hosted:
            fetch = pltpu.make_async_copy(chunk_ref, chunk, load)
            fetch.start()
            for d in range(1, far):
                to = (f + d) % far * NEAR + e
                pl.semaphore_signal(barrier, inc=1, device_id={"dp": to}, device_id_type=MESH)
            fetch.wait()
        pl.semaphore_wait(barrier, far if hosted else 1)
        if hosted:
            for d in range(1, far):
                spread(d).start()

    @pl.when(step < NEAR)
    def _():
        send[step] = dot(right_ref[0], other_ref[...]).astype(jnp.bfloat16)
        swapped(step).start()

    @pl.when(step >= NEAR)
    def _():
        total = dot(right_ref[0], own_ref[...])
        tile = step - NEAR
        swapped(tile).wait_recv()
        value = (total + recv[tile].astype(jnp.float32)).astype(jnp.bfloat16)
        if hosted:
            tiles[tile] = value
            for d in range(NEAR):

                @pl.when(flip(d) == tile)
                def _(d=d):
                    kept(d).start()

        else:
            out_ref[0] = value

    @pl.when(step == 2 * NEAR - 1)
    def _():
        for i in range(NEAR):
            swapped(i).wait_send()
        if hosted:
            for d in range(NEAR):
                kept(d).wait()
            total = chunk[f].astype(jnp.float32)
            for d in range(1, far):
                spread(d).wait()
                total = total + land[d].astype(jnp.float32)
            share_ref[...] = total.astype(jnp.bfloat16)


def weight_grads(own, other, right, size, chunk=None):
    rows, lefts = own.shape
    count, width, _ = right.shape
    block = lefts // NEAR
    far = size // NEAR
    bf16 = jnp.bfloat16
    dma = pltpu.SemaphoreType.DMA

    def pick(i):
        return (i % NEAR // (NEAR - 1) if count == 2 else 0, 0, 0)

    out_shape = [struct((NEAR, width, block), bf16)]
    in_specs = [
        pl.BlockSpec((rows, block), lambda i: (0, jnp.minimum(i, NEAR - 1))),
        pl.BlockSpec((rows, block), lambda i: (0, jnp.maximum(i - NEAR, 0))),
        pl.BlockSpec((1, width, rows), pick),
    ]
    out_specs = [pl.BlockSpec((1, width, block), lambda i: (jnp.maximum(i - NEAR, 0), 0, 0))]
    scratch = [pltpu.VMEM((NEAR, width, block), bf16)] * 2 + [dma((NEAR,))] * 2
    operands = [other, own, right]
    if chunk is not None:
        share, cols = chunk.shape[0] // far, chunk.shape[1]
        out_shape = [struct((width, block), bf16)] * NEAR + [struct((share, cols), bf16)]
        out_specs = [ANYWHERE] * NEAR
        in_specs.append(ANYWHERE)
        out_specs.append(pl.BlockSpec((share, cols), lambda i: (0, 0)))
        scratch += [pltpu.VMEM((far, share, cols), bf16)] * 2 + [dma((far,))] * 2 + [dma]
        scratch += [pltpu.VMEM((NEAR, width, block), bf16), dma((NEAR,))]
        operands.append(chunk.reshape(far, share, cols))
    return pl.pallas_call(
        functools.partial(weight_kernel, size, chunk is not None),
        grid=(2 * NEAR,),
        out_shape=out_shape,
        in_specs=in_specs,
        out_specs=out_specs,
        scratch_shapes=scratch,
        compiler_params=pltpu.CompilerParams(
            collective_id=2 if chunk is None else 3, has_side_effects=True, vmem_limit_bytes=60 * MIB
        ),
        cost_estimate=cost(4 * rows * width * lefts, 20e6),
        name="weight_grads",
    )(*operands)


def padded(rows, size):
    return -(-rows // (16 * size)) * 16 * size


def near_send(block, d, size):
    return lax.ppermute(block, "dp", [(i, i ^ d) for i in range(size)])


def close_kernel(
    size, own_ref, other_ref, down_in, gain_ref, norm2_ref,
    block_0, block_1, block_2, block_3, grads_in, ht_in, w_in, dy1_in, x_in,
    up_out, down_out, second_out, rows_own, rows_other, norms_out,
    blocks, up_in, grads_ref, ht_ref, w_ref, dy1_ref, x_ref, mine_a, mine_c, part, natural, swap_s, swap_r, dx, acc_a, acc_c, land_a, land_c, near_b, near_m, sum_b, norm_s, norm_r, norm_t,
    near_sem_s, near_sem_r, far_sem_s, far_sem_r, part_s, part_r, trade_s, trade_r, pass_s, pass_r,
    small_s, small_r, mp_s, mp_r, local, load, store,
):
    far = size // NEAR
    bits = [1 << b for b in range(far.bit_length() - 1)]
    me = lax.axis_index("dp")
    core = lax.axis_index("mp")
    f, e = me // NEAR, me % NEAR
    rows_all, local_width = grads_ref.shape[1:]
    width = w_ref.shape[1]
    block = min(256, rows_all)
    bf16 = jnp.bfloat16

    def flip(value, mask, top):
        out, b = 0, 1
        while b < top:
            out = out + b * ((value // b + mask // b) % 2)
            b *= 2
        return out

    loads = [
        pltpu.make_async_copy(source, target, load.at[i])
        for i, (source, target) in enumerate(
            ((grads_in, grads_ref), (ht_in, ht_ref), (w_in, w_ref), (dy1_in, dy1_ref), (x_in, x_ref))
        )
    ]
    ups = [
        pltpu.make_async_copy(one, blocks.at[i], load.at[5 + i])
        for i, one in enumerate((block_0, block_1, block_2, block_3))
    ]
    for one in (*ups, *loads):
        one.start()

    barrier = pltpu.get_barrier_semaphore()

    def greet(d, carry):
        pl.semaphore_signal(barrier, inc=1, device_id={"dp": (me + d) % size}, device_id_type=MESH)
        return carry

    lax.fori_loop(1, size, greet, 0)
    pl.semaphore_signal(barrier, inc=1, device_id={"mp": 1 - core}, device_id_type=MESH)
    pl.semaphore_wait(barrier, size)

    def remote(source, target, send, recv, device):
        return pltpu.make_async_remote_copy(
            source, target, send, recv, device_id={"dp": device}, device_id_type=MESH
        )

    def beside(source, target, send, recv):
        return pltpu.make_async_remote_copy(
            source, target, send, recv, device_id={"mp": 1 - core}, device_id_type=MESH
        )

    def views(*refs):
        return lambda s, *at: refs[s].at[at]

    inputs, accs = views(up_in, None, sum_b), views(acc_a, None, acc_c)
    lands, outs = views(land_a, None, land_c), views(up_out, down_out, second_out)
    mines = (mine_a, down_in, mine_c)
    held = {b: [m for m in range(far) if m % (2 * b) == 0] for b in bits}
    slot = {}
    for b in bits:
        for m in held[b]:
            slot[b, m] = len(slot)
    arrivals = [(b, m) for b in reversed(bits) for m in held[b]]

    def reduce_copy(s, b, m):
        source = inputs(s, flip(f, m + b, far)) if b == 1 else accs(s, m + b)
        k = slot[b, m]
        return remote(source, lands(s, k), far_sem_s.at[s, k], far_sem_r.at[s, k], flip(f, b, far) * NEAR + e)

    def reduce_start(s, b):
        for m in held[b]:
            reduce_copy(s, b, m).start()

    def reduce_step(s, b):
        for m in held[b]:
            reduce_copy(s, b, m).wait_recv()
            base = inputs(s, flip(f, m, far)) if b == 1 else accs(s, m)
            total = (base[...].astype(jnp.float32) + lands(s, slot[b, m])[...].astype(jnp.float32)).astype(bf16)
            if 2 * b == far:
                mines[s][...] = total
            else:
                accs(s, m)[...] = total
        if 2 * b < far:
            reduce_start(s, 2 * b)
        else:
            kept(s).start()
            available(s, 0)

    def kept(s):
        return pltpu.make_async_copy(mines[s], outs(s, e, f), store.at[s])

    def held_at(s, m):
        return mines[s] if m == 0 else outs(s, e, flip(f, m, far))

    def spread_copy(s, b, m):
        piece = outs(s, e, flip(f, m, far))
        k = slot[b, m]
        return remote(held_at(s, m), piece, far_sem_s.at[3 + s, k], far_sem_r.at[3 + s, k], flip(f, b, far) * NEAR + e)

    def spread_arrival(s, b, m):
        piece = outs(s, e, flip(f, m + b, far))
        k = slot[b, m]
        return remote(piece, piece, far_sem_s.at[3 + s, k], far_sem_r.at[3 + s, k], flip(f, b, far) * NEAR + e)

    def near_copy(s, d, m):
        piece = outs(s, e, flip(f, m, far))
        return remote(held_at(s, m), piece, near_sem_s.at[s, d, m], near_sem_r.at[s, d, m], f * NEAR + flip(e, d, NEAR))

    def near_arrival(s, d, m):
        piece = outs(s, flip(e, d, NEAR), flip(f, m, far))
        return remote(piece, piece, near_sem_s.at[s, d, m], near_sem_r.at[s, d, m], f * NEAR + flip(e, d, NEAR))

    def near_pass(s, m):
        source, to = (1, 2) if m % 2 == 0 else (2, 1)
        piece = outs(s, flip(e, source, NEAR), flip(f, m, far))
        return remote(piece, piece, near_sem_s.at[s, 3, m], near_sem_r.at[s, 3, m], f * NEAR + flip(e, to, NEAR))

    def near_passed(s, m):
        to = 2 if m % 2 == 0 else 1
        piece = outs(s, flip(e, 3, NEAR), flip(f, m, far))
        return remote(piece, piece, near_sem_s.at[s, 3, m], near_sem_r.at[s, 3, m], f * NEAR + flip(e, to, NEAR))

    def available(s, m):
        for b in reversed(bits):
            if m % (2 * b) == 0:
                spread_copy(s, b, m).start()
        for d in (1, 2):
            near_copy(s, d, m).start()

    def arrive(s, b, m):
        spread_arrival(s, b, m).wait_recv()
        available(s, m + b)

    def pass_on(s, m):
        for d in (1, 2):
            near_arrival(s, d, m).wait_recv()
        near_pass(s, m).start()

    share = land_c.shape[1]

    half_block = far * share // 2

    def near_half(index, h):
        return pl.ds(pl.multiple_of(index * (2 * half_block) + h * half_block, 16), half_block)

    def part_copy(n):
        source, d = (
            (part.at[near_half(flip(e, 1, NEAR), 0)], 1),
            (part.at[near_half(flip(e, 3, NEAR), 0)], 1),
            (part.at[near_half(flip(e, 2, NEAR), 1)], 2),
            (part.at[near_half(flip(e, 3, NEAR), 1)], 2),
            (near_m.at[0], 2),
            (near_m.at[1], 1),
        )[n]
        return remote(source, near_b.at[n], part_s.at[n], part_r.at[n], f * NEAR + flip(e, d, NEAR))

    def trade(d):
        to = (me + d) % size
        return remote(dx.at[to], rows_own.at[me], trade_s.at[d], trade_r.at[d], to)

    def trade_arrival(d):
        source = (me - d + size) % size
        return remote(dx.at[source], rows_own.at[source], trade_s.at[d], trade_r.at[d], source)

    def passing(d):
        source = (me - d + size) % size
        return beside(rows_own.at[source], rows_other.at[source], pass_s.at[d], pass_r.at[d])

    def small(d):
        to = (me + d) % size
        return remote(norm_s, norm_r.at[me], small_s.at[d], small_r.at[d], to)

    def small_arrival(d):
        source = (me - d + size) % size
        return remote(norm_s, norm_r.at[source], small_s.at[d], small_r.at[d], source)

    for one in ups:
        one.wait()
    for j in range(far):
        total = blocks[0, j].astype(jnp.float32)
        for d in range(1, NEAR):
            total = total + blocks[d, j].astype(jnp.float32)
        up_in[j] = total.astype(bf16)
    reduce_start(0, 1)
    kept(1).start()
    available(1, 0)

    tall = width // 4

    def part_step(i, carry):
        for c in range(4):
            value = dot(ht_ref[c * tall : (c + 1) * tall, :], grads_ref[i])
            at = pl.multiple_of(i * width + c * tall, 16)
            part[pl.ds(at, tall), :] = value.astype(bf16)
        return carry

    loads[0].wait()
    loads[1].wait()
    lax.fori_loop(0, 3, part_step, 0)
    used = 3 * width
    if part.shape[0] > used:
        part[used:, :] = jnp.zeros((part.shape[0] - used, local_width), bf16)
    for n in (1, 3, 0, 2):
        part_copy(n).start()

    pieces = block // PIECE

    def grad_step(i, carry):
        at = pl.ds(pl.multiple_of(i * block, block), block)
        value = dot(grads_ref[0, at, :], w_ref[0], NT)
        value += dot(grads_ref[1, at, :], w_ref[1], NT)
        value += dot(grads_ref[2, at, :], w_ref[2], NT)
        natural[pl.ds(i * pieces, pieces)] = value.reshape(pieces, PIECE, width)
        return carry

    loads[2].wait()
    lax.fori_loop(0, rows_all // block, grad_step, 0)

    def pack(j, carry):
        swap_s[j] = natural[other_ref[j]].astype(bf16)
        return carry

    lax.fori_loop(0, swap_s.shape[0], pack, 0, unroll=8)
    half = beside(swap_s, swap_r, mp_s.at[0], mp_r.at[0])
    half.start()
    reduce_step(0, 1)
    for b, m in arrivals[:1]:
        arrive(1, b, m)

    half.wait_recv()
    loads[3].wait()
    loads[4].wait()
    group_rows = dx.shape[1]
    norm_s[...] = jnp.zeros_like(norm_s)
    norm_s[2:4, :] = norm2_ref[...]
    mine = x_ref.shape[0]
    step_rows = min(256, mine)
    step_pieces = step_rows // PIECE

    def finish_step(i, carry):
        def take(j, inner):
            k = i * step_pieces + j
            natural_own[j] = natural[own_ref[k]] + swap_r[k].astype(jnp.float32)
            return inner

        lax.fori_loop(0, step_pieces, take, 0, unroll=8)
        at = pl.ds(pl.multiple_of(i * step_rows, step_rows), step_rows)
        dh = natural_own[...].reshape(step_rows, width)
        unit, inverse = norm_unit(x_ref[at, :].astype(jnp.float32))
        norm_s[0:1, :] += jnp.sum(dh * unit, axis=0, keepdims=True)
        norm_s[1:2, :] += jnp.sum(dh, axis=0, keepdims=True)
        value = dy1_ref[at, :] + norm_back(dh * gain_ref[...], unit, inverse)
        per_step = step_rows // group_rows
        dx[pl.ds(i * per_step, per_step)] = value.astype(bf16).reshape(per_step, group_rows, width)
        return carry

    natural_own = norm_t
    lax.fori_loop(0, mine // step_rows, finish_step, 0)

    def send(d, carry):
        trade(d).start()
        return carry

    lax.fori_loop(1, size, send, 0)

    def send_small(d, carry):
        small(d).start()
        return carry

    lax.fori_loop(1, size, send_small, 0)
    keep = pltpu.make_async_copy(dx.at[me], rows_own.at[me], local.at[0])
    keep.start()
    keep_small = pltpu.make_async_copy(norm_s, norm_r.at[me], local.at[1])
    keep_small.start()

    for b in bits[1:]:
        reduce_step(0, b)
    f32 = jnp.float32
    for h, n in ((0, 1), (1, 3)):
        part_copy(n).wait_recv()
        base = part[near_half(flip(e, 2 - h, NEAR), h), :]
        near_m[h] = (base.astype(f32) + near_b[n].astype(f32)).astype(bf16)
        part_copy(4 + h).start()
    for h, n in ((0, 0), (1, 2)):
        part_copy(n).wait_recv()
        part_copy(4 + h).wait_recv()
        base = part[near_half(e, h), :]
        total = base.astype(f32) + near_b[n].astype(f32) + near_b[4 + h].astype(f32)
        for j in range(far // 2):
            sum_b[h * (far // 2) + j] = total[j * share : (j + 1) * share].astype(bf16)
    reduce_start(2, 1)

    pass_on(1, 0)
    for b, m in arrivals[1:]:
        arrive(1, b, m)
    for b, m in arrivals:
        pass_on(1, m + b)
    reduce_step(2, 1)
    pass_on(0, 0)
    arrive(0, *arrivals[0])
    for b in bits[1:]:
        reduce_step(2, b)
    for b, m in arrivals[1:]:
        arrive(0, b, m)
    for b, m in arrivals:
        pass_on(0, m + b)
    pass_on(2, 0)
    for b, m in arrivals:
        arrive(2, b, m)
    keep.wait()
    passing(0).start()

    def settle(d, carry):
        trade_arrival(d).wait_recv()
        passing(d).start()
        return carry

    lax.fori_loop(1, size, settle, 0)
    keep_small.wait()

    def settle_small(d, carry):
        small_arrival(d).wait_recv()
        return carry

    lax.fori_loop(1, size, settle_small, 0)

    def add(g, carry):
        return carry + norm_r[g]

    total = lax.fori_loop(0, size, add, jnp.zeros(norm_s.shape, jnp.float32))
    for d in range(1, size):
        small(d).wait_send()
    norm_s[...] = total
    last = beside(norm_s, norm_r.at[size], mp_s.at[1], mp_r.at[1])
    last.start()
    last.wait()
    norms_out[...] = norm_s[...] + norm_r[size]

    for b, m in arrivals:
        pass_on(2, m + b)
    for s in range(3):
        for m in range(far):
            near_passed(s, m).wait_recv()
    half.wait_send()
    for s in range(3):
        kept(s).wait()
    for n in range(6):
        part_copy(n).wait_send()
    for s in range(3):
        for b in bits:
            for m in held[b]:
                if s != 1:
                    reduce_copy(s, b, m).wait_send()
                spread_copy(s, b, m).wait_send()
        for m in range(far):
            near_copy(s, 1, m).wait_send()
            near_copy(s, 2, m).wait_send()
            near_pass(s, m).wait_send()

    passing(0).wait()

    def close(d, carry):
        trade(d).wait_send()
        passing(d).wait()
        return carry

    lax.fori_loop(1, size, close, 0)


def close(own, other, up_blocks, down_share, grads, ht, w, x, dy1, gain, norm2, size):
    far = size // NEAR
    rows, local = grads.shape[1:]
    width = w.shape[1]
    b = padded(3 * width, size)
    n = x.shape[0] // size
    bf16, f32 = jnp.bfloat16, jnp.float32
    shares = (up_blocks[0].shape[0] // far, down_share.shape[0])
    cols = (up_blocks[0].shape[1], down_share.shape[1])
    up_blocks = [one.reshape(far, shares[0], cols[0]) for one in up_blocks]
    share_b = b // size
    dma = pltpu.SemaphoreType.DMA
    step = min(256, x.shape[0])
    up_sum, down_sum, second, rows_own, rows_other, norms = pl.pallas_call(
        functools.partial(close_kernel, size),
        out_shape=[
            struct((NEAR, far, shares[0], cols[0]), bf16),
            struct((NEAR, far, shares[1], cols[1]), bf16),
            struct((NEAR, far, share_b, local), bf16),
            struct((size, n, width), bf16),
            struct((size, n, width), bf16),
            struct((8, width), f32),
        ],
        in_specs=[SMEM, SMEM] + [VMEM] * 3 + [ANYWHERE] * 9,
        out_specs=[ANYWHERE] * 5 + [VMEM],
        scratch_shapes=[
            pltpu.VMEM((NEAR, far, shares[0], cols[0]), bf16),
            pltpu.VMEM((far, shares[0], cols[0]), bf16),
            pltpu.VMEM(grads.shape, bf16),
            pltpu.VMEM(ht.shape, bf16),
            pltpu.VMEM(w.shape, bf16),
            pltpu.VMEM(dy1.shape, f32),
            pltpu.VMEM(x.shape, bf16),
            pltpu.VMEM((shares[0], cols[0]), bf16),
            pltpu.VMEM((share_b, local), bf16),
            pltpu.VMEM((b, local), bf16),
            pltpu.VMEM((rows // PIECE, PIECE, width), f32),
            pltpu.VMEM((x.shape[0] // PIECE, PIECE, width), bf16),
            pltpu.VMEM((x.shape[0] // PIECE, PIECE, width), bf16),
            pltpu.VMEM((size, n, width), bf16),
            pltpu.VMEM((far, shares[0], cols[0]), bf16),
            pltpu.VMEM((far, share_b, local), bf16),
            pltpu.VMEM((far, shares[0], cols[0]), bf16),
            pltpu.VMEM((far, share_b, local), bf16),
            pltpu.VMEM((6, b // NEAR // 2, local), bf16),
            pltpu.VMEM((2, b // NEAR // 2, local), bf16),
            pltpu.VMEM((far, share_b, local), bf16),
            pltpu.VMEM((8, width), f32),
            pltpu.VMEM((size + 1, 8, width), f32),
            pltpu.VMEM((step // PIECE, PIECE, width), f32),
            dma((3, NEAR, far)),
            dma((3, NEAR, far)),
            dma((6, far)),
            dma((6, far)),
            dma((6,)),
            dma((6,)),
            dma((size,)),
            dma((size,)),
            dma((size,)),
            dma((size,)),
            dma((size,)),
            dma((size,)),
            dma((2,)),
            dma((2,)),
            dma((2,)),
            dma((9,)),
            dma((3,)),
        ],
        compiler_params=pltpu.CompilerParams(
            collective_id=0, has_side_effects=True, vmem_limit_bytes=60 * MIB
        ),
        cost_estimate=cost(8 * rows * width * local, 1e8),
        name="close",
    )(
        own, other, down_share, gain, norm2, *up_blocks, grads, ht, w, dy1, x,
    )
    return (
        up_sum.reshape(NEAR, -1, cols[0]),
        down_sum.reshape(NEAR, -1, cols[1]),
        second.reshape(b, local),
        rows_own.reshape(-1, width),
        rows_other.reshape(-1, width),
        norms,
    )


def settle_kernel(
    own_ref, other_ref, mixed_a, mixed_b, dx_a, dx_b, up_in, down_in, qkv_in,
    mixed_out, dx_out, up_out, down_out, wo_out, qkv_out,
    halves, mixed, dx, up_v, down_v, qkv_v, up, down, wo, qkv, load, store,
):
    f32 = jnp.float32
    sources = (mixed_a, mixed_b, dx_a, dx_b)
    loads = [pltpu.make_async_copy(one, halves.at[i], load.at[i]) for i, one in enumerate(sources)]
    more = ((up_in, up_v), (down_in, down_v), (qkv_in, qkv_v))
    loads += [pltpu.make_async_copy(one, to, load.at[4 + i]) for i, (one, to) in enumerate(more)]
    for one in loads:
        one.start()
    stores = []

    def keep(source, target):
        stores.append(pltpu.make_async_copy(source, target, store.at[len(stores)]))
        stores[-1].start()

    for i, (merged, target) in enumerate(((mixed, mixed_out), (dx, dx_out))):
        loads[2 * i].wait()
        loads[2 * i + 1].wait()

        def step(j, carry):
            merged[own_ref[j]] = halves[2 * i, j]
            merged[other_ref[j]] = halves[2 * i + 1, j]
            return carry

        lax.fori_loop(0, halves.shape[1], step, 0, unroll=8)
        keep(merged, target)
    loads[4].wait()
    width = up.shape[0]
    cols = up.shape[1] // (NEAR - 1)
    for e in range(NEAR - 1):
        up[:, e * cols : (e + 1) * cols] = up_v[e, :width, :].astype(f32)
    keep(up, up_out)
    wo[...] = up_v[NEAR - 1, :width, : wo.shape[0]].astype(f32).T
    keep(wo, wo_out)
    loads[5].wait()
    cols = down.shape[0] // NEAR
    for e in range(NEAR):
        down[e * cols : (e + 1) * cols, :] = down_v[e, :width, :].astype(f32).T
    keep(down, down_out)
    loads[6].wait()
    qkv[...] = qkv_v[: qkv.shape[0], :].astype(f32)
    keep(qkv, qkv_out)
    for one in stores:
        one.wait()


def settle(own, other, mixed, dx, up_sum, down_sum, qkv_sum, hidden, local):
    rows, width = mixed[0].shape
    count = rows // PIECE
    pieces = (count, PIECE, width)
    f32, bf16 = jnp.float32, jnp.bfloat16
    outs = [
        struct((2 * count, PIECE, width), bf16),
        struct((2 * count, PIECE, width), bf16),
        struct((width, hidden), f32),
        struct((hidden, width), f32),
        struct((local, width), f32),
        struct((3 * width, local), f32),
    ]
    held = [pltpu.VMEM(one.shape, one.dtype) for one in outs]
    sums = [pltpu.VMEM(one.shape, bf16) for one in (up_sum, down_sum, qkv_sum)]
    mixed_out, dx_out, *grads = pl.pallas_call(
        settle_kernel,
        out_shape=outs,
        in_specs=[SMEM] * 2 + [ANYWHERE] * 7,
        out_specs=[ANYWHERE] * 6,
        scratch_shapes=[
            pltpu.VMEM((4, *pieces), bf16),
            *held[:2],
            *sums,
            *held[2:],
            pltpu.SemaphoreType.DMA((7,)),
            pltpu.SemaphoreType.DMA((6,)),
        ],
        compiler_params=params(60),
        cost_estimate=cost(0, 34e6),
        name="settle",
    )(own, other, *[one.reshape(pieces) for one in (*mixed, *dx)], up_sum, down_sum, qkv_sum)
    return mixed_out.reshape(2 * rows, width), dx_out.reshape(2 * rows, width), *grads


def swap(value):
    return lax.ppermute(value, "mp", [(0, 1), (1, 0)])


def held_kernel(value_ref, after_ref, out_ref):
    del value_ref, after_ref, out_ref


def held_until(value, after):
    return pl.pallas_call(
        held_kernel,
        out_shape=struct(value.shape, value.dtype),
        in_specs=[ANYWHERE] * 2,
        out_specs=ANYWHERE,
        input_output_aliases={0: 0},
        name="held_until",
    )(value, after)


def exchange(value):
    return lax.all_to_all(value, "dp", split_axis=0, concat_axis=0, tiled=True)


def body(
    tokens, out_grad, lengths, counts, dest_slot, qkv_weight, out_weight, up_weight, down_weight,
    norm1_gain, norm1_shift, norm2_gain, norm2_shift,
):
    groups = lax.axis_size("dp")
    me = lax.axis_index("dp")
    core = lax.axis_index("mp")
    rows, width = tokens.shape
    per = rows // PIECE
    capacity = per // groups
    half = capacity // 2
    local = qkv_weight.shape[2]
    bf16 = jnp.bfloat16

    slots = dest_slot.reshape(groups, per)
    my_slots = lax.dynamic_index_in_dim(slots, me, 0, keepdims=True)
    group_ids = jnp.arange(groups, dtype=jnp.int32)[:, None]
    piece_ids = jnp.broadcast_to(jnp.arange(per, dtype=jnp.int32)[None, :], (groups, per))
    source = slot_table(my_slots // per == group_ids, piece_ids, capacity)
    target = slot_table(slots // per == me, slots - me * per, capacity)

    def halves(table):
        own = lax.dynamic_slice_in_dim(table, core * half, half, 1)
        other = lax.dynamic_slice_in_dim(table, (1 - core) * half, half, 1)
        return own.reshape(-1), other.reshape(-1)

    src_own, src_other = halves(source)
    own, other = halves(target)

    x_own = exchange(gather_pieces(src_own, tokens))
    dy_send = gather_pieces(src_own, out_grad)
    place = (own[:, None] * PIECE + jnp.arange(PIECE, dtype=jnp.int32)[None, :]).reshape(-1, 1)
    real, start = jnp.zeros(place.shape, jnp.bool_), jnp.int32(0)
    for c in range(lengths.shape[1]):
        live = start + jnp.minimum(lengths[0, c], counts[0, c])
        real, start = real | ((place >= start) & (place < live)), start + lengths[0, c]
    real = real.astype(jnp.float32)
    wo_other, up_other, down_other = swap(out_weight), swap(up_weight), swap(down_weight)
    gain1, shift1 = norm1_gain[None], norm1_shift[None]
    gain2, shift2 = norm2_gain[None], norm2_shift[None]
    x_own, dy_send, real, wo_other, up_other, down_other, own, other, gain1, shift1, gain2, shift2, src_other = (
        lax.optimization_barrier(
            (
                x_own, dy_send, real, wo_other, up_other, down_other,
                own, other, gain1, shift1, gain2, shift2, src_other,
            )
        )
    )
    wo, up, down = (out_weight, wo_other), (up_weight, up_other), (down_weight, down_other)
    x_other = swap(x_own)

    h1_t, q, k, v, qt, kt, vt = project(own, other, x_own, x_other, gain1, shift1, qkv_weight)

    dy_own = exchange(dy_send)
    ot, o_own, o_send, lse = attend(own, other, lengths, counts, k, qt, vt)
    o_other = swap(o_send)

    out_rows, y1, gr, gr_turned, act_own, act_other, slope_own, slope_other = feed(
        x_own, o_own, o_other, dy_own, real, wo, up, down, gain2, shift2
    )
    [down_blocks] = weight_grads(act_own, act_other, gr_turned, groups)
    left_own, left_other, right, do_own, do_send, dy1, norm2, down_chunk = feed_back(
        y1, gr, (slope_own, slope_other), o_own, o_other, wo, up, down, gain2, shift2, down_blocks
    )
    do_other = swap(do_send)
    unit = 16 * (groups // NEAR)
    down_chunk = jnp.pad(down_chunk, ((0, -down_chunk.shape[0] % unit), (0, 0)))
    *up_blocks, down_share = weight_grads(left_own, left_other, right, groups, down_chunk)
    up_blocks, do_own, do_other = lax.optimization_barrier((up_blocks, do_own, do_other))
    up_got = [near_send(up_blocks[d], d, groups) for d in range(1, NEAR)]
    out_back = exchange(held_until(out_rows, swap(up_blocks[0][:16, :128])))
    grads = attend_back(own, other, lengths, counts, q, k, v, qt, kt, ot, lse, do_own, do_other)
    up_got, grads, out_back = lax.optimization_barrier((up_got, grads, out_back))
    out_other = swap(out_back)
    parts = [jnp.pad(one, ((0, -one.shape[0] % unit), (0, 0))) for one in (up_blocks[0], *up_got)]
    up_sum, down_sum, qkv_grad, dx_own, dx_other, norms = close(
        own, other, parts, down_share, grads, h1_t, qkv_weight, x_own, dy1, gain1, norm2, groups
    )
    mixed_out, input_grad, up_grad, down_grad, wo_grad, qkv_grad = settle(
        src_own, src_other, (out_back, out_other), (dx_own, dx_other), up_sum, down_sum, qkv_grad,
        up_weight.shape[1], local,
    )
    qkv_grad = qkv_grad.reshape(3, width, local)

    return (
        mixed_out, input_grad, qkv_grad, wo_grad, up_grad, down_grad,
        norms[0], norms[1], norms[2], norms[3],
    )


def solution(mesh):
    in_specs = (
        P("dp", None), P("dp", None), P("dp", None), P("dp", None), P(),
        P(None, None, "mp"), P("mp", None), P(None, "mp"), P("mp", None), P(), P(), P(), P(),
    )
    out_specs = (
        P("dp", None), P("dp", None), P(None, None, "mp"), P("mp", None), P(None, "mp"), P("mp", None),
        P(), P(), P(), P(),
    )
    return jax.shard_map(body, mesh=mesh, in_specs=in_specs, out_specs=out_specs, check_vma=False)
```
